32 devices in a mesh: grp: 4 (over y, core), blk: 8 (over z, x).
Axes of the slice: x: 2, y: 2, z: 4, core: 2. Of those that a mesh axis runs over, the one named last changes fastest.
Arguments:
- head_table: bfloat16 [8192, 256], P(('grp', 'blk')), may hold values from -4 to 4
- tail_table: bfloat16 [131072, 256], P(('grp', 'blk')), may hold values from -0.25 to 0.25
- qual_table: bfloat16 [32768, 256], P(('grp', 'blk')), may hold values from -4 to 4
- rel_table: float32 [512, 256], replicated, may hold values from -3 to 3
- proj: float32 [256, 256], replicated, may hold values from -0.375 to 0.375
- head_id: int32 [32768], P(('grp', 'blk')), may hold values from 0 to 2047, as said below
- tail_id: int32 [32768], P(('grp', 'blk')), may hold values from 0 to 4095
- rel_id: int32 [32768], P(('grp', 'blk')), may hold values from 0 to 511
- qual_rel: int32 [32768, 4], P(('grp', 'blk')), may hold values from 0 to 511
- qual_ref: int32 [32768, 4], P(('grp', 'blk')), may hold values from 0 to 255
- qual_req: int32 [8192], P(('grp', 'blk')), may hold values from 0 to 1023
- neg_id: int32 [32768], P(('grp', 'blk')), may hold values from 0 to 4095
- edge_count: int32 [32], P(('grp', 'blk')), may hold values from 128 to 1024
Outputs:
- head_grad: float32 [8192, 256], P(('grp', 'blk'))
- tail_grad: float32 [131072, 256], P(('grp', 'blk'))
- qual_grad: float32 [32768, 256], P(('grp', 'blk'))
- rel_grad: float32 [512, 256], replicated
- proj_grad: float32 [256, 256], replicated
The draws below stay inside these ranges and needn't reach their ends.
Inputs may be any that keep to these rules, and one draw needn't show every extreme that they name: Among the edges of one device, at most 192 have head rows held by any one device of blk (head_id // 256), and some device of blk is named that often by every device's edges.
All inputs are finite; a program needn't handle non-finite values.
Results may differ from the reference program's by a relative error of at most 0.0046.
Values may be sent and summed in bfloat16 or wider, within the bound.
No kernel may reach another device: no remote copies, remote signals or barrier semaphores. Data moves between devices by JAX's collectives and lax.ppermute only.
A program may use at most 128 MiB of HBM per device.

```python
import math
import jax
import jax.numpy as jnp
import numpy as np
from jax import lax

W = 256
REL = 512
NQ = 4
EDGES = 1024
NEG = 1024
HEAD_DEV = 256
TAIL_DEV = 4096
QROWS_DEV = 1024
CAP = 8
PARTITIONS = 32
HEADS = 8192
TAILS = 131072
QROWS = 32768
SLOTS = 256
ALL_EDGES = 32768
ALL_NEG = 32768
N_GRP = 4
N_BLK = 8


def draw_head_table(key, part):
    values = jax.random.truncated_normal(key, -4.0, 4.0, (HEADS, W), jnp.float32)
    return values.astype(jnp.bfloat16)


def draw_tail_table(key, part):
    scale_now = W ** (-0.5)
    values = jax.random.truncated_normal(key, -4.0, 4.0, (TAILS, W), jnp.float32) * scale_now
    return values.astype(jnp.bfloat16)


def draw_rel_table(key, part):
    values = jax.random.truncated_normal(key, -6.0, 6.0, (REL, W), jnp.float32) * 0.5
    return values


def draw_head_id(key, part):
    unit = EDGES // (2 * N_BLK)
    half_count = N_BLK // 2
    slots = jnp.arange(EDGES, dtype=jnp.int32)
    heavy_span = 3 * unit * half_count
    ranks = jnp.where(slots < heavy_span, slots // (3 * unit), half_count + (slots - heavy_span) // unit)

    def one_device(device_key):
        first_key, second_key, third_key = jax.random.split(device_key, 3)
        order = jax.random.permutation(first_key, N_BLK).astype(jnp.int32)
        owners = jax.random.permutation(second_key, order[ranks])
        offsets = jax.random.randint(third_key, (EDGES,), 0, HEAD_DEV, dtype=jnp.int32)
        return (owners * HEAD_DEV + offsets).astype(jnp.int32)
    keys = jax.random.split(key, PARTITIONS)
    return jax.vmap(one_device)(keys).reshape(-1)


def touch_ends(values, own_key, smallest, top_value):
    dims = values.shape
    spot = [jax.random.randint(jax.random.fold_in(own_key, axis), (), 0, dims[axis]) for axis in range(len(dims))]
    values = values.at[tuple(spot)].set(smallest)
    longest = dims.index(max(dims))
    spot[longest] = (spot[longest] + 1) % dims[longest]
    return values.at[tuple(spot)].set(top_value)


def level_of(rng, shape, cuts, least, largest):
    def one(position, shards_of):
        draws = jax.random.uniform(jax.random.fold_in(jax.random.fold_in(rng, 6), position), (shards_of,), jnp.float32, least / len(cuts), largest / len(cuts))
        return jnp.repeat(jnp.exp(draws), shape[position] // shards_of).reshape((-1,) + (1,) * (len(shape) - position - 1))

    loudness = one(*cuts[0])
    for cut in cuts[1:]:
        loudness = loudness * one(*cut)
    return loudness


def rank_bounds(count, skew):
    loads = [(1 << 20) // math.isqrt(grade ** skew) + 1 for grade in range(1, count + 1)]
    spread = 1 + sum(loads) // (1 << 30)
    return np.cumsum(np.array([max(1, weight // spread) for weight in loads]))


def ranked_ids(rng, dims, count, skew):
    grid = rank_bounds(count, skew)
    ticket = jax.random.randint(jax.random.fold_in(rng, 1), dims, 0, int(grid[count - 1]))
    rank = jnp.searchsorted(jnp.asarray(grid, jnp.int32), ticket, side="right")
    return jax.random.permutation(jax.random.fold_in(rng, 2), count)[rank].astype(jnp.int32)


def centred(rng, extent, scale, limit, shards=(), kind=jnp.bfloat16):
    entries = scale * jax.random.normal(rng, extent, jnp.float32)
    if shards:
        entries = entries * level_of(rng, extent, shards, -0.22, 0.18)
    return jnp.clip(entries, -limit, limit).astype(kind)


def setup_inputs(seed: int = 0) -> dict:
    arg_keys = jax.random.split(jax.random.key(seed), 14)
    return {
        "head_table": draw_head_table(jax.random.fold_in(arg_keys[13], 71), 0),
        "tail_table": draw_tail_table(jax.random.fold_in(arg_keys[13], 71), 0),
        "qual_table": centred(arg_keys[2], (QROWS, W), 1.0, 4.0, ((0, 32),)),
        "rel_table": draw_rel_table(jax.random.fold_in(arg_keys[13], 71), 0),
        "proj": centred(arg_keys[4], (W, W), W ** -0.5, 0.375, (), jnp.float32),
        "head_id": draw_head_id(jax.random.fold_in(arg_keys[13], 71), 0),
        "tail_id": touch_ends(jax.random.randint(arg_keys[6], (ALL_EDGES,), 0, TAIL_DEV), jax.random.fold_in(arg_keys[6], 1), 0, TAIL_DEV - 1).astype(jnp.int32),
        "rel_id": touch_ends(ranked_ids(arg_keys[7], (ALL_EDGES,), REL, 2), jax.random.fold_in(arg_keys[7], 3), 0, REL - 1).astype(jnp.int32),
        "qual_rel": touch_ends(ranked_ids(arg_keys[8], (ALL_EDGES, NQ), REL, 2), jax.random.fold_in(arg_keys[8], 3), 0, REL - 1).astype(jnp.int32),
        "qual_ref": touch_ends(jax.random.randint(arg_keys[9], (ALL_EDGES, NQ), 0, SLOTS), jax.random.fold_in(arg_keys[9], 1), 0, SLOTS - 1).astype(jnp.int32),
        "qual_req": touch_ends(jax.random.randint(arg_keys[10], (PARTITIONS * SLOTS,), 0, QROWS_DEV), jax.random.fold_in(arg_keys[10], 1), 0, QROWS_DEV - 1).astype(jnp.int32),
        "neg_id": touch_ends(jax.random.randint(arg_keys[11], (ALL_NEG,), 0, TAIL_DEV), jax.random.fold_in(arg_keys[11], 1), 0, TAIL_DEV - 1).astype(jnp.int32),
        "edge_count": touch_ends(jax.random.randint(arg_keys[12], (PARTITIONS,), EDGES // 8, EDGES + 1), jax.random.fold_in(arg_keys[12], 1), EDGES // 8, EDGES).astype(jnp.int32),
    }


HIGHEST = lax.Precision.HIGHEST


def local_backward(heads, tail_part, fetched, rel_table, proj, tail_ids, rel_ids, qual_rels, qual_refs, neg_ids, count):
    edge_total = heads.shape[0]
    rel_rows = rel_table[rel_ids]
    composed = jnp.zeros(heads.shape, jnp.float32)
    for qual_index in range(NQ):
        composed = composed + rel_table[qual_rels[:, qual_index]] * fetched[qual_refs[:, qual_index]].astype(jnp.float32)
    relation = rel_rows + jnp.dot(composed, proj, precision=HIGHEST)
    query = (heads * relation).astype(jnp.bfloat16)
    tails = tail_part[tail_ids]
    negatives = tail_part[neg_ids]
    positive = jnp.sum(query.astype(jnp.float32) * tails.astype(jnp.float32), axis=1)
    live_mask = (jnp.arange(edge_total, dtype=jnp.int32) < count).astype(jnp.float32)
    scores = jnp.dot(query, negatives.T, preferred_element_type=jnp.float32)
    top_score = jnp.maximum(jnp.max(scores, axis=1), positive)
    neg_exp = jnp.exp(scores - top_score[:, None])
    pos_exp = jnp.exp(positive - top_score)
    total_exp = jnp.sum(neg_exp, axis=1) + pos_exp
    pos_weight = pos_exp / total_exp * live_mask
    neg_round = (neg_exp / total_exp[:, None] * live_mask[:, None]).astype(jnp.bfloat16)
    pos_coef = pos_weight - live_mask
    query_grad = pos_coef[:, None] * tails.astype(jnp.float32) + jnp.dot(neg_round, negatives, preferred_element_type=jnp.float32)
    negative_grad = jnp.dot(neg_round.T, query, preferred_element_type=jnp.float32)
    tail_grad = jax.ops.segment_sum(pos_coef[:, None] * query.astype(jnp.float32), tail_ids, tail_part.shape[0])
    tail_grad = tail_grad + jax.ops.segment_sum(negative_grad, neg_ids, tail_part.shape[0])
    head_rows_grad = query_grad * relation
    relation_grad = query_grad * heads
    composed_grad = jnp.dot(relation_grad, proj.T, precision=HIGHEST)
    proj_grad = jnp.dot(composed.T, relation_grad, precision=HIGHEST)
    rel_grad = jax.ops.segment_sum(relation_grad, rel_ids, REL)
    fetched_grad = jnp.zeros((fetched.shape[0], fetched.shape[1]), jnp.float32)
    for qual_index in range(NQ):
        refs_now = qual_refs[:, qual_index]
        rels_now = qual_rels[:, qual_index]
        rel_grad = rel_grad + jax.ops.segment_sum(composed_grad * fetched[refs_now].astype(jnp.float32), rels_now, REL)
        fetched_grad = fetched_grad + jax.ops.segment_sum(composed_grad * rel_table[rels_now], refs_now, fetched.shape[0])
    return head_rows_grad, tail_grad, fetched_grad, rel_grad, proj_grad


def reference(head_table, tail_table, qual_table, rel_table, proj, head_id, tail_id, rel_id, qual_rel, qual_ref, qual_req, neg_id, edge_count):
    device_total = N_GRP * N_BLK
    slot_count = CAP * device_total
    owners = jnp.arange(slot_count, dtype=jnp.int32) // CAP

    def one_device(running, index):
        rel_acc, proj_acc = running
        group_start = (index // N_BLK) * (HEAD_DEV * N_BLK)
        edge_start = index * EDGES
        head_ids = lax.dynamic_slice_in_dim(head_id, edge_start, EDGES, 0) + group_start
        tail_ids = lax.dynamic_slice_in_dim(tail_id, edge_start, EDGES, 0)
        rel_ids = lax.dynamic_slice_in_dim(rel_id, edge_start, EDGES, 0)
        qual_rels = lax.dynamic_slice_in_dim(qual_rel, edge_start, EDGES, 0)
        qual_refs = lax.dynamic_slice_in_dim(qual_ref, edge_start, EDGES, 0)
        requests = lax.dynamic_slice_in_dim(qual_req, index * slot_count, slot_count, 0)
        fetched = qual_table[owners * QROWS_DEV + requests]
        neg_ids = lax.dynamic_slice_in_dim(neg_id, index * NEG, NEG, 0)
        tail_part = lax.dynamic_slice_in_dim(tail_table, index * TAIL_DEV, TAIL_DEV, 0)
        count = lax.dynamic_slice_in_dim(edge_count, index, 1, 0)[0]
        heads = head_table[head_ids].astype(jnp.float32)
        head_rows_grad, tail_grad, fetched_grad, rel_grad, proj_grad = local_backward(
            heads, tail_part, fetched, rel_table, proj, tail_ids, rel_ids, qual_rels, qual_refs, neg_ids, count)
        return (rel_acc + rel_grad, proj_acc + proj_grad), (head_rows_grad, tail_grad, fetched_grad)

    start_state = (jnp.zeros((REL, W), jnp.float32), jnp.zeros((W, W), jnp.float32))
    indices = jnp.arange(device_total, dtype=jnp.int32)
    (rel_grad, proj_grad), (head_rows_all, tail_all, fetched_all) = lax.scan(one_device, start_state, indices)
    edge_device = jnp.arange(device_total * EDGES, dtype=jnp.int32) // EDGES
    head_global = (edge_device // N_BLK) * (HEAD_DEV * N_BLK) + head_id
    head_grad = jax.ops.segment_sum(head_rows_all.reshape(-1, W), head_global, HEAD_DEV * device_total)
    tail_grad = tail_all.reshape(TAIL_DEV * device_total, W)
    slot_index = jnp.arange(device_total * slot_count, dtype=jnp.int32)
    qual_rows = ((slot_index % slot_count) // CAP) * QROWS_DEV + qual_req
    qual_grad = jax.ops.segment_sum(fetched_all.reshape(-1, W), qual_rows, QROWS_DEV * device_total)
    return head_grad, tail_grad, qual_grad, rel_grad, proj_grad
```

```python
import functools

import jax
import jax.numpy as jnp
from jax import lax
from jax.experimental import pallas as pl
from jax.experimental.pallas import tpu as pltpu
from jax.sharding import PartitionSpec as P

BF = jnp.bfloat16
F32 = jnp.float32
VMEM_BYTES = 56 * 1024 * 1024
BOTH = ("grp", "blk")
BLOCK = 256


def nn(a, b):
    return jnp.dot(a, b, preferred_element_type=F32)


def nt(a, b):
    return lax.dot_general(a, b, (((1,), (1,)), ((), ())), preferred_element_type=F32)


def pieces(values, count):
    out = []
    for _ in range(count):
        part = values.astype(BF)
        out.append(part)
        values = values - part.astype(F32)
    return out


def onehot(ids_row, first, rows):
    iota = lax.broadcasted_iota(jnp.int32, (rows, ids_row.shape[1]), 0)
    return jnp.where(iota == ids_row - first, 1.0, 0.0).astype(BF)


def lookup_kernel(rel_ref, tail_ref, rel_ids, tn_ids, rel_out, tails_out, negt_out, neg_out, rel_t, tail_t):
    width = rel_ref.shape[1]
    rel_rows = rel_ref.shape[0]
    tail_rows = tail_ref.shape[0]
    edges = rel_ids.shape[1]
    for index, part in enumerate(pieces(rel_ref[...].T, 3)):
        rel_t[index * width : (index + 1) * width, :] = part

    @pl.loop(0, tail_rows // BLOCK)
    def _(step):
        start = pl.multiple_of(step * BLOCK, BLOCK)
        tail_t[:, pl.ds(start, BLOCK)] = tail_ref[pl.ds(start, BLOCK), :].T

    for which in range(rel_ids.shape[0]):

        @pl.loop(0, edges // BLOCK)
        def _(step):
            at = pl.ds(pl.multiple_of(step * BLOCK, BLOCK), BLOCK)
            got = nn(rel_t[...], onehot(rel_ids[which : which + 1, at], 0, rel_rows))
            rel_out[which, :, at] = got[:width] + got[width : 2 * width] + got[2 * width :]

    for which, out in ((0, tails_out), (1, negt_out)):

        @pl.loop(0, edges // BLOCK)
        def _(step):
            at = pl.ds(pl.multiple_of(step * BLOCK, BLOCK), BLOCK)
            got = nn(tail_t[...], onehot(tn_ids[which : which + 1, at], 0, tail_rows))
            out[:, at] = got.astype(BF)
            if which == 1:
                neg_out[at, :] = got.T.astype(BF)


def edge_kernel(
    count_ref,
    rel_ref,
    fetched_ref,
    ref_ids,
    head_ref,
    head_ids,
    proj_ref,
    tails_ref,
    negt_ref,
    neg_ref,
    head_out,
    rg_out,
    cg_out,
    comp_out,
    nr_out,
    query_out,
    pq_out,
    fetched_t,
    head_terms,
    proj_n,
    proj_t,
):
    width, edges = tails_ref.shape
    slots = fetched_ref.shape[0]
    owners, _, head_rows = head_ref.shape
    fetched_t[...] = fetched_ref[...].astype(F32).T.astype(BF)
    for index, part in enumerate(pieces(proj_ref[...], 2)):
        proj_n[index] = part
    for index, part in enumerate(pieces(proj_ref[...].T, 2)):
        proj_t[index] = part

    @pl.loop(0, edges // BLOCK)
    def _(step):
        start = pl.multiple_of(step * BLOCK, BLOCK)
        at = pl.ds(start, BLOCK)
        composed = jnp.zeros((width, BLOCK), F32)
        for k in range(ref_ids.shape[0]):
            rows = nn(fetched_t[...], onehot(ref_ids[k : k + 1, at], 0, slots))
            composed = composed + rel_ref[k + 1, :, at] * rows
        comp_hi, comp_lo = pieces(composed, 2)
        comp_out[0, :, at] = comp_hi
        comp_out[1, :, at] = comp_lo
        relation = rel_ref[0, :, at] + (
            nn(proj_t[0], comp_hi) + (nn(proj_t[0], comp_lo) + nn(proj_t[1], comp_hi))
        )
        heads = jnp.zeros((width, BLOCK), F32)
        for owner in range(owners):
            heads = heads + nn(head_ref[owner], onehot(head_ids[:, at], owner * head_rows, head_rows))
        query = (heads * relation).astype(BF)
        query_out[:, at] = query
        query_f = query.astype(F32)
        tails = tails_ref[:, at].astype(F32)
        positive = jnp.sum(query_f * tails, axis=0, keepdims=True)
        scores = nn(neg_ref[...], query)
        top = jnp.maximum(jnp.max(scores, axis=0, keepdims=True), positive)
        neg_exp = jnp.exp(scores - top)
        pos_exp = jnp.exp(positive - top)
        total = jnp.sum(neg_exp, axis=0, keepdims=True) + pos_exp
        slot = lax.broadcasted_iota(jnp.int32, (1, BLOCK), 1) + start
        live = jnp.where(slot < count_ref[0], 1.0, 0.0)
        scale = live / total
        neg_round = (neg_exp * scale).astype(BF)
        nr_out[:, at] = neg_round
        coef = pos_exp * scale - live
        pq_out[:, at] = (coef * query_f).astype(BF)
        query_grad = coef * tails + nn(negt_ref[...], neg_round)
        head_terms[:, at] = (query_grad * relation).astype(BF)
        relation_grad = query_grad * heads
        rg_hi, rg_lo = pieces(relation_grad, 2)
        rg_out[0, :, at] = rg_hi
        rg_out[1, :, at] = rg_lo
        cg_out[:, at] = nn(proj_n[0], rg_hi) + (nn(proj_n[0], rg_lo) + nn(proj_n[1], rg_hi))

    @pl.loop(0, owners)
    def _(owner):
        at = pl.ds(pl.multiple_of(owner * head_rows, head_rows), head_rows)
        head_out[at, :] = nt(onehot(head_ids[...], owner * head_rows, head_rows), head_terms[...]).astype(BF)


def relation_kernel(rel_ref, fetched_ref, ref_ids, rel_ids, rg_ref, cg_ref, comp_ref, sums_out, fetched_out, fetched_t):
    rel_rows = sums_out.shape[0] - rg_ref.shape[1]
    slots = fetched_ref.shape[0]
    fetched_t[...] = fetched_ref[...].astype(F32).T.astype(BF)
    comp_grad = cg_ref[...]
    rel_sum = nt(onehot(rel_ids[0:1, :], 0, rel_rows), rg_ref[0])
    fetched_sum = jnp.zeros(fetched_ref.shape, F32)
    for k in range(ref_ids.shape[0]):
        hot = onehot(ref_ids[k : k + 1, :], 0, slots)
        rows = nn(fetched_t[...], hot)
        rel_sum = rel_sum + nt(onehot(rel_ids[k + 1 : k + 2, :], 0, rel_rows), (comp_grad * rows).astype(BF))
        fetched_sum = fetched_sum + nt(hot, (comp_grad * rel_ref[k + 1]).astype(BF))
    sums_out[:rel_rows, :] = rel_sum.astype(BF)
    fetched_out[...] = fetched_sum.astype(BF)
    proj_sum = nt(comp_ref[0], rg_ref[0]) + (nt(comp_ref[0], rg_ref[1]) + nt(comp_ref[1], rg_ref[0]))
    sums_out[rel_rows:, :] = proj_sum.astype(BF)


def tail_kernel(tn_ids, nr_ref, query_ref, pq_ref, tail_out, terms):
    edges = query_ref.shape[1]
    rows = tail_out.shape[0]
    step = pl.program_id(0)

    @pl.when(step == 0)
    def _():
        terms[:edges, :] = pq_ref[...].astype(F32).T.astype(BF)
        terms[edges:, :] = nt(nr_ref[...], query_ref[...]).astype(BF)

    first = step * rows
    tail_out[...] = nn(onehot(tn_ids[0:1, :], first, rows), terms[:edges, :]) + nn(
        onehot(tn_ids[1:2, :], first, rows), terms[edges:, :]
    )


def call(kernel, outs, scratch, cost, *args, smem=()):
    specs = [
        pl.BlockSpec(memory_space=pltpu.SMEM if index in smem else pltpu.VMEM) for index in range(len(args))
    ]
    return pl.pallas_call(
        kernel,
        out_shape=[jax.ShapeDtypeStruct(shape, dtype) for shape, dtype in outs],
        in_specs=specs,
        out_specs=[pl.BlockSpec(memory_space=pltpu.VMEM)] * len(outs),
        scratch_shapes=[pltpu.VMEM(shape, dtype) for shape, dtype in scratch],
        compiler_params=pltpu.CompilerParams(vmem_limit_bytes=VMEM_BYTES),
        cost_estimate=pl.CostEstimate(flops=cost, bytes_accessed=1 << 22, transcendentals=0),
    )(*args)


def exchange(values, axes):
    return lax.all_to_all(values, axes, split_axis=0, concat_axis=0, tiled=True)


def body(
    head_table,
    tail_table,
    qual_table,
    rel_table,
    proj,
    head_id,
    tail_id,
    rel_id,
    qual_rel,
    qual_ref,
    qual_req,
    neg_id,
    edge_count,
):
    head_rows, width = head_table.shape
    tail_rows = tail_table.shape[0]
    qual_rows = qual_table.shape[0]
    rel_rows = rel_table.shape[0]
    edges = head_id.shape[0]
    negs = neg_id.shape[0]
    slots = qual_req.shape[0]
    members = lax.axis_size("blk")
    devices = lax.axis_size("grp") * members

    arrived = exchange(qual_req.reshape(devices, -1), BOTH)
    picked = jnp.take(qual_table, arrived, axis=0)
    fetched = exchange(picked, BOTH).reshape(slots, width)
    head_all = exchange(jnp.broadcast_to(head_table.T[None], (members, width, head_rows)), "blk")

    rel_ids = jnp.concatenate([rel_id[None, :], qual_rel.T], axis=0)
    ref_ids = qual_ref.T
    tn_ids = jnp.stack([tail_id, neg_id])
    rel_looked, tails, neg_t, neg = call(
        lookup_kernel,
        [((5, width, edges), F32), ((width, edges), BF), ((width, negs), BF), ((negs, width), BF)],
        [((3 * width, rel_rows), BF), ((width, tail_rows), BF)],
        8 << 30,
        rel_table,
        tail_table,
        rel_ids,
        tn_ids,
    )
    head_part, rg, cg, comp, neg_round, query, pq = call(
        edge_kernel,
        [
            ((members * head_rows, width), BF),
            ((2, width, edges), BF),
            ((width, edges), F32),
            ((2, width, edges), BF),
            ((negs, edges), BF),
            ((width, edges), BF),
            ((width, edges), BF),
        ],
        [((width, slots), BF), ((width, edges), BF), ((2, width, width), BF), ((2, width, width), BF)],
        8 << 30,
        edge_count,
        rel_looked,
        fetched,
        ref_ids,
        head_all,
        head_id[None, :],
        proj,
        tails,
        neg_t,
        neg,
        smem=(0,),
    )
    sums_part, fetched_part = call(
        relation_kernel,
        [((rel_rows + width, width), BF), ((slots, width), BF)],
        [((width, slots), BF)],
        4 << 30,
        rel_looked,
        fetched,
        ref_ids,
        rel_ids,
        rg,
        cg,
        comp,
    )
    head_got = exchange(head_part.reshape(members, head_rows, width), "blk")
    sums_got = exchange(sums_part.reshape(devices, -1, width), BOTH)
    sums_own = jnp.sum(sums_got.astype(F32), axis=0).astype(BF)
    sums_all = exchange(jnp.broadcast_to(sums_own[None], (devices,) + sums_own.shape), BOTH)
    returned = exchange(fetched_part.reshape(devices, -1, width), BOTH).reshape(-1, width)

    block = min(512, tail_rows)
    tail_grad = pl.pallas_call(
        tail_kernel,
        out_shape=jax.ShapeDtypeStruct((tail_rows, width), F32),
        grid=(tail_rows // block,),
        in_specs=[pl.BlockSpec(memory_space=pltpu.VMEM)] * 4,
        out_specs=pl.BlockSpec((block, width), lambda i: (i, 0)),
        scratch_shapes=[pltpu.VMEM((edges + negs, width), BF)],
        compiler_params=pltpu.CompilerParams(vmem_limit_bytes=VMEM_BYTES),
        cost_estimate=pl.CostEstimate(flops=8 << 30, bytes_accessed=1 << 22, transcendentals=0),
    )(tn_ids, neg_round, query, pq)

    head_grad = jnp.sum(head_got.astype(F32), axis=0)
    hot = (jnp.arange(qual_rows, dtype=jnp.int32)[:, None] == arrived.reshape(1, -1)).astype(BF)
    qual_grad = jnp.dot(hot, returned, preferred_element_type=F32)
    sums = sums_all.reshape(rel_rows + width, width).astype(F32)
    return (head_grad, tail_grad, qual_grad, sums[:rel_rows], sums[rel_rows:])


def solution(mesh):
    rows = P(BOTH, None)
    ids = P(BOTH)
    in_specs = (rows, rows, rows, P(), P(), ids, ids, ids, rows, rows, ids, ids, ids)
    out_specs = (rows, rows, rows, P(), P())
    return jax.shard_map(body, mesh=mesh, in_specs=in_specs, out_specs=out_specs, check_vma=False)
```

```python
import functools

import jax
import jax.numpy as jnp
from jax import lax
from jax.experimental import pallas as pl
from jax.experimental.pallas import tpu as pltpu
from jax.sharding import PartitionSpec as P

BF = jnp.bfloat16
F32 = jnp.float32
VMEM_BYTES = 56 * 1024 * 1024
BOTH = ("grp", "blk")
BLOCK = 256


def nn(a, b):
    return jnp.dot(a, b, preferred_element_type=F32)


def nt(a, b):
    return lax.dot_general(a, b, (((1,), (1,)), ((), ())), preferred_element_type=F32)


def pieces(values, count):
    out = []
    for _ in range(count):
        part = values.astype(BF)
        out.append(part)
        values = values - part.astype(F32)
    return out


def onehot(ids_row, first, rows):
    iota = lax.broadcasted_iota(jnp.int32, (rows, ids_row.shape[1]), 0)
    return jnp.where(iota == ids_row - first, 1.0, 0.0).astype(BF)


def relation_lookup_kernel(rel_ref, rel_ids, rel_out, rel_t):
    rel_rows, width = rel_ref.shape
    edges = rel_ids.shape[1]
    for index, part in enumerate(pieces(rel_ref[...].T, 3)):
        rel_t[index * width : (index + 1) * width, :] = part
    for which in range(rel_ids.shape[0]):

        @pl.loop(0, edges // BLOCK)
        def _(step):
            at = pl.ds(pl.multiple_of(step * BLOCK, BLOCK), BLOCK)
            got = nn(rel_t[...], onehot(rel_ids[which : which + 1, at], 0, rel_rows))
            rel_out[which, :, at] = got[:width] + got[width : 2 * width] + got[2 * width :]


def tail_lookup_kernel(tail_ref, tn_ids, tails_out, negt_out, neg_out, tail_t):
    tail_rows = tail_ref.shape[0]
    edges = tn_ids.shape[1]

    @pl.loop(0, tail_rows // BLOCK)
    def _(step):
        start = pl.multiple_of(step * BLOCK, BLOCK)
        tail_t[:, pl.ds(start, BLOCK)] = tail_ref[pl.ds(start, BLOCK), :].T

    for which, out in ((0, tails_out), (1, negt_out)):

        @pl.loop(0, edges // BLOCK)
        def _(step):
            at = pl.ds(pl.multiple_of(step * BLOCK, BLOCK), BLOCK)
            got = nn(tail_t[...], onehot(tn_ids[which : which + 1, at], 0, tail_rows))
            out[:, at] = got.astype(BF)
            if which == 1:
                neg_out[at, :] = got.T.astype(BF)


def edge_kernel(
    count_ref,
    rel_ref,
    fetched_ref,
    ref_ids,
    head_near_ref,
    head_far_ref,
    head_ids,
    proj_ref,
    tails_ref,
    negt_ref,
    neg_ref,
    head_near_out,
    head_far_out,
    rg_out,
    cg_out,
    comp_out,
    nr_out,
    query_out,
    pq_out,
    fetched_t,
    head_terms,
    proj_n,
    proj_t,
):
    width, edges = tails_ref.shape
    slots = fetched_ref.shape[0]
    half, _, head_rows = head_near_ref.shape
    fetched_t[...] = fetched_ref[...].astype(F32).T.astype(BF)
    for index, part in enumerate(pieces(proj_ref[...], 2)):
        proj_n[index] = part
    for index, part in enumerate(pieces(proj_ref[...].T, 2)):
        proj_t[index] = part

    @pl.loop(0, edges // BLOCK)
    def _(step):
        start = pl.multiple_of(step * BLOCK, BLOCK)
        at = pl.ds(start, BLOCK)
        composed = jnp.zeros((width, BLOCK), F32)
        for k in range(ref_ids.shape[0]):
            rows = nn(fetched_t[...], onehot(ref_ids[k : k + 1, at], 0, slots))
            composed = composed + rel_ref[k + 1, :, at] * rows
        comp_hi, comp_lo = pieces(composed, 2)
        comp_out[0, :, at] = comp_hi
        comp_out[1, :, at] = comp_lo
        relation = rel_ref[0, :, at] + (
            nn(proj_t[0], comp_hi) + (nn(proj_t[0], comp_lo) + nn(proj_t[1], comp_hi))
        )
        heads = jnp.zeros((width, BLOCK), F32)
        for first, table in ((0, head_near_ref), (half, head_far_ref)):
            for owner in range(half):
                hot = onehot(head_ids[:, at], (first + owner) * head_rows, head_rows)
                heads = heads + nn(table[owner], hot)
        query = (heads * relation).astype(BF)
        query_out[:, at] = query
        query_f = query.astype(F32)
        tails = tails_ref[:, at].astype(F32)
        positive = jnp.sum(query_f * tails, axis=0, keepdims=True)
        scores = nn(neg_ref[...], query)
        top = jnp.maximum(jnp.max(scores, axis=0, keepdims=True), positive)
        neg_exp = jnp.exp(scores - top)
        pos_exp = jnp.exp(positive - top)
        total = jnp.sum(neg_exp, axis=0, keepdims=True) + pos_exp
        slot = lax.broadcasted_iota(jnp.int32, (1, BLOCK), 1) + start
        live = jnp.where(slot < count_ref[0], 1.0, 0.0)
        scale = live / total
        neg_round = (neg_exp * scale).astype(BF)
        nr_out[:, at] = neg_round
        coef = pos_exp * scale - live
        pq_out[:, at] = (coef * query_f).astype(BF)
        query_grad = coef * tails + nn(negt_ref[...], neg_round)
        head_terms[:, at] = (query_grad * relation).astype(BF)
        relation_grad = query_grad * heads
        rg_hi, rg_lo = pieces(relation_grad, 2)
        rg_out[0, :, at] = rg_hi
        rg_out[1, :, at] = rg_lo
        cg_out[:, at] = nn(proj_n[0], rg_hi) + (nn(proj_n[0], rg_lo) + nn(proj_n[1], rg_hi))

    for first, out in ((0, head_near_out), (half, head_far_out)):

        @pl.loop(0, half)
        def _(owner):
            hot = onehot(head_ids[...], (first + owner) * head_rows, head_rows)
            out[owner] = nt(hot, head_terms[...]).astype(BF)


def relation_kernel(
    group_ref, rel_ref, fetched_ref, ref_ids, rel_ids, rg_ref, cg_ref, comp_ref, sums_out, fetched_out, fetched_t, sums
):
    groups, share, _ = sums_out.shape
    rel_rows = sums.shape[0] - rg_ref.shape[1]
    slots = fetched_ref.shape[0]
    fetched_t[...] = fetched_ref[...].astype(F32).T.astype(BF)
    comp_grad = cg_ref[...]
    rel_sum = nt(onehot(rel_ids[0:1, :], 0, rel_rows), rg_ref[0])
    fetched_sum = jnp.zeros(fetched_ref.shape, F32)
    for k in range(ref_ids.shape[0]):
        hot = onehot(ref_ids[k : k + 1, :], 0, slots)
        rows = nn(fetched_t[...], hot)
        rel_sum = rel_sum + nt(onehot(rel_ids[k + 1 : k + 2, :], 0, rel_rows), (comp_grad * rows).astype(BF))
        fetched_sum = fetched_sum + nt(hot, (comp_grad * rel_ref[k + 1]).astype(BF))
    sums[:rel_rows, :] = rel_sum
    sums[rel_rows:, :] = nt(comp_ref[0], rg_ref[0]) + (nt(comp_ref[0], rg_ref[1]) + nt(comp_ref[1], rg_ref[0]))
    fetched_out[...] = fetched_sum.astype(BF)
    for offset in range(groups):
        start = pl.multiple_of(jnp.bitwise_xor(group_ref[0], offset) * share, share)
        sums_out[offset] = sums[pl.ds(start, share), :].astype(BF)


def finish_kernel(group_ref, own_ref, other_ref, rel_out, proj_out, sums):
    pairs, share, _ = own_ref.shape
    for pair in range(pairs):
        for bit, table in ((0, own_ref), (1, other_ref)):
            start = pl.multiple_of(jnp.bitwise_xor(group_ref[0], 2 * pair + bit) * share, share)
            sums[pl.ds(start, share), :] = table[pair].astype(F32)
    rel_rows = rel_out.shape[0]
    rel_out[...] = sums[:rel_rows, :]
    proj_out[...] = sums[rel_rows:, :]


def tail_kernel(tn_ids, nr_ref, query_ref, pq_ref, tail_out, terms):
    edges = query_ref.shape[1]
    rows = tail_out.shape[0]
    step = pl.program_id(0)

    @pl.when(step == 0)
    def _():
        terms[:edges, :] = pq_ref[...].astype(F32).T.astype(BF)
        terms[edges:, :] = nt(nr_ref[...], query_ref[...]).astype(BF)

    first = step * rows
    tail_out[...] = nn(onehot(tn_ids[0:1, :], first, rows), terms[:edges, :]) + nn(
        onehot(tn_ids[1:2, :], first, rows), terms[edges:, :]
    )


def call(kernel, outs, scratch, cost, *args, smem=()):
    specs = [
        pl.BlockSpec(memory_space=pltpu.SMEM if index in smem else pltpu.VMEM) for index in range(len(args))
    ]
    return pl.pallas_call(
        kernel,
        out_shape=[jax.ShapeDtypeStruct(shape, dtype) for shape, dtype in outs],
        in_specs=specs,
        out_specs=[pl.BlockSpec(memory_space=pltpu.VMEM)] * len(outs),
        scratch_shapes=[pltpu.VMEM(shape, dtype) for shape, dtype in scratch],
        compiler_params=pltpu.CompilerParams(vmem_limit_bytes=VMEM_BYTES),
        cost_estimate=pl.CostEstimate(flops=cost, bytes_accessed=1 << 22, transcendentals=0),
    )(*args)


def exchange(values, axes):
    return lax.all_to_all(values, axes, split_axis=0, concat_axis=0, tiled=True)


def swap(values, axis, offset):
    count = lax.axis_size(axis)
    return lax.ppermute(values, axis, [(i, i ^ offset) for i in range(count)])


def body(
    head_table,
    tail_table,
    qual_table,
    rel_table,
    proj,
    head_id,
    tail_id,
    rel_id,
    qual_rel,
    qual_ref,
    qual_req,
    neg_id,
    edge_count,
):
    head_rows, width = head_table.shape
    tail_rows = tail_table.shape[0]
    qual_rows = qual_table.shape[0]
    rel_rows = rel_table.shape[0]
    edges = head_id.shape[0]
    negs = neg_id.shape[0]
    slots = qual_req.shape[0]
    members = lax.axis_size("blk")
    devices = lax.axis_size("grp") * members

    groups = lax.axis_size("grp")
    half = members // 2
    me = lax.axis_index("blk")
    group = lax.axis_index("grp").reshape(1)

    arrived = exchange(qual_req.reshape(devices, -1), BOTH)
    head_t = head_table.T
    head_near = jnp.stack([head_t] + [swap(head_t, "blk", 2 * m) for m in range(1, half)])
    head_far = swap(head_near, "blk", 1)
    offset = jnp.bitwise_xor(head_id // head_rows, me)
    head_slot = ((offset % 2) * half + offset // 2) * head_rows + head_id % head_rows
    head_slot = head_slot[None, :]

    rel_ids = jnp.concatenate([rel_id[None, :], qual_rel.T], axis=0)
    ref_ids = qual_ref.T
    tn_ids = jnp.stack([tail_id, neg_id])
    (rel_looked,) = call(
        relation_lookup_kernel,
        [((5, width, edges), F32)],
        [((3 * width, rel_rows), BF)],
        5 << 30,
        rel_table,
        rel_ids,
    )
    arrived, rel_looked = lax.optimization_barrier((arrived, rel_looked))
    picked = jnp.take(qual_table, arrived, axis=0)
    fetched = exchange(picked, BOTH).reshape(slots, width)
    tails, neg_t, neg = call(
        tail_lookup_kernel,
        [((width, edges), BF), ((width, negs), BF), ((negs, width), BF)],
        [((width, tail_rows), BF)],
        8 << 30,
        tail_table,
        tn_ids,
    )
    near_part, far_part, rg, cg, comp, neg_round, query, pq = call(
        edge_kernel,
        [
            ((half, head_rows, width), BF),
            ((half, head_rows, width), BF),
            ((2, width, edges), BF),
            ((width, edges), F32),
            ((2, width, edges), BF),
            ((negs, edges), BF),
            ((width, edges), BF),
            ((width, edges), BF),
        ],
        [((width, slots), BF), ((width, edges), BF), ((2, width, width), BF), ((2, width, width), BF)],
        8 << 30,
        edge_count,
        rel_looked,
        fetched,
        ref_ids,
        head_near,
        head_far,
        head_slot,
        proj,
        tails,
        neg_t,
        neg,
        smem=(0,),
    )
    far_got = swap(far_part, "blk", 1)
    share = (rel_rows + width) // groups
    sums_part, fetched_part = call(
        relation_kernel,
        [((groups, share, width), BF), ((slots, width), BF)],
        [((width, slots), BF), ((rel_rows + width, width), F32)],
        4 << 30,
        group,
        rel_looked,
        fetched,
        ref_ids,
        rel_ids,
        rg,
        cg,
        comp,
        smem=(0,),
    )
    sums_part = sums_part.reshape(groups // 2, 2, share, width)
    core_got = swap(sums_part[:, 1], "grp", 1)
    pair_sum = sums_part[:, 0].astype(F32) + core_got.astype(F32)
    quarter = pair_sum[0]
    for pair in range(1, groups // 2):
        quarter = quarter + swap(pair_sum[pair].astype(BF), "grp", 2 * pair).astype(F32)
    parts = exchange(quarter.astype(BF).reshape(members, -1, width), "blk")
    own = jnp.sum(parts.astype(F32), axis=0).astype(BF)
    whole = exchange(jnp.broadcast_to(own[None], (members,) + own.shape), "blk").reshape(share, width)
    sums_own = jnp.stack([whole] + [swap(whole, "grp", 2 * pair) for pair in range(1, groups // 2)])
    sums_other = swap(sums_own, "grp", 1)

    near_sum = near_part.astype(F32) + far_got.astype(F32)
    head_grad = near_sum[0]
    near_send = near_sum.astype(BF)
    for m in range(1, half):
        head_grad = head_grad + swap(near_send[m], "blk", 2 * m).astype(F32)

    returned = exchange(fetched_part.reshape(devices, -1, width), BOTH).reshape(-1, width)

    block = min(512, tail_rows)
    tail_grad = pl.pallas_call(
        tail_kernel,
        out_shape=jax.ShapeDtypeStruct((tail_rows, width), F32),
        grid=(tail_rows // block,),
        in_specs=[pl.BlockSpec(memory_space=pltpu.VMEM)] * 4,
        out_specs=pl.BlockSpec((block, width), lambda i: (i, 0)),
        scratch_shapes=[pltpu.VMEM((edges + negs, width), BF)],
        compiler_params=pltpu.CompilerParams(vmem_limit_bytes=VMEM_BYTES),
        cost_estimate=pl.CostEstimate(flops=8 << 30, bytes_accessed=1 << 22, transcendentals=0),
    )(tn_ids, neg_round, query, pq)

    hot = (jnp.arange(qual_rows, dtype=jnp.int32)[:, None] == arrived.reshape(1, -1)).astype(BF)
    qual_grad = jnp.dot(hot, returned, preferred_element_type=F32)
    rel_grad, proj_grad = call(
        finish_kernel,
        [((rel_rows, width), F32), ((width, width), F32)],
        [((rel_rows + width, width), F32)],
        1 << 20,
        group,
        sums_own,
        sums_other,
        smem=(0,),
    )
    return (head_grad, tail_grad, qual_grad, rel_grad, proj_grad)


def solution(mesh):
    rows = P(BOTH, None)
    ids = P(BOTH)
    in_specs = (rows, rows, rows, P(), P(), ids, ids, ids, rows, rows, ids, ids, ids)
    out_specs = (rows, rows, rows, P(), P())
    return jax.shard_map(body, mesh=mesh, in_specs=in_specs, out_specs=out_specs, check_vma=False)
```

```python
import jax
import jax.numpy as jnp
from jax import lax
from jax.experimental import pallas as pl
from jax.experimental.pallas import tpu as pltpu
from jax.sharding import Mesh, PartitionSpec as P

BF = jnp.bfloat16
F32 = jnp.float32
MIB = 1024 * 1024
AXES = ("pair", "core", "line", "near")
MEMBER = ("line", "near")
BLOCK = 256


def nn(a, b):
    return jnp.dot(a, b, preferred_element_type=F32)


def nt(a, b):
    return lax.dot_general(a, b, (((1,), (1,)), ((), ())), preferred_element_type=F32)


def pieces(values, count):
    out = []
    for _ in range(count):
        part = values.astype(BF)
        out.append(part)
        values = values - part.astype(F32)
    return out


def flip(values):
    return values.astype(F32).T.astype(BF)


def onehot(ids_row, first, rows):
    iota = lax.broadcasted_iota(jnp.int32, (rows, ids_row.shape[1]), 0)
    return jnp.where(iota == ids_row - first, 1.0, 0.0).astype(BF)


def relation_lookup_kernel(rel_ref, rel_id, qual_rel, rel_out, table):
    rel_rows, width = rel_ref.shape
    edges = rel_id.shape[1]
    step = pl.program_id(0)

    @pl.when(step == 0)
    def _():
        for index, part in enumerate(pieces(rel_ref[...].T, 2)):
            table[index * width : (index + 1) * width, :] = part

    def look(ids):
        for start in range(0, edges, BLOCK):
            at = pl.ds(start, BLOCK)
            got = nn(table[...], onehot(ids[:, at], 0, rel_rows))
            rel_out[0, :, at] = got[:width] + got[width:]

    @pl.when(step == 0)
    def _():
        look(rel_id)

    for k in range(qual_rel.shape[0]):

        @pl.when(step == k + 1)
        def _():
            look(qual_rel.at[k : k + 1])


def tail_lookup_kernel(tail_ref, tail_id, neg_id, tails_out, negt_out, neg_out, table):
    tail_rows = tail_ref.shape[0]
    for start in range(0, tail_rows, BLOCK):
        at = pl.ds(start, BLOCK)
        table[:, at] = tail_ref[at, :].T
    for ids, out in ((tail_id, tails_out), (neg_id, negt_out)):
        for start in range(0, ids.shape[1], BLOCK):
            at = pl.ds(start, BLOCK)
            got = nn(table[...], onehot(ids[:, at], 0, tail_rows))
            out[:, at] = got.astype(BF)
            if ids is neg_id:
                neg_out[at, :] = got.T.astype(BF)


def edge_kernel(
    count_ref,
    rel_ref,
    fetched_ref,
    ref_ids,
    rel_id,
    qual_rel,
    near_ref,
    far_ref,
    head_slot,
    proj_ref,
    tails_ref,
    negt_ref,
    neg_ref,
    near_out,
    far_out,
    sums_out,
    nr_out,
    query_out,
    pq_out,
    sums,
    *,
    rel_rows,
):
    width, edges = tails_ref.shape
    slots = fetched_ref.shape[0]
    half, head_rows, _ = near_ref.shape
    devices, sent_rows, _ = sums_out.shape
    share = sums.shape[0] // devices
    quals = ref_ids.shape[0]
    fetched_t = flip(fetched_ref[...])
    proj_hi, proj_lo = pieces(proj_ref[...], 2)
    projt_hi, projt_lo = pieces(proj_ref[...].T, 2)

    composed = jnp.zeros((width, edges), F32)
    rows = []
    for k in range(quals):
        rows.append(nn(fetched_t, onehot(ref_ids[k : k + 1, :], 0, slots)))
        composed = composed + rel_ref[k + 1] * rows[k]
    comp_hi, comp_lo = pieces(composed, 2)
    relation = rel_ref[0] + (nn(projt_hi, comp_hi) + (nn(projt_hi, comp_lo) + nn(projt_lo, comp_hi)))
    heads = jnp.zeros((width, edges), F32)
    for first, table in ((0, near_ref), (half, far_ref)):
        for owner in range(half):
            heads = heads + nn(flip(table[owner]), onehot(head_slot[...], (first + owner) * head_rows, head_rows))
    query = (heads * relation).astype(BF)
    query_out[...] = query
    query_f = query.astype(F32)
    tails = tails_ref[...].astype(F32)
    positive = jnp.sum(query_f * tails, axis=0, keepdims=True)
    scores = nn(neg_ref[...], query)
    top = jnp.maximum(jnp.max(scores, axis=0, keepdims=True), positive)
    neg_exp = jnp.exp(scores - top)
    pos_exp = jnp.exp(positive - top)
    total = jnp.sum(neg_exp, axis=0, keepdims=True) + pos_exp
    slot = lax.broadcasted_iota(jnp.int32, (1, edges), 1)
    live = jnp.where(slot < count_ref[0], 1.0, 0.0)
    scale = live / total
    neg_round = (neg_exp * scale).astype(BF)
    nr_out[...] = neg_round
    coef = pos_exp * scale - live
    pq_out[...] = (coef * query_f).astype(BF)
    query_grad = coef * tails + nn(negt_ref[...], neg_round)

    head_terms = (query_grad * relation).astype(BF)
    for first, out in ((0, near_out), (half, far_out)):
        for owner in range(half):
            hot = onehot(head_slot[...], (first + owner) * head_rows, head_rows)
            out[owner] = nt(hot, head_terms).astype(BF)

    relation_grad = query_grad * heads
    rg_hi, rg_lo = pieces(relation_grad, 2)
    comp_grad = nn(proj_hi, rg_hi) + (nn(proj_hi, rg_lo) + nn(proj_lo, rg_hi))
    rel_sum = nt(onehot(rel_id[...], 0, rel_rows), rg_hi)
    fetched_sum = jnp.zeros((slots, width), F32)
    for k in range(quals):
        hot = onehot(ref_ids[k : k + 1, :], 0, slots)
        rel_sum = rel_sum + nt(onehot(qual_rel[k : k + 1, :], 0, rel_rows), (comp_grad * rows[k]).astype(BF))
        fetched_sum = fetched_sum + nt(hot, (comp_grad * rel_ref[k + 1]).astype(BF))
    sums[:rel_rows, :] = rel_sum
    sums[rel_rows : rel_rows + width, :] = nt(comp_hi, rg_hi) + (nt(comp_hi, rg_lo) + nt(comp_lo, rg_hi))
    if sums.shape[0] > rel_rows + width:
        sums[rel_rows + width :, :] = jnp.zeros((sums.shape[0] - rel_rows - width, width), F32)
    both = [sums[...].reshape(devices, share, width), fetched_sum.reshape(devices, sent_rows - share, width)]
    sums_out[...] = jnp.concatenate(both, axis=1).astype(BF)


def add_kernel(got_ref, out_ref):
    devices, share, _ = out_ref.shape
    total = got_ref[0, :share, :].astype(F32)
    for index in range(1, devices):
        total = total + got_ref[index, :share, :].astype(F32)
    total = total.astype(BF)
    for index in range(devices):
        out_ref[index] = total


def tail_kernel(tail_id, neg_id, nr_ref, query_ref, pq_ref, tail_out, terms):
    edges = query_ref.shape[1]
    rows = tail_out.shape[0]
    step = pl.program_id(0)

    @pl.when(step == 0)
    def _():
        terms[:edges, :] = flip(pq_ref[...])
        terms[edges:, :] = nt(nr_ref[...], query_ref[...]).astype(BF)

    first = step * rows
    tail_out[...] = nn(onehot(tail_id[...], first, rows), terms[:edges, :]) + nn(
        onehot(neg_id[...], first, rows), terms[edges:, :]
    )


WHOLE = pl.BlockSpec(memory_space=pltpu.VMEM)


def call(kernel, outs, scratch, micros, vmem, *args, smem=(), grid=(), out_specs=None):
    shapes = [jax.ShapeDtypeStruct(shape, dtype) for shape, dtype in outs]
    return pl.pallas_call(
        kernel,
        out_shape=shapes,
        grid=grid,
        in_specs=[pl.BlockSpec(memory_space=pltpu.SMEM) if index in smem else WHOLE for index in range(len(args))],
        out_specs=out_specs or [WHOLE] * len(outs),
        scratch_shapes=[pltpu.VMEM(shape, dtype) for shape, dtype in scratch],
        compiler_params=pltpu.CompilerParams(vmem_limit_bytes=vmem * MIB),
        cost_estimate=pl.CostEstimate(flops=micros << 30, bytes_accessed=MIB, transcendentals=0),
    )(*args)


def exchange(values, axes):
    return lax.all_to_all(values, axes, split_axis=0, concat_axis=0, tiled=True)


def swap(values, axis):
    return lax.ppermute(values, axis, [(0, 1), (1, 0)])


def body(
    head_table,
    tail_table,
    qual_table,
    rel_table,
    proj,
    head_id,
    tail_id,
    rel_id,
    qual_rel,
    qual_ref,
    qual_req,
    neg_id,
    edge_count,
):
    head_rows, width = head_table.shape
    tail_rows = tail_table.shape[0]
    qual_rows = qual_table.shape[0]
    rel_rows = rel_table.shape[0]
    edges = head_id.shape[0]
    negs = neg_id.shape[0]
    slots = qual_req.shape[0]
    half = lax.axis_size("line")
    devices = lax.axis_size(AXES)
    quals = qual_ref.shape[1]
    cap = slots // devices
    near = lax.axis_index("near")

    arrived = exchange(qual_req.reshape(devices, cap), AXES)
    head_near = exchange(jnp.broadcast_to(head_table[None], (half, head_rows, width)), "line")
    head_far = swap(head_near, "near")
    owner = head_id // head_rows
    head_slot = ((jnp.bitwise_xor(owner, near) % 2) * half + owner // 2) * head_rows + head_id % head_rows
    head_slot = head_slot[None, :]

    rel_row = rel_id[None, :]
    qual_row = qual_rel.T
    ref_row = qual_ref.T
    tail_row = tail_id[None, :]
    neg_row = neg_id[None, :]
    (rel_looked,) = call(
        relation_lookup_kernel,
        [((quals + 1, width, edges), F32)],
        [((2 * width, rel_rows), BF)],
        5,
        24,
        rel_table,
        rel_row,
        qual_row,
        grid=(quals + 1,),
        out_specs=[pl.BlockSpec((1, width, edges), lambda i: (i, 0, 0))],
    )
    arrived, rel_looked = lax.optimization_barrier((arrived, rel_looked))
    picked = qual_table.at[arrived].get(mode="promise_in_bounds")
    fetched = exchange(picked, AXES).reshape(slots, width)
    tails, neg_t, neg = call(
        tail_lookup_kernel,
        [((width, edges), BF), ((width, negs), BF), ((negs, width), BF)],
        [((width, tail_rows), BF)],
        7,
        32,
        tail_table,
        tail_row,
        neg_row,
    )
    share = -(-(rel_rows + width) // (8 * devices)) * 8

    def edge(*refs):
        edge_kernel(*refs, rel_rows=rel_rows)

    near_part, far_part, sums_part, neg_round, query, pq = call(
        edge,
        [
            ((half, head_rows, width), BF),
            ((half, head_rows, width), BF),
            ((devices, share + cap, width), BF),
            ((negs, edges), BF),
            ((width, edges), BF),
            ((width, edges), BF),
        ],
        [((devices * share, width), F32)],
        15,
        48,
        edge_count,
        rel_looked,
        fetched,
        ref_row,
        rel_row,
        qual_row,
        head_near,
        head_far,
        head_slot,
        proj,
        tails,
        neg_t,
        neg,
        smem=(0,),
    )
    far_got = swap(far_part, "near")
    sums_got = exchange(sums_part, AXES)
    (sums_own,) = call(add_kernel, [((devices, share, width), BF)], [], 1, 16, sums_got)
    sums = exchange(sums_own, AXES).reshape(devices * share, width)

    near_sum = (near_part.astype(F32) + far_got.astype(F32)).astype(BF)
    head_got = exchange(near_sum, "line")
    head_grad = jnp.sum(head_got.astype(F32), axis=0)

    block = min(1024, tail_rows)
    (tail_grad,) = call(
        tail_kernel,
        [((tail_rows, width), F32)],
        [((edges + negs, width), BF)],
        8,
        32,
        tail_row,
        neg_row,
        neg_round,
        query,
        pq,
        grid=(tail_rows // block,),
        out_specs=[pl.BlockSpec((block, width), lambda i: (i, 0))],
    )
    returned = sums_got[:, share:, :].reshape(slots, width)
    hot = (jnp.arange(qual_rows, dtype=jnp.int32)[:, None] == arrived.reshape(1, -1)).astype(BF)
    qual_grad = jnp.dot(hot, returned, preferred_element_type=F32)
    rel_grad = sums[:rel_rows].astype(F32)
    proj_grad = sums[rel_rows : rel_rows + width].astype(F32)
    return (head_grad, tail_grad, qual_grad, rel_grad, proj_grad)


def solution(mesh):
    groups, members = mesh.devices.shape
    view = Mesh(mesh.devices.reshape(groups // 2, 2, members // 2, 2), AXES)
    rows = P(AXES, None)
    ids = P(AXES)
    in_specs = (rows, rows, rows, P(), P(), ids, ids, ids, rows, rows, ids, ids, ids)
    out_specs = (rows, rows, rows, P(), P())
    return jax.shard_map(body, mesh=view, in_specs=in_specs, out_specs=out_specs, check_vma=False)
```

```python
import jax
import jax.numpy as jnp
from jax import lax
from jax.experimental import pallas as pl
from jax.experimental.pallas import tpu as pltpu
from jax.sharding import Mesh, PartitionSpec as P

BF = jnp.bfloat16
F32 = jnp.float32
MIB = 1024 * 1024
AXES = ("pair", "core", "line", "near")
MEMBER = ("line", "near")
CHIPS = ("pair", "line", "near")
PAIRS = 2
BLOCK = 256


def nn(a, b):
    return jnp.dot(a, b, preferred_element_type=F32)


def nt(a, b):
    return lax.dot_general(a, b, (((1,), (1,)), ((), ())), preferred_element_type=F32)


def pieces(values, count):
    out = []
    for _ in range(count):
        part = values.astype(BF)
        out.append(part)
        values = values - part.astype(F32)
    return out


def flip(values):
    return values.astype(F32).T.astype(BF)


def onehot(ids_row, first, rows):
    iota = lax.broadcasted_iota(jnp.int32, (rows, ids_row.shape[1]), 0)
    return jnp.where(iota == ids_row - first, 1.0, 0.0).astype(BF)


def relation_lookup_kernel(rel_ref, rel_id, qual_rel, rel_out, table):
    rel_rows, width = rel_ref.shape
    edges = rel_id.shape[1]
    step = pl.program_id(0)

    @pl.when(step == 0)
    def _():
        for index, part in enumerate(pieces(rel_ref[...].T, 2)):
            table[index * width : (index + 1) * width, :] = part

    def look(ids):
        for start in range(0, edges, BLOCK):
            at = pl.ds(start, BLOCK)
            got = nn(table[...], onehot(ids[:, at], 0, rel_rows))
            rel_out[0, :, at] = got[:width] + got[width:]

    @pl.when(step == 0)
    def _():
        look(rel_id)

    for k in range(qual_rel.shape[0]):

        @pl.when(step == k + 1)
        def _():
            look(qual_rel.at[k : k + 1])


def tail_lookup_kernel(
    tail_hbm, tail_id, neg_id, tails_out, negt_out, neg_out, tail_ref, table, tails, negt, neg, in_sems, out_sems
):
    tail_rows = tail_ref.shape[0]
    chunks = in_sems.shape[0]
    size = tail_rows // chunks
    loads = []
    for index in range(chunks):
        at = pl.ds(index * size, size)
        loads.append(pltpu.make_async_copy(tail_hbm.at[at, :], tail_ref.at[at, :], in_sems.at[index]))
        loads[index].start()
    for index in range(chunks):
        loads[index].wait()
        for start in range(index * size, (index + 1) * size, BLOCK):
            at = pl.ds(start, BLOCK)
            table[:, at] = tail_ref[at, :].T
    stores = []

    def store(source, target):
        stores.append(pltpu.make_async_copy(source, target, out_sems.at[len(stores)]))
        stores[-1].start()

    for ids, out in ((neg_id, negt), (tail_id, tails)):
        for start in range(0, ids.shape[1], BLOCK):
            at = pl.ds(start, BLOCK)
            got = nn(table[...], onehot(ids[:, at], 0, tail_rows))
            out[:, at] = got.astype(BF)
            if ids is neg_id:
                neg[at, :] = got.T.astype(BF)
        if ids is neg_id:
            store(negt, negt_out)
            store(neg, neg_out)
    store(tails, tails_out)
    for copy in stores:
        copy.wait()


def edge_kernel(
    count_ref,
    place_ref,
    rel_hbm,
    near_hbm,
    far_hbm,
    tails_hbm,
    neg_hbm,
    negt_hbm,
    fetched_ref,
    ref_ids,
    rel_id,
    qual_rel,
    head_id,
    proj_ref,
    far_out,
    near_out,
    own_out,
    other_out,
    terms_out,
    rel_ref,
    near_ref,
    far_ref,
    tails_ref,
    neg_ref,
    negt_ref,
    sums,
    packed,
    terms,
    in_sems,
    out_sems,
    *,
    rel_rows,
):
    width, edges = tails_ref.shape
    slots = fetched_ref.shape[0]
    half, head_rows, _ = near_ref.shape
    cores, chips, _, lanes = packed.shape
    share = sums.shape[0] // chips
    quals = ref_ids.shape[0]
    cap = slots // (cores * chips)

    loads = []
    for index, (source, target) in enumerate(
        (
            (rel_hbm, rel_ref),
            (near_hbm, near_ref),
            (far_hbm, far_ref),
            (tails_hbm, tails_ref),
            (neg_hbm, neg_ref),
            (negt_hbm, negt_ref),
        )
    ):
        loads.append(pltpu.make_async_copy(source, target, in_sems.at[index]))
        loads[index].start()

    fetched_t = flip(fetched_ref[...])
    proj_hi, proj_lo = pieces(proj_ref[...], 2)
    projt_hi, projt_lo = pieces(proj_ref[...].T, 2)
    rows = [nn(fetched_t, onehot(ref_ids[k : k + 1, :], 0, slots)) for k in range(quals)]
    loads[0].wait()
    composed = rel_ref[1] * rows[0]
    for k in range(1, quals):
        composed = composed + rel_ref[k + 1] * rows[k]
    comp_hi, comp_lo = pieces(composed, 2)
    relation = rel_ref[0] + (nn(projt_hi, comp_hi) + (nn(projt_hi, comp_lo) + nn(projt_lo, comp_hi)))
    loads[1].wait()
    loads[2].wait()
    offset = jnp.bitwise_xor(head_id[...] // head_rows, place_ref[1])
    head_slot = ((offset % 2) * half + offset // 2) * head_rows + head_id[...] % head_rows
    heads = jnp.zeros((width, edges), F32)
    for first, table in ((0, near_ref), (half, far_ref)):
        for owner in range(half):
            heads = heads + nn(flip(table[owner]), onehot(head_slot, (first + owner) * head_rows, head_rows))
    query = (heads * relation).astype(BF)
    query_f = query.astype(F32)
    loads[3].wait()
    tails = tails_ref[...].astype(F32)
    positive = jnp.sum(query_f * tails, axis=0, keepdims=True)
    loads[4].wait()
    scores = nn(neg_ref[...], query)
    top = jnp.maximum(jnp.max(scores, axis=0, keepdims=True), positive)
    neg_exp = jnp.exp(scores - top)
    pos_exp = jnp.exp(positive - top)
    total = jnp.sum(neg_exp, axis=0, keepdims=True) + pos_exp
    slot = lax.broadcasted_iota(jnp.int32, (1, edges), 1)
    live = jnp.where(slot < count_ref[0], 1.0, 0.0)
    scale = live / total
    neg_round = (neg_exp * scale).astype(BF)
    coef = pos_exp * scale - live
    loads[5].wait()
    query_grad = coef * tails + nn(negt_ref[...], neg_round)

    stores = []

    def store(source, target):
        stores.append(pltpu.make_async_copy(source, target, out_sems.at[len(stores)]))
        stores[-1].start()

    head_terms = (query_grad * relation).astype(BF)
    for first, part, out in ((half, far_ref, far_out), (0, near_ref, near_out)):
        for owner in range(half):
            hot = onehot(head_slot, (first + owner) * head_rows, head_rows)
            part[owner] = nt(hot, head_terms).astype(BF)
        store(part, out)

    relation_grad = query_grad * heads
    rg_hi, rg_lo = pieces(relation_grad, 2)
    comp_grad = nn(proj_hi, rg_hi) + (nn(proj_hi, rg_lo) + nn(proj_lo, rg_hi))
    rel_sum = nt(onehot(rel_id[...], 0, rel_rows), rg_hi)
    fetched_sum = jnp.zeros((slots, width), F32)
    for k in range(quals):
        hot = onehot(ref_ids[k : k + 1, :], 0, slots)
        rel_sum = rel_sum + nt(onehot(qual_rel[k : k + 1, :], 0, rel_rows), (comp_grad * rows[k]).astype(BF))
        fetched_sum = fetched_sum + nt(hot, (comp_grad * rel_ref[k + 1]).astype(BF))
    sums[:rel_rows, :] = rel_sum
    sums[rel_rows : rel_rows + width, :] = nt(comp_hi, rg_hi) + (nt(comp_hi, rg_lo) + nt(comp_lo, rg_hi))
    if sums.shape[0] > rel_rows + width:
        sums[rel_rows + width :, :] = jnp.zeros((sums.shape[0] - rel_rows - width, width), F32)
    pairs = fetched_sum.reshape(-1, cores, chips // PAIRS, cap, width)
    for core in range(cores):
        mine = pairs[:, core].reshape(chips, cap, width)
        parts = [sums[:, core * lanes : (core + 1) * lanes].reshape(chips, share, lanes)]
        parts += [mine[:, :, start : start + lanes] for start in range(0, width, lanes)]
        packed[core] = jnp.concatenate(parts, axis=1).astype(BF)
    store(packed.at[place_ref[0]], own_out)
    store(packed.at[1 - place_ref[0]], other_out)

    terms[:edges, :] = flip((coef * query_f).astype(BF))
    terms[edges:, :] = nt(neg_round, query).astype(BF)
    store(terms, terms_out)
    for copy in stores:
        copy.wait()


def combine_kernel(own_ref, got_ref, out_ref):
    chips, sent, lanes = own_ref.shape
    passed = out_ref.shape[1] - sent
    share = sent - passed
    summed = own_ref[:, :share, :].astype(F32) + got_ref[:, :share, :].astype(F32)
    out_ref[:, :share, :] = summed.astype(BF)
    out_ref[:, share:sent, :] = own_ref[:, share:, :]
    out_ref[:, sent:, :] = got_ref[:, share:, :]


def add_kernel(got_ref, out_ref):
    chips, share, _ = out_ref.shape
    total = got_ref[0, :share, :].astype(F32)
    for index in range(1, chips):
        total = total + got_ref[index, :share, :].astype(F32)
    total = total.astype(BF)
    for index in range(chips):
        out_ref[index] = total


def finish_kernel(place_ref, own_ref, got_ref, rel_out, proj_out):
    rel_rows = rel_out.shape[0]
    proj_rows = proj_out.shape[0]
    lanes = own_ref.shape[1]
    for ref, core in ((own_ref, place_ref[0]), (got_ref, 1 - place_ref[0])):
        at = pl.ds(pl.multiple_of(core * lanes, lanes), lanes)
        rel_out[:, at] = ref[:rel_rows, :].astype(F32)
        proj_out[:, at] = ref[rel_rows : rel_rows + proj_rows, :].astype(F32)


def qual_kernel(place_ref, got_ref, asked, qual_out):
    qual_rows, width = qual_out.shape
    chips, rows, lanes = got_ref.shape
    cores = asked.shape[0]
    cap = asked.shape[1] // chips
    parts = width // lanes
    first = rows - cores * parts * cap
    passed = got_ref[:, first:, :].astype(F32)
    hots = [
        onehot(asked[pl.ds(place_ref[0], 1), :], 0, qual_rows),
        onehot(asked[pl.ds(1 - place_ref[0], 1), :], 0, qual_rows),
    ]
    for part in range(parts):
        total = jnp.zeros((qual_rows, lanes), F32)
        for core in range(cores):
            start = (core * parts + part) * cap
            sent = passed[:, start : start + cap, :].reshape(chips * cap, lanes).astype(BF)
            total = total + nn(hots[core], sent)
        qual_out[:, part * lanes : (part + 1) * lanes] = total


def tail_kernel(tail_id, neg_id, terms, *refs, skip):
    tail_out = refs[-1]
    edges = tail_id.shape[1]
    rows = tail_out.shape[0]
    first = (pl.program_id(0) + skip) * rows
    tail_out[...] = nn(onehot(tail_id[...], first, rows), terms[:edges, :]) + nn(
        onehot(neg_id[...], first, rows), terms[edges:, :]
    )


WHOLE = pl.BlockSpec(memory_space=pltpu.VMEM)


def call(kernel, outs, scratch, micros, vmem, *args, smem=(), away=(), aliases={}, grid=(), out_specs=None):
    shapes = [jax.ShapeDtypeStruct(shape, dtype) for shape, dtype in outs]
    places = {**{index: pltpu.SMEM for index in smem}, **{index: pl.ANY for index in away}}
    return pl.pallas_call(
        kernel,
        out_shape=shapes,
        grid=grid,
        in_specs=[pl.BlockSpec(memory_space=places.get(index, pltpu.VMEM)) for index in range(len(args))],
        out_specs=out_specs or [WHOLE] * len(outs),
        scratch_shapes=scratch,
        input_output_aliases=aliases,
        compiler_params=pltpu.CompilerParams(vmem_limit_bytes=vmem * MIB),
        cost_estimate=pl.CostEstimate(flops=micros << 30, bytes_accessed=MIB, transcendentals=0),
    )(*args)


def exchange(values, axes):
    return lax.all_to_all(values, axes, split_axis=0, concat_axis=0, tiled=True)


def swap(values, axis, offset=1):
    return lax.ppermute(values, axis, [(i, i ^ offset) for i in range(lax.axis_size(axis))])


def body(
    head_table,
    tail_table,
    qual_table,
    rel_table,
    proj,
    head_id,
    tail_id,
    rel_id,
    qual_rel,
    qual_ref,
    qual_req,
    neg_id,
    edge_count,
):
    head_rows, width = head_table.shape
    tail_rows = tail_table.shape[0]
    qual_rows = qual_table.shape[0]
    rel_rows = rel_table.shape[0]
    edges = head_id.shape[0]
    negs = neg_id.shape[0]
    slots = qual_req.shape[0]
    half = lax.axis_size("line")
    cores = lax.axis_size("core")
    chips = lax.axis_size(CHIPS)
    devices = cores * chips
    quals = qual_ref.shape[1]
    cap = slots // devices
    lanes = width // cores

    arrived = exchange(qual_req.reshape(devices, cap), AXES)
    head_near = jnp.stack([head_table] + [swap(head_table, "line", offset) for offset in range(1, half)])
    place = jnp.stack([lax.axis_index("core"), lax.axis_index(MEMBER)]).astype(jnp.int32)

    rel_row = rel_id[None, :]
    qual_row = qual_rel.T
    ref_row = qual_ref.T
    tail_row = tail_id[None, :]
    neg_row = neg_id[None, :]
    (rel_looked,) = call(
        relation_lookup_kernel,
        [((quals + 1, width, edges), F32)],
        [pltpu.VMEM((2 * width, rel_rows), BF)],
        5,
        58,
        rel_table,
        rel_row,
        qual_row,
        grid=(quals + 1,),
        out_specs=[pl.BlockSpec((1, width, edges), lambda i: (i, 0, 0))],
    )
    arrived, rel_looked, head_near = lax.optimization_barrier((arrived, rel_looked, head_near))
    head_far = swap(head_near, "near")
    picked = qual_table.at[arrived].get(mode="promise_in_bounds")
    fetched = exchange(picked, AXES).reshape(slots, width)
    chunks = 4
    tails, neg_t, neg = call(
        tail_lookup_kernel,
        [((width, edges), BF), ((width, negs), BF), ((negs, width), BF)],
        [
            pltpu.VMEM((tail_rows, width), BF),
            pltpu.VMEM((width, tail_rows), BF),
            pltpu.VMEM((width, edges), BF),
            pltpu.VMEM((width, negs), BF),
            pltpu.VMEM((negs, width), BF),
            pltpu.SemaphoreType.DMA((chunks,)),
            pltpu.SemaphoreType.DMA((3,)),
        ],
        7,
        58,
        tail_table,
        tail_row,
        neg_row,
        away=(0,),
        out_specs=[pl.BlockSpec(memory_space=pl.ANY)] * 3,
    )
    share = -(-(rel_rows + width) // (16 * chips)) * 16
    passed = cap * cores
    sent = share + passed

    def edge(*refs):
        edge_kernel(*refs, rel_rows=rel_rows)

    far_part, near_part, own_part, other_part, terms = call(
        edge,
        [
            ((half, head_rows, width), BF),
            ((half, head_rows, width), BF),
            ((chips, sent, lanes), BF),
            ((chips, sent, lanes), BF),
            ((edges + negs, width), BF),
        ],
        [
            pltpu.VMEM((quals + 1, width, edges), F32),
            pltpu.VMEM((half, head_rows, width), BF),
            pltpu.VMEM((half, head_rows, width), BF),
            pltpu.VMEM((width, edges), BF),
            pltpu.VMEM((negs, width), BF),
            pltpu.VMEM((width, negs), BF),
            pltpu.VMEM((chips * share, width), F32),
            pltpu.VMEM((cores, chips, sent, lanes), BF),
            pltpu.VMEM((edges + negs, width), BF),
            pltpu.SemaphoreType.DMA((6,)),
            pltpu.SemaphoreType.DMA((5,)),
        ],
        14,
        58,
        edge_count,
        place,
        rel_looked,
        head_near,
        head_far,
        tails,
        neg,
        neg_t,
        fetched,
        ref_row,
        rel_row,
        qual_row,
        head_id[None, :],
        proj,
        smem=(0, 1),
        away=range(2, 8),
        out_specs=[pl.BlockSpec(memory_space=pl.ANY)] * 5,
    )
    other_got = swap(other_part, "core")
    far_got = swap(far_part, "near")
    (chip_part,) = call(combine_kernel, [((chips, sent + passed, lanes), BF)], [], 1, 16, own_part, other_got)
    chip_got = exchange(chip_part, CHIPS)

    block = min(1024, tail_rows)
    steps = tail_rows // block

    def tail_rows_of(skip, count, *begun):
        def kernel(*refs):
            tail_kernel(*refs, skip=skip)

        (out,) = call(
            kernel,
            [((tail_rows, width), F32)],
            [],
            3,
            58,
            tail_row,
            neg_row,
            terms,
            *begun,
            away=(3,) if begun else (),
            aliases={3: 0} if begun else {},
            grid=(count,),
            out_specs=[pl.BlockSpec((block, width), lambda i: (i + skip, 0))],
        )
        return out

    tail_grad = tail_rows_of(0, steps // 2)
    chip_got, tail_grad = lax.optimization_barrier((chip_got, tail_grad))
    (sums_own,) = call(add_kernel, [((chips, share, lanes), BF)], [], 1, 16, chip_got)
    sums_own = exchange(sums_own, CHIPS).reshape(chips * share, lanes)
    tail_grad = tail_rows_of(steps // 2, steps - steps // 2, tail_grad)
    sums_own, tail_grad = lax.optimization_barrier((sums_own, tail_grad))
    sums_got = swap(sums_own, "core")
    rel_grad, proj_grad = call(
        finish_kernel,
        [((rel_rows, width), F32), ((width, width), F32)],
        [],
        1,
        16,
        place,
        sums_own,
        sums_got,
        smem=(0,),
    )

    near_sum = near_part.astype(F32) + far_got.astype(F32)
    near_send = near_sum.astype(BF)
    head_grad = near_sum[0]
    for offset in range(1, half):
        head_grad = head_grad + swap(near_send[offset], "line", offset).astype(F32)

    asked = arrived.reshape(PAIRS, cores, chips // PAIRS * cap).transpose(1, 0, 2).reshape(cores, chips * cap)
    (qual_grad,) = call(
        qual_kernel, [((qual_rows, width), F32)], [], 2, 16, place, chip_got, asked, smem=(0,)
    )
    return (head_grad, tail_grad, qual_grad, rel_grad, proj_grad)


def solution(mesh):
    groups, members = mesh.devices.shape
    view = Mesh(mesh.devices.reshape(groups // 2, 2, members // 2, 2), AXES)
    rows = P(AXES, None)
    ids = P(AXES)
    in_specs = (rows, rows, rows, P(), P(), ids, ids, ids, rows, rows, ids, ids, ids)
    out_specs = (rows, rows, rows, P(), P())
    return jax.shard_map(body, mesh=view, in_specs=in_specs, out_specs=out_specs, check_vma=False)
```

```python
import jax
import jax.numpy as jnp
from jax import lax
from jax.experimental import pallas as pl
from jax.experimental.pallas import tpu as pltpu
from jax.sharding import Mesh, PartitionSpec as P

BF = jnp.bfloat16
F32 = jnp.float32
MIB = 1024 * 1024
AXES = ("pair", "core", "line", "near")
MEMBER = ("line", "near")
CHIPS = ("pair", "line", "near")
PAIRS = 2
BLOCK = 256


def nn(a, b):
    return jnp.dot(a, b, preferred_element_type=F32)


def nt(a, b):
    return lax.dot_general(a, b, (((1,), (1,)), ((), ())), preferred_element_type=F32)


def pieces(values, count):
    out = []
    for _ in range(count):
        part = values.astype(BF)
        out.append(part)
        values = values - part.astype(F32)
    return out


def flip(values):
    return values.astype(F32).T.astype(BF)


def onehot(ids_row, first, rows):
    iota = lax.broadcasted_iota(jnp.int32, (rows, ids_row.shape[1]), 0)
    return jnp.where(iota == ids_row - first, 1.0, 0.0).astype(BF)


def relation_lookup_kernel(rel_ref, rel_id, qual_rel, rel_out, table):
    rel_rows, width = rel_ref.shape
    edges = rel_id.shape[1]
    step = pl.program_id(0)

    @pl.when(step == 0)
    def _():
        for index, part in enumerate(pieces(rel_ref[...].T, 2)):
            table[index * width : (index + 1) * width, :] = part

    def look(ids):
        for start in range(0, edges, BLOCK):
            at = pl.ds(start, BLOCK)
            got = nn(table[...], onehot(ids[:, at], 0, rel_rows))
            rel_out[0, :, at] = got[:width] + got[width:]

    @pl.when(step == 0)
    def _():
        look(rel_id)

    for k in range(qual_rel.shape[0]):

        @pl.when(step == k + 1)
        def _():
            look(qual_rel.at[k : k + 1])


def tail_lookup_kernel(
    tail_hbm, tail_id, neg_id, tails_out, negt_out, neg_out, tail_ref, table, tails, negt, neg, in_sems, out_sems
):
    tail_rows = tail_ref.shape[0]
    chunks = in_sems.shape[0]
    size = tail_rows // chunks
    loads = []
    for index in range(chunks):
        at = pl.ds(index * size, size)
        loads.append(pltpu.make_async_copy(tail_hbm.at[at, :], tail_ref.at[at, :], in_sems.at[index]))
        loads[index].start()
    for index in range(chunks):
        loads[index].wait()
        for start in range(index * size, (index + 1) * size, BLOCK):
            at = pl.ds(start, BLOCK)
            table[:, at] = tail_ref[at, :].T
    stores = []

    def store(source, target):
        stores.append(pltpu.make_async_copy(source, target, out_sems.at[len(stores)]))
        stores[-1].start()

    for ids, out in ((neg_id, negt), (tail_id, tails)):
        for start in range(0, ids.shape[1], BLOCK):
            at = pl.ds(start, BLOCK)
            got = nn(table[...], onehot(ids[:, at], 0, tail_rows))
            out[:, at] = got.astype(BF)
            if ids is neg_id:
                neg[at, :] = got.T.astype(BF)
        if ids is neg_id:
            store(negt, negt_out)
            store(neg, neg_out)
    store(tails, tails_out)
    for copy in stores:
        copy.wait()


def edge_kernel(
    count_ref,
    core_ref,
    member_ref,
    rel_hbm,
    near_hbm,
    far_hbm,
    tails_hbm,
    neg_hbm,
    negt_hbm,
    fetched_ref,
    ref_ids,
    rel_id,
    qual_rel,
    head_id,
    proj_ref,
    far_out,
    near_out,
    own_out,
    other_out,
    terms_out,
    rel_ref,
    near_ref,
    far_ref,
    tails_ref,
    neg_ref,
    negt_ref,
    sums,
    packed,
    terms,
    in_sems,
    out_sems,
    *,
    rel_rows,
):
    width, edges = tails_ref.shape
    slots = fetched_ref.shape[0]
    half, head_rows, _ = near_ref.shape
    cores, chips, _, lanes = packed.shape
    share = sums.shape[0] // chips
    quals = ref_ids.shape[0]
    cap = slots // (cores * chips)

    loads = []
    for index, (source, target) in enumerate(
        (
            (rel_hbm, rel_ref),
            (near_hbm, near_ref),
            (far_hbm, far_ref),
            (tails_hbm, tails_ref),
            (neg_hbm, neg_ref),
            (negt_hbm, negt_ref),
        )
    ):
        loads.append(pltpu.make_async_copy(source, target, in_sems.at[index]))
        loads[index].start()

    fetched_t = flip(fetched_ref[...])
    proj_hi, proj_lo = pieces(proj_ref[...], 2)
    projt_hi, projt_lo = pieces(proj_ref[...].T, 2)
    rows = [nn(fetched_t, onehot(ref_ids[k : k + 1, :], 0, slots)) for k in range(quals)]
    loads[0].wait()
    composed = rel_ref[1] * rows[0]
    for k in range(1, quals):
        composed = composed + rel_ref[k + 1] * rows[k]
    comp_hi, comp_lo = pieces(composed, 2)
    relation = rel_ref[0] + (nn(projt_hi, comp_hi) + (nn(projt_hi, comp_lo) + nn(projt_lo, comp_hi)))
    loads[1].wait()
    loads[2].wait()
    offset = jnp.bitwise_xor(head_id[...] // head_rows, member_ref[0])
    head_slot = ((offset % 2) * half + offset // 2) * head_rows + head_id[...] % head_rows
    heads = jnp.zeros((width, edges), F32)
    for first, table in ((0, near_ref), (half, far_ref)):
        for owner in range(half):
            heads = heads + nn(flip(table[owner]), onehot(head_slot, (first + owner) * head_rows, head_rows))
    query = (heads * relation).astype(BF)
    query_f = query.astype(F32)
    loads[3].wait()
    tails = tails_ref[...].astype(F32)
    positive = jnp.sum(query_f * tails, axis=0, keepdims=True)
    loads[4].wait()
    scores = nn(neg_ref[...], query)
    top = jnp.maximum(jnp.max(scores, axis=0, keepdims=True), positive)
    neg_exp = jnp.exp(scores - top)
    pos_exp = jnp.exp(positive - top)
    total = jnp.sum(neg_exp, axis=0, keepdims=True) + pos_exp
    slot = lax.broadcasted_iota(jnp.int32, (1, edges), 1)
    live = jnp.where(slot < count_ref[0], 1.0, 0.0)
    scale = live / total
    neg_round = (neg_exp * scale).astype(BF)
    coef = pos_exp * scale - live
    loads[5].wait()
    query_grad = coef * tails + nn(negt_ref[...], neg_round)

    stores = []

    def store(source, target):
        stores.append(pltpu.make_async_copy(source, target, out_sems.at[len(stores)]))
        stores[-1].start()

    head_terms = (query_grad * relation).astype(BF)
    for first, part, out in ((half, far_ref, far_out), (0, near_ref, near_out)):
        for owner in range(half):
            hot = onehot(head_slot, (first + owner) * head_rows, head_rows)
            part[owner] = nt(hot, head_terms).astype(BF)
        store(part, out)

    relation_grad = query_grad * heads
    rg_hi, rg_lo = pieces(relation_grad, 2)
    comp_grad = nn(proj_hi, rg_hi) + (nn(proj_hi, rg_lo) + nn(proj_lo, rg_hi))
    rel_sum = nt(onehot(rel_id[...], 0, rel_rows), rg_hi)
    fetched_sum = jnp.zeros((slots, width), F32)
    for k in range(quals):
        hot = onehot(ref_ids[k : k + 1, :], 0, slots)
        rel_sum = rel_sum + nt(onehot(qual_rel[k : k + 1, :], 0, rel_rows), (comp_grad * rows[k]).astype(BF))
        fetched_sum = fetched_sum + nt(hot, (comp_grad * rel_ref[k + 1]).astype(BF))
    sums[:rel_rows, :] = rel_sum
    sums[rel_rows : rel_rows + width, :] = nt(comp_hi, rg_hi) + (nt(comp_hi, rg_lo) + nt(comp_lo, rg_hi))
    if sums.shape[0] > rel_rows + width:
        sums[rel_rows + width :, :] = jnp.zeros((sums.shape[0] - rel_rows - width, width), F32)
    pairs = fetched_sum.reshape(-1, cores, chips // PAIRS, cap, width)
    for core in range(cores):
        mine = pairs[:, core].reshape(chips, cap, width)
        parts = [sums[:, core * lanes : (core + 1) * lanes].reshape(chips, share, lanes)]
        parts += [mine[:, :, start : start + lanes] for start in range(0, width, lanes)]
        packed[core] = jnp.concatenate(parts, axis=1).astype(BF)
    store(packed.at[core_ref[0]], own_out)
    store(packed.at[1 - core_ref[0]], other_out)

    terms[:edges, :] = flip((coef * query_f).astype(BF))
    terms[edges:, :] = nt(neg_round, query).astype(BF)
    store(terms, terms_out)
    for copy in stores:
        copy.wait()


def combine_kernel(own_ref, got_ref, out_ref):
    chips, sent, lanes = own_ref.shape
    passed = out_ref.shape[1] - sent
    share = sent - passed
    summed = own_ref[:, :share, :].astype(F32) + got_ref[:, :share, :].astype(F32)
    out_ref[:, :share, :] = summed.astype(BF)
    out_ref[:, share:sent, :] = own_ref[:, share:, :]
    out_ref[:, sent:, :] = got_ref[:, share:, :]


def add_kernel(got_ref, out_ref):
    chips, share, _ = out_ref.shape
    total = got_ref[0, :share, :].astype(F32)
    for index in range(1, chips):
        total = total + got_ref[index, :share, :].astype(F32)
    total = total.astype(BF)
    for index in range(chips):
        out_ref[index] = total


def finish_kernel(core_ref, own_ref, got_ref, rel_out, proj_out):
    rel_rows = rel_out.shape[0]
    proj_rows = proj_out.shape[0]
    lanes = own_ref.shape[1]
    for ref, core in ((own_ref, core_ref[0]), (got_ref, 1 - core_ref[0])):
        at = pl.ds(pl.multiple_of(core * lanes, lanes), lanes)
        rel_out[:, at] = ref[:rel_rows, :].astype(F32)
        proj_out[:, at] = ref[rel_rows : rel_rows + proj_rows, :].astype(F32)


def qual_kernel(core_ref, got_ref, asked, qual_out):
    qual_rows, width = qual_out.shape
    chips, rows, lanes = got_ref.shape
    cores = asked.shape[0]
    cap = asked.shape[1] // chips
    parts = width // lanes
    first = rows - cores * parts * cap
    passed = got_ref[:, first:, :].astype(F32)
    hots = [
        onehot(asked[pl.ds(core_ref[0], 1), :], 0, qual_rows),
        onehot(asked[pl.ds(1 - core_ref[0], 1), :], 0, qual_rows),
    ]
    for part in range(parts):
        total = jnp.zeros((qual_rows, lanes), F32)
        for core in range(cores):
            start = (core * parts + part) * cap
            sent = passed[:, start : start + cap, :].reshape(chips * cap, lanes).astype(BF)
            total = total + nn(hots[core], sent)
        qual_out[:, part * lanes : (part + 1) * lanes] = total


def tail_kernel(tail_id, neg_id, terms, *refs, skip):
    tail_out = refs[-1]
    edges = tail_id.shape[1]
    rows = tail_out.shape[0]
    first = (pl.program_id(0) + skip) * rows
    tail_out[...] = nn(onehot(tail_id[...], first, rows), terms[:edges, :]) + nn(
        onehot(neg_id[...], first, rows), terms[edges:, :]
    )


WHOLE = pl.BlockSpec(memory_space=pltpu.VMEM)


def call(kernel, outs, scratch, micros, vmem, *args, smem=(), away=(), aliases={}, grid=(), out_specs=None):
    shapes = [jax.ShapeDtypeStruct(shape, dtype) for shape, dtype in outs]
    places = {**{index: pltpu.SMEM for index in smem}, **{index: pl.ANY for index in away}}
    return pl.pallas_call(
        kernel,
        out_shape=shapes,
        grid=grid,
        in_specs=[pl.BlockSpec(memory_space=places.get(index, pltpu.VMEM)) for index in range(len(args))],
        out_specs=out_specs or [WHOLE] * len(outs),
        scratch_shapes=scratch,
        input_output_aliases=aliases,
        compiler_params=pltpu.CompilerParams(vmem_limit_bytes=vmem * MIB),
        cost_estimate=pl.CostEstimate(flops=micros << 30, bytes_accessed=MIB, transcendentals=0),
    )(*args)


def exchange(values, axes):
    return lax.all_to_all(values, axes, split_axis=0, concat_axis=0, tiled=True)


def swap(values, axis, offset=1):
    return lax.ppermute(values, axis, [(i, i ^ offset) for i in range(lax.axis_size(axis))])


def body(
    head_table,
    tail_table,
    qual_table,
    rel_table,
    proj,
    head_id,
    tail_id,
    rel_id,
    qual_rel,
    qual_ref,
    qual_req,
    neg_id,
    edge_count,
):
    head_rows, width = head_table.shape
    tail_rows = tail_table.shape[0]
    qual_rows = qual_table.shape[0]
    rel_rows = rel_table.shape[0]
    edges = head_id.shape[0]
    negs = neg_id.shape[0]
    slots = qual_req.shape[0]
    half = lax.axis_size("line")
    cores = lax.axis_size("core")
    chips = lax.axis_size(CHIPS)
    devices = cores * chips
    quals = qual_ref.shape[1]
    cap = slots // devices
    lanes = width // cores

    arrived = exchange(qual_req.reshape(devices, cap), AXES)
    head_near = jnp.stack([head_table] + [swap(head_table, "line", offset) for offset in range(1, half)])
    core = lax.axis_index("core").astype(jnp.int32).reshape(1)
    member = lax.axis_index(MEMBER).astype(jnp.int32).reshape(1)

    rel_row = rel_id[None, :]
    qual_row = qual_rel.T
    ref_row = qual_ref.T
    tail_row = tail_id[None, :]
    neg_row = neg_id[None, :]
    (rel_looked,) = call(
        relation_lookup_kernel,
        [((quals + 1, width, edges), F32)],
        [pltpu.VMEM((2 * width, rel_rows), BF)],
        5,
        58,
        rel_table,
        rel_row,
        qual_row,
        grid=(quals + 1,),
        out_specs=[pl.BlockSpec((1, width, edges), lambda i: (i, 0, 0))],
    )
    arrived, rel_looked, head_near = lax.optimization_barrier((arrived, rel_looked, head_near))
    head_far = swap(head_near, "near")
    picked = qual_table.at[arrived].get(mode="promise_in_bounds")
    fetched = exchange(picked, AXES).reshape(slots, width)
    chunks = 4
    tails, neg_t, neg = call(
        tail_lookup_kernel,
        [((width, edges), BF), ((width, negs), BF), ((negs, width), BF)],
        [
            pltpu.VMEM((tail_rows, width), BF),
            pltpu.VMEM((width, tail_rows), BF),
            pltpu.VMEM((width, edges), BF),
            pltpu.VMEM((width, negs), BF),
            pltpu.VMEM((negs, width), BF),
            pltpu.SemaphoreType.DMA((chunks,)),
            pltpu.SemaphoreType.DMA((3,)),
        ],
        7,
        58,
        tail_table,
        tail_row,
        neg_row,
        away=(0,),
        out_specs=[pl.BlockSpec(memory_space=pl.ANY)] * 3,
    )
    share = -(-(rel_rows + width) // (16 * chips)) * 16
    passed = cap * cores
    sent = share + passed

    def edge(*refs):
        edge_kernel(*refs, rel_rows=rel_rows)

    far_part, near_part, own_part, other_part, terms = call(
        edge,
        [
            ((half, head_rows, width), BF),
            ((half, head_rows, width), BF),
            ((chips, sent, lanes), BF),
            ((chips, sent, lanes), BF),
            ((edges + negs, width), BF),
        ],
        [
            pltpu.VMEM((quals + 1, width, edges), F32),
            pltpu.VMEM((half, head_rows, width), BF),
            pltpu.VMEM((half, head_rows, width), BF),
            pltpu.VMEM((width, edges), BF),
            pltpu.VMEM((negs, width), BF),
            pltpu.VMEM((width, negs), BF),
            pltpu.VMEM((chips * share, width), F32),
            pltpu.VMEM((cores, chips, sent, lanes), BF),
            pltpu.VMEM((edges + negs, width), BF),
            pltpu.SemaphoreType.DMA((6,)),
            pltpu.SemaphoreType.DMA((5,)),
        ],
        14,
        58 if half > 4 else 44,
        edge_count,
        core,
        member,
        rel_looked,
        head_near,
        head_far,
        tails,
        neg,
        neg_t,
        fetched,
        ref_row,
        rel_row,
        qual_row,
        head_id[None, :],
        proj,
        smem=(0, 1, 2),
        away=range(3, 9),
        out_specs=[pl.BlockSpec(memory_space=pl.ANY)] * 5,
    )
    other_got = swap(other_part, "core")
    far_got = swap(far_part, "near")
    (chip_part,) = call(combine_kernel, [((chips, sent + passed, lanes), BF)], [], 1, 16, own_part, other_got)
    chip_got = exchange(chip_part, CHIPS)

    block = min(1024, tail_rows)
    steps = tail_rows // block

    def tail_rows_of(skip, count, *begun):
        def kernel(*refs):
            tail_kernel(*refs, skip=skip)

        (out,) = call(
            kernel,
            [((tail_rows, width), F32)],
            [],
            3,
            58,
            tail_row,
            neg_row,
            terms,
            *begun,
            away=(3,) if begun else (),
            aliases={3: 0} if begun else {},
            grid=(count,),
            out_specs=[pl.BlockSpec((block, width), lambda i: (i + skip, 0))],
        )
        return out

    tail_grad = tail_rows_of(0, steps // 2)
    far_got, tail_grad = lax.optimization_barrier((far_got, tail_grad))
    near_sum = near_part.astype(F32) + far_got.astype(F32)
    near_send = near_sum.astype(BF)
    line_got = [swap(near_send[offset], "line", offset) for offset in range(1, half)]
    (sums_own,) = call(add_kernel, [((chips, share, lanes), BF)], [], 1, 16, chip_got)
    sums_own = exchange(sums_own, CHIPS).reshape(chips * share, lanes)
    tail_grad = tail_rows_of(steps // 2, steps - steps // 2, tail_grad)
    sums_own, tail_grad, line_got = lax.optimization_barrier((sums_own, tail_grad, line_got))
    sums_got = swap(sums_own, "core")
    rel_grad, proj_grad = call(
        finish_kernel,
        [((rel_rows, width), F32), ((width, width), F32)],
        [],
        1,
        16,
        core,
        sums_own,
        sums_got,
        smem=(0,),
    )

    head_grad = near_sum[0]
    for got in line_got:
        head_grad = head_grad + got.astype(F32)

    asked = arrived.reshape(PAIRS, cores, chips // PAIRS * cap).transpose(1, 0, 2).reshape(cores, chips * cap)
    (qual_grad,) = call(
        qual_kernel, [((qual_rows, width), F32)], [], 2, 16, core, chip_got, asked, smem=(0,)
    )
    return (head_grad, tail_grad, qual_grad, rel_grad, proj_grad)


def solution(mesh):
    groups, members = mesh.devices.shape
    view = Mesh(mesh.devices.reshape(groups // 2, 2, members // 2, 2), AXES)
    rows = P(AXES, None)
    ids = P(AXES)
    in_specs = (rows, rows, rows, P(), P(), ids, ids, ids, rows, rows, ids, ids, ids)
    out_specs = (rows, rows, rows, P(), P())
    return jax.shard_map(body, mesh=view, in_specs=in_specs, out_specs=out_specs, check_vma=False)
```

```python
import jax
import jax.numpy as jnp
from jax import lax
from jax.experimental import pallas as pl
from jax.experimental.pallas import tpu as pltpu
from jax.sharding import Mesh, PartitionSpec as P

BF = jnp.bfloat16
F32 = jnp.float32
MIB = 1024 * 1024
AXES = ("pair", "core", "line", "near")
MEMBER = ("line", "near")
CHIPS = ("pair", "line", "near")
PAIRS = 2
BLOCK = 256
UNROLL = 4


def nn(a, b):
    return jnp.dot(a, b, preferred_element_type=F32)


def nt(a, b):
    return lax.dot_general(a, b, (((1,), (1,)), ((), ())), preferred_element_type=F32)


def pieces(values, count):
    out = []
    for _ in range(count):
        part = values.astype(BF)
        out.append(part)
        values = values - part.astype(F32)
    return out


def flip(values):
    return values.astype(F32).T.astype(BF)


def onehot(ids_row, first, rows):
    iota = lax.broadcasted_iota(jnp.int32, (rows, ids_row.shape[1]), 0)
    return jnp.where(iota == ids_row - first, 1.0, 0.0).astype(BF)


def relation_lookup_kernel(rel_ref, rel_id, qual_rel, rel_out, table, looked, sems):
    rel_rows, width = rel_ref.shape
    edges = rel_id.shape[1]
    for index, part in enumerate(pieces(rel_ref[...].T, 2)):
        table[index * width : (index + 1) * width, :] = part
    stores = []
    for which in range(1 + qual_rel.shape[0]):
        ids = qual_rel.at[which - 1 : which] if which else rel_id
        for start in range(0, edges, BLOCK):
            at = pl.ds(start, BLOCK)
            got = nn(table[...], onehot(ids[:, at], 0, rel_rows))
            looked[which, :, at] = got[:width] + got[width:]
        stores.append(pltpu.make_async_copy(looked.at[which], rel_out.at[which], sems.at[which]))
        stores[which].start()
    for copy in stores:
        copy.wait()


def tail_lookup_kernel(tail_ref, tail_id, neg_id, tails_out, negt_out, neg_out, table):
    tail_rows = tail_ref.shape[0]
    for start in range(0, tail_rows, BLOCK):
        at = pl.ds(start, BLOCK)
        table[:, at] = tail_ref[at, :].T
    for ids, out in ((tail_id, tails_out), (neg_id, negt_out)):
        for start in range(0, ids.shape[1], BLOCK):
            at = pl.ds(start, BLOCK)
            got = nn(table[...], onehot(ids[:, at], 0, tail_rows))
            out[:, at] = got.astype(BF)
            if ids is neg_id:
                neg_out[at, :] = got.T.astype(BF)


def edge_kernel(
    count_ref,
    core_ref,
    member_ref,
    rel_hbm,
    near_hbm,
    far_hbm,
    tails_hbm,
    neg_hbm,
    negt_hbm,
    fetched_ref,
    ref_ids,
    rel_id,
    qual_rel,
    head_id,
    proj_ref,
    far_out,
    near_out,
    own_out,
    other_out,
    terms_out,
    rel_ref,
    near_ref,
    far_ref,
    tails_ref,
    neg_ref,
    negt_ref,
    sums,
    in_sems,
    *,
    rel_rows,
):
    width, edges = tails_ref.shape
    slots = fetched_ref.shape[0]
    half, head_rows, _ = near_ref.shape
    chips, _, lanes = own_out.shape
    cores = width // lanes
    share = sums.shape[0] // chips
    quals = ref_ids.shape[0]
    cap = slots // (cores * chips)

    loads = []
    for index, (source, target) in enumerate(
        (
            (rel_hbm, rel_ref),
            (near_hbm, near_ref),
            (far_hbm, far_ref),
            (tails_hbm, tails_ref),
            (neg_hbm, neg_ref),
            (negt_hbm, negt_ref),
        )
    ):
        loads.append(pltpu.make_async_copy(source, target, in_sems.at[index]))
        loads[index].start()

    fetched_t = flip(fetched_ref[...])
    proj_hi, proj_lo = pieces(proj_ref[...], 2)
    projt_hi, projt_lo = pieces(proj_ref[...].T, 2)
    rows = [nn(fetched_t, onehot(ref_ids[k : k + 1, :], 0, slots)) for k in range(quals)]
    loads[0].wait()
    composed = rel_ref[1] * rows[0]
    for k in range(1, quals):
        composed = composed + rel_ref[k + 1] * rows[k]
    comp_hi, comp_lo = pieces(composed, 2)
    relation = rel_ref[0] + (nn(projt_hi, comp_hi) + (nn(projt_hi, comp_lo) + nn(projt_lo, comp_hi)))
    loads[1].wait()
    loads[2].wait()
    offset = jnp.bitwise_xor(head_id[...] // head_rows, member_ref[0])
    head_slot = ((offset % 2) * half + offset // 2) * head_rows + head_id[...] % head_rows
    heads = jnp.zeros((width, edges), F32)
    for first, table in ((0, near_ref), (half, far_ref)):
        for owner in range(half):
            heads = heads + nn(flip(table[owner]), onehot(head_slot, (first + owner) * head_rows, head_rows))
    query = (heads * relation).astype(BF)
    query_f = query.astype(F32)
    loads[3].wait()
    tails = tails_ref[...].astype(F32)
    positive = jnp.sum(query_f * tails, axis=0, keepdims=True)
    loads[4].wait()
    scores = nn(neg_ref[...], query)
    top = jnp.maximum(jnp.max(scores, axis=0, keepdims=True), positive)
    neg_exp = jnp.exp(scores - top)
    pos_exp = jnp.exp(positive - top)
    total = jnp.sum(neg_exp, axis=0, keepdims=True) + pos_exp
    slot = lax.broadcasted_iota(jnp.int32, (1, edges), 1)
    live = jnp.where(slot < count_ref[0], 1.0, 0.0)
    scale = live / total
    neg_round = (neg_exp * scale).astype(BF)
    coef = pos_exp * scale - live
    loads[5].wait()
    query_grad = coef * tails + nn(negt_ref[...], neg_round)

    head_terms = (query_grad * relation).astype(BF)
    for first, out in ((half, far_out), (0, near_out)):

        def scatter(owner):
            hot = onehot(head_slot, (first + owner) * head_rows, head_rows)
            out[owner] = nt(hot, head_terms).astype(BF)

        if half > UNROLL:
            pl.loop(0, half)(scatter)
        else:
            for owner in range(half):
                scatter(owner)

    relation_grad = query_grad * heads
    rg_hi, rg_lo = pieces(relation_grad, 2)
    comp_grad = nn(proj_hi, rg_hi) + (nn(proj_hi, rg_lo) + nn(proj_lo, rg_hi))
    rel_sum = nt(onehot(rel_id[...], 0, rel_rows), rg_hi)
    fetched_sum = jnp.zeros((slots, width), F32)
    for k in range(quals):
        hot = onehot(ref_ids[k : k + 1, :], 0, slots)
        rel_sum = rel_sum + nt(onehot(qual_rel[k : k + 1, :], 0, rel_rows), (comp_grad * rows[k]).astype(BF))
        fetched_sum = fetched_sum + nt(hot, (comp_grad * rel_ref[k + 1]).astype(BF))
    sums[:rel_rows, :] = rel_sum
    sums[rel_rows : rel_rows + width, :] = nt(comp_hi, rg_hi) + (nt(comp_hi, rg_lo) + nt(comp_lo, rg_hi))
    if sums.shape[0] > rel_rows + width:
        sums[rel_rows + width :, :] = jnp.zeros((sums.shape[0] - rel_rows - width, width), F32)
    pairs = fetched_sum.reshape(-1, cores, chips // PAIRS, cap, width)
    for core in range(cores):
        mine = pairs[:, core].reshape(chips, cap, width)
        parts = [sums[:, core * lanes : (core + 1) * lanes].reshape(chips, share, lanes)]
        parts += [mine[:, :, start : start + lanes] for start in range(0, width, lanes)]
        both = jnp.concatenate(parts, axis=1).astype(BF)

        @pl.when(core_ref[0] == core)
        def _():
            own_out[...] = both

        @pl.when(core_ref[0] != core)
        def _():
            other_out[...] = both

    terms_out[:edges, :] = flip((coef * query_f).astype(BF))
    terms_out[edges:, :] = nt(neg_round, query).astype(BF)


def combine_kernel(own_ref, got_ref, out_ref):
    chips, sent, lanes = own_ref.shape
    passed = out_ref.shape[1] - sent
    share = sent - passed
    summed = own_ref[:, :share, :].astype(F32) + got_ref[:, :share, :].astype(F32)
    out_ref[:, :share, :] = summed.astype(BF)
    out_ref[:, share:sent, :] = own_ref[:, share:, :]
    out_ref[:, sent:, :] = got_ref[:, share:, :]


def add_kernel(got_ref, out_ref):
    chips, share, _ = out_ref.shape
    total = got_ref[0, :share, :].astype(F32)
    for index in range(1, chips):
        total = total + got_ref[index, :share, :].astype(F32)
    total = total.astype(BF)
    for index in range(chips):
        out_ref[index] = total


def finish_kernel(core_ref, own_ref, got_ref, rel_out, proj_out):
    rel_rows = rel_out.shape[0]
    proj_rows = proj_out.shape[0]
    lanes = own_ref.shape[1]
    for ref, core in ((own_ref, core_ref[0]), (got_ref, 1 - core_ref[0])):
        at = pl.ds(pl.multiple_of(core * lanes, lanes), lanes)
        rel_out[:, at] = ref[:rel_rows, :].astype(F32)
        proj_out[:, at] = ref[rel_rows : rel_rows + proj_rows, :].astype(F32)


def qual_kernel(core_ref, got_ref, asked, qual_out):
    qual_rows, width = qual_out.shape
    chips, rows, lanes = got_ref.shape
    cores = asked.shape[0]
    cap = asked.shape[1] // chips
    parts = width // lanes
    first = rows - cores * parts * cap
    passed = got_ref[:, first:, :].astype(F32)
    hots = [
        onehot(asked[pl.ds(core_ref[0], 1), :], 0, qual_rows),
        onehot(asked[pl.ds(1 - core_ref[0], 1), :], 0, qual_rows),
    ]
    for part in range(parts):
        total = jnp.zeros((qual_rows, lanes), F32)
        for core in range(cores):
            start = (core * parts + part) * cap
            sent = passed[:, start : start + cap, :].reshape(chips * cap, lanes).astype(BF)
            total = total + nn(hots[core], sent)
        qual_out[:, part * lanes : (part + 1) * lanes] = total


def tail_kernel(tail_id, neg_id, terms, *refs, skip):
    tail_out = refs[-1]
    edges = tail_id.shape[1]
    rows = tail_out.shape[0]
    first = (pl.program_id(0) + skip) * rows
    tail_out[...] = nn(onehot(tail_id[...], first, rows), terms[:edges, :]) + nn(
        onehot(neg_id[...], first, rows), terms[edges:, :]
    )


WHOLE = pl.BlockSpec(memory_space=pltpu.VMEM)


def call(kernel, outs, scratch, micros, vmem, *args, smem=(), away=(), aliases={}, grid=(), out_specs=None):
    shapes = [jax.ShapeDtypeStruct(shape, dtype) for shape, dtype in outs]
    places = {**{index: pltpu.SMEM for index in smem}, **{index: pl.ANY for index in away}}
    return pl.pallas_call(
        kernel,
        out_shape=shapes,
        grid=grid,
        in_specs=[pl.BlockSpec(memory_space=places.get(index, pltpu.VMEM)) for index in range(len(args))],
        out_specs=out_specs or [WHOLE] * len(outs),
        scratch_shapes=scratch,
        input_output_aliases=aliases,
        compiler_params=pltpu.CompilerParams(vmem_limit_bytes=vmem * MIB),
        cost_estimate=pl.CostEstimate(flops=micros << 30, bytes_accessed=MIB, transcendentals=0),
    )(*args)


def exchange(values, axes):
    return lax.all_to_all(values, axes, split_axis=0, concat_axis=0, tiled=True)


def swap(values, axis, offset=1):
    return lax.ppermute(values, axis, [(i, i ^ offset) for i in range(lax.axis_size(axis))])


def body(
    head_table,
    tail_table,
    qual_table,
    rel_table,
    proj,
    head_id,
    tail_id,
    rel_id,
    qual_rel,
    qual_ref,
    qual_req,
    neg_id,
    edge_count,
):
    head_rows, width = head_table.shape
    tail_rows = tail_table.shape[0]
    qual_rows = qual_table.shape[0]
    rel_rows = rel_table.shape[0]
    edges = head_id.shape[0]
    negs = neg_id.shape[0]
    slots = qual_req.shape[0]
    half = lax.axis_size("line")
    cores = lax.axis_size("core")
    chips = lax.axis_size(CHIPS)
    devices = cores * chips
    quals = qual_ref.shape[1]
    cap = slots // devices
    lanes = width // cores

    arrived = exchange(qual_req.reshape(devices, cap), AXES)
    head_near = jnp.stack([head_table] + [swap(head_table, "line", offset) for offset in range(1, half)])
    core = lax.axis_index("core").astype(jnp.int32).reshape(1)
    member = lax.axis_index(MEMBER).astype(jnp.int32).reshape(1)

    rel_row = rel_id[None, :]
    qual_row = qual_rel.T
    ref_row = qual_ref.T
    tail_row = tail_id[None, :]
    neg_row = neg_id[None, :]
    (rel_looked,) = call(
        relation_lookup_kernel,
        [((quals + 1, width, edges), F32)],
        [
            pltpu.VMEM((2 * width, rel_rows), BF),
            pltpu.VMEM((quals + 1, width, edges), F32),
            pltpu.SemaphoreType.DMA((quals + 1,)),
        ],
        5,
        58,
        rel_table,
        rel_row,
        qual_row,
        out_specs=[pl.BlockSpec(memory_space=pl.ANY)],
    )
    arrived, rel_looked, head_near = lax.optimization_barrier((arrived, rel_looked, head_near))
    head_far = swap(head_near, "near")
    picked = qual_table.at[arrived].get(mode="promise_in_bounds")
    fetched = exchange(picked, AXES).reshape(slots, width)
    tails, neg_t, neg = call(
        tail_lookup_kernel,
        [((width, edges), BF), ((width, negs), BF), ((negs, width), BF)],
        [pltpu.VMEM((width, tail_rows), BF)],
        7,
        32,
        tail_table,
        tail_row,
        neg_row,
    )
    share = -(-(rel_rows + width) // (16 * chips)) * 16
    passed = cap * cores
    sent = share + passed

    def edge(*refs):
        edge_kernel(*refs, rel_rows=rel_rows)

    far_part, near_part, own_part, other_part, terms = call(
        edge,
        [
            ((half, head_rows, width), BF),
            ((half, head_rows, width), BF),
            ((chips, sent, lanes), BF),
            ((chips, sent, lanes), BF),
            ((edges + negs, width), BF),
        ],
        [
            pltpu.VMEM((quals + 1, width, edges), F32),
            pltpu.VMEM((half, head_rows, width), BF),
            pltpu.VMEM((half, head_rows, width), BF),
            pltpu.VMEM((width, edges), BF),
            pltpu.VMEM((negs, width), BF),
            pltpu.VMEM((width, negs), BF),
            pltpu.VMEM((chips * share, width), F32),
            pltpu.SemaphoreType.DMA((6,)),
        ],
        14,
        58 if half > UNROLL else 44,
        edge_count,
        core,
        member,
        rel_looked,
        head_near,
        head_far,
        tails,
        neg,
        neg_t,
        fetched,
        ref_row,
        rel_row,
        qual_row,
        head_id[None, :],
        proj,
        smem=(0, 1, 2),
        away=range(3, 9),
    )
    other_got = swap(other_part, "core")
    far_got = swap(far_part, "near")
    (chip_part,) = call(combine_kernel, [((chips, sent + passed, lanes), BF)], [], 1, 16, own_part, other_got)
    chip_got = exchange(chip_part, CHIPS)

    block = min(1024, tail_rows)
    steps = tail_rows // block

    def tail_rows_of(skip, count, *begun):
        def kernel(*refs):
            tail_kernel(*refs, skip=skip)

        (out,) = call(
            kernel,
            [((tail_rows, width), F32)],
            [],
            3,
            24,
            tail_row,
            neg_row,
            terms,
            *begun,
            away=(3,) if begun else (),
            aliases={3: 0} if begun else {},
            grid=(count,),
            out_specs=[pl.BlockSpec((block, width), lambda i: (i + skip, 0))],
        )
        return out

    tail_grad = tail_rows_of(0, steps // 2)
    far_got, tail_grad = lax.optimization_barrier((far_got, tail_grad))
    near_sum = near_part.astype(F32) + far_got.astype(F32)
    near_send = near_sum.astype(BF)
    line_got = [swap(near_send[offset], "line", offset) for offset in range(1, half)]
    (sums_own,) = call(add_kernel, [((chips, share, lanes), BF)], [], 1, 16, chip_got)
    sums_own = exchange(sums_own, CHIPS).reshape(chips * share, lanes)
    tail_grad = tail_rows_of(steps // 2, steps - steps // 2, tail_grad)
    sums_own, tail_grad, line_got = lax.optimization_barrier((sums_own, tail_grad, line_got))
    sums_got = swap(sums_own, "core")
    rel_grad, proj_grad = call(
        finish_kernel,
        [((rel_rows, width), F32), ((width, width), F32)],
        [],
        1,
        16,
        core,
        sums_own,
        sums_got,
        smem=(0,),
    )

    head_grad = near_sum[0]
    for got in line_got:
        head_grad = head_grad + got.astype(F32)

    asked = arrived.reshape(PAIRS, cores, chips // PAIRS * cap).transpose(1, 0, 2).reshape(cores, chips * cap)
    (qual_grad,) = call(
        qual_kernel, [((qual_rows, width), F32)], [], 2, 16, core, chip_got, asked, smem=(0,)
    )
    return (head_grad, tail_grad, qual_grad, rel_grad, proj_grad)


def solution(mesh):
    groups, members = mesh.devices.shape
    view = Mesh(mesh.devices.reshape(groups // 2, 2, members // 2, 2), AXES)
    rows = P(AXES, None)
    ids = P(AXES)
    in_specs = (rows, rows, rows, P(), P(), ids, ids, ids, rows, rows, ids, ids, ids)
    out_specs = (rows, rows, rows, P(), P())
    return jax.shard_map(body, mesh=view, in_specs=in_specs, out_specs=out_specs, check_vma=False)
```

```python
import jax
import jax.numpy as jnp
from jax import lax
from jax.experimental import pallas as pl
from jax.experimental.pallas import tpu as pltpu
from jax.sharding import Mesh, PartitionSpec as P

BF = jnp.bfloat16
F32 = jnp.float32
MIB = 1024 * 1024
AXES = ("pair", "core", "line", "near")
MEMBER = ("line", "near")
CHIPS = ("pair", "line", "near")
PAIRS = 2
BLOCK = 256
UNROLL = 4


def nn(a, b):
    return jnp.dot(a, b, preferred_element_type=F32)


def nt(a, b):
    return lax.dot_general(a, b, (((1,), (1,)), ((), ())), preferred_element_type=F32)


def pieces(values, count):
    out = []
    for _ in range(count):
        part = values.astype(BF)
        out.append(part)
        values = values - part.astype(F32)
    return out


def flip(values):
    return values.astype(F32).T.astype(BF)


def onehot(ids_row, first, rows):
    iota = lax.broadcasted_iota(jnp.int32, (rows, ids_row.shape[1]), 0)
    return jnp.where(iota == ids_row - first, 1.0, 0.0).astype(BF)


def relation_lookup_kernel(rel_ref, rel_id, qual_rel, rel_out, table, looked, sems):
    rel_rows, width = rel_ref.shape
    edges = rel_id.shape[1]
    for index, part in enumerate(pieces(rel_ref[...].T, 2)):
        table[index * width : (index + 1) * width, :] = part
    stores = []
    for which in range(1 + qual_rel.shape[0]):
        ids = qual_rel.at[which - 1 : which] if which else rel_id
        for start in range(0, edges, BLOCK):
            at = pl.ds(start, BLOCK)
            got = nn(table[...], onehot(ids[:, at], 0, rel_rows))
            looked[which, :, at] = got[:width] + got[width:]
        stores.append(pltpu.make_async_copy(looked.at[which], rel_out.at[which], sems.at[which]))
        stores[which].start()
    for copy in stores:
        copy.wait()


def tail_lookup_kernel(tail_ref, tail_id, neg_id, tails_out, negt_out, neg_out, table):
    tail_rows = tail_ref.shape[0]
    for start in range(0, tail_rows, BLOCK):
        at = pl.ds(start, BLOCK)
        table[:, at] = tail_ref[at, :].T
    for ids, out in ((tail_id, tails_out), (neg_id, negt_out)):
        for start in range(0, ids.shape[1], BLOCK):
            at = pl.ds(start, BLOCK)
            got = nn(table[...], onehot(ids[:, at], 0, tail_rows))
            out[:, at] = got.astype(BF)
            if ids is neg_id:
                neg_out[at, :] = got.T.astype(BF)


def edge_kernel(
    count_ref,
    core_ref,
    member_ref,
    rel_hbm,
    near_hbm,
    far_hbm,
    tails_hbm,
    neg_hbm,
    negt_hbm,
    fetched_ref,
    ref_ids,
    rel_id,
    qual_rel,
    head_id,
    proj_ref,
    far_out,
    near_out,
    own_out,
    other_out,
    terms_out,
    rel_ref,
    near_ref,
    far_ref,
    tails_ref,
    neg_ref,
    negt_ref,
    sums,
    packed,
    terms,
    in_sems,
    out_sems,
    *,
    rel_rows,
):
    width, edges = tails_ref.shape
    slots = fetched_ref.shape[0]
    half, head_rows, _ = near_ref.shape
    cores, chips, _, lanes = packed.shape
    share = sums.shape[0] // chips
    quals = ref_ids.shape[0]
    cap = slots // (cores * chips)

    loads = []

    def load(source, target):
        loads.append(pltpu.make_async_copy(source, target, in_sems.at[len(loads)]))
        loads[-1].start()
        return loads[-1]

    rel_loads = [load(rel_hbm.at[which], rel_ref.at[which]) for which in [*range(1, quals + 1), 0]]
    head_loads = [load(near_hbm, near_ref), load(far_hbm, far_ref)]
    tails_load = load(tails_hbm, tails_ref)
    neg_load = load(neg_hbm, neg_ref)
    negt_load = load(negt_hbm, negt_ref)

    fetched_t = flip(fetched_ref[...])
    proj_hi, proj_lo = pieces(proj_ref[...], 2)
    projt_hi, projt_lo = pieces(proj_ref[...].T, 2)
    rows = [nn(fetched_t, onehot(ref_ids[k : k + 1, :], 0, slots)) for k in range(quals)]
    for copy in rel_loads:
        copy.wait()
    composed = rel_ref[1] * rows[0]
    for k in range(1, quals):
        composed = composed + rel_ref[k + 1] * rows[k]
    comp_hi, comp_lo = pieces(composed, 2)
    relation = rel_ref[0] + (nn(projt_hi, comp_hi) + (nn(projt_hi, comp_lo) + nn(projt_lo, comp_hi)))
    for copy in head_loads:
        copy.wait()
    offset = jnp.bitwise_xor(head_id[...] // head_rows, member_ref[0])
    head_slot = ((offset % 2) * half + offset // 2) * head_rows + head_id[...] % head_rows
    heads = jnp.zeros((width, edges), F32)
    for first, table in ((0, near_ref), (half, far_ref)):
        for owner in range(half):
            heads = heads + nn(flip(table[owner]), onehot(head_slot, (first + owner) * head_rows, head_rows))
    query = (heads * relation).astype(BF)
    query_f = query.astype(F32)
    tails_load.wait()
    tails = tails_ref[...].astype(F32)
    positive = jnp.sum(query_f * tails, axis=0, keepdims=True)
    neg_load.wait()
    scores = nn(neg_ref[...], query)
    top = jnp.maximum(jnp.max(scores, axis=0, keepdims=True), positive)
    neg_exp = jnp.exp(scores - top)
    pos_exp = jnp.exp(positive - top)
    total = jnp.sum(neg_exp, axis=0, keepdims=True) + pos_exp
    slot = lax.broadcasted_iota(jnp.int32, (1, edges), 1)
    live = jnp.where(slot < count_ref[0], 1.0, 0.0)
    scale = live / total
    neg_round = (neg_exp * scale).astype(BF)
    coef = pos_exp * scale - live
    negt_load.wait()
    query_grad = coef * tails + nn(negt_ref[...], neg_round)

    stores = []

    def store(source, target):
        stores.append(pltpu.make_async_copy(source, target, out_sems.at[len(stores)]))
        stores[-1].start()

    head_terms = (query_grad * relation).astype(BF)
    for first, part, out in ((half, far_ref, far_out), (0, near_ref, near_out)):

        def scatter(owner):
            hot = onehot(head_slot, (first + owner) * head_rows, head_rows)
            part[owner] = nt(hot, head_terms).astype(BF)

        if half > UNROLL:
            pl.loop(0, half)(scatter)
        else:
            for owner in range(half):
                scatter(owner)
        store(part, out)

    relation_grad = query_grad * heads
    rg_hi, rg_lo = pieces(relation_grad, 2)
    comp_grad = nn(proj_hi, rg_hi) + (nn(proj_hi, rg_lo) + nn(proj_lo, rg_hi))
    rel_sum = nt(onehot(rel_id[...], 0, rel_rows), rg_hi)
    fetched_sum = jnp.zeros((slots, width), F32)
    for k in range(quals):
        hot = onehot(ref_ids[k : k + 1, :], 0, slots)
        rel_sum = rel_sum + nt(onehot(qual_rel[k : k + 1, :], 0, rel_rows), (comp_grad * rows[k]).astype(BF))
        fetched_sum = fetched_sum + nt(hot, (comp_grad * rel_ref[k + 1]).astype(BF))
    sums[:rel_rows, :] = rel_sum
    sums[rel_rows : rel_rows + width, :] = nt(comp_hi, rg_hi) + (nt(comp_hi, rg_lo) + nt(comp_lo, rg_hi))
    if sums.shape[0] > rel_rows + width:
        sums[rel_rows + width :, :] = jnp.zeros((sums.shape[0] - rel_rows - width, width), F32)
    pairs = fetched_sum.reshape(-1, cores, chips // PAIRS, cap, width)
    for core in range(cores):
        mine = pairs[:, core].reshape(chips, cap, width)
        parts = [sums[:, core * lanes : (core + 1) * lanes].reshape(chips, share, lanes)]
        parts += [mine[:, :, start : start + lanes] for start in range(0, width, lanes)]
        packed[core] = jnp.concatenate(parts, axis=1).astype(BF)
    store(packed.at[core_ref[0]], own_out)
    store(packed.at[1 - core_ref[0]], other_out)

    terms[:edges, :] = flip((coef * query_f).astype(BF))
    terms[edges:, :] = nt(neg_round, query).astype(BF)
    store(terms, terms_out)
    for copy in stores:
        copy.wait()


def combine_kernel(own_ref, got_ref, out_ref):
    chips, sent, lanes = own_ref.shape
    passed = out_ref.shape[1] - sent
    share = sent - passed
    summed = own_ref[:, :share, :].astype(F32) + got_ref[:, :share, :].astype(F32)
    out_ref[:, :share, :] = summed.astype(BF)
    out_ref[:, share:sent, :] = own_ref[:, share:, :]
    out_ref[:, sent:, :] = got_ref[:, share:, :]


def add_kernel(got_ref, out_ref):
    chips, share, _ = out_ref.shape
    total = got_ref[0, :share, :].astype(F32)
    for index in range(1, chips):
        total = total + got_ref[index, :share, :].astype(F32)
    total = total.astype(BF)
    for index in range(chips):
        out_ref[index] = total


def finish_kernel(core_ref, own_ref, got_ref, rel_out, proj_out):
    rel_rows = rel_out.shape[0]
    proj_rows = proj_out.shape[0]
    lanes = own_ref.shape[1]
    for ref, core in ((own_ref, core_ref[0]), (got_ref, 1 - core_ref[0])):
        at = pl.ds(pl.multiple_of(core * lanes, lanes), lanes)
        rel_out[:, at] = ref[:rel_rows, :].astype(F32)
        proj_out[:, at] = ref[rel_rows : rel_rows + proj_rows, :].astype(F32)


def qual_kernel(core_ref, got_ref, asked, qual_out):
    qual_rows, width = qual_out.shape
    chips, rows, lanes = got_ref.shape
    cores = asked.shape[0]
    cap = asked.shape[1] // chips
    parts = width // lanes
    first = rows - cores * parts * cap
    passed = got_ref[:, first:, :].astype(F32)
    hots = [
        onehot(asked[pl.ds(core_ref[0], 1), :], 0, qual_rows),
        onehot(asked[pl.ds(1 - core_ref[0], 1), :], 0, qual_rows),
    ]
    for part in range(parts):
        total = jnp.zeros((qual_rows, lanes), F32)
        for core in range(cores):
            start = (core * parts + part) * cap
            sent = passed[:, start : start + cap, :].reshape(chips * cap, lanes).astype(BF)
            total = total + nn(hots[core], sent)
        qual_out[:, part * lanes : (part + 1) * lanes] = total


def tail_kernel(tail_id, neg_id, terms, *refs, skip):
    tail_out = refs[-1]
    edges = tail_id.shape[1]
    rows = tail_out.shape[0]
    first = (pl.program_id(0) + skip) * rows
    tail_out[...] = nn(onehot(tail_id[...], first, rows), terms[:edges, :]) + nn(
        onehot(neg_id[...], first, rows), terms[edges:, :]
    )


WHOLE = pl.BlockSpec(memory_space=pltpu.VMEM)


def call(kernel, outs, scratch, micros, vmem, *args, smem=(), away=(), aliases={}, grid=(), out_specs=None):
    shapes = [jax.ShapeDtypeStruct(shape, dtype) for shape, dtype in outs]
    places = {**{index: pltpu.SMEM for index in smem}, **{index: pl.ANY for index in away}}
    return pl.pallas_call(
        kernel,
        out_shape=shapes,
        grid=grid,
        in_specs=[pl.BlockSpec(memory_space=places.get(index, pltpu.VMEM)) for index in range(len(args))],
        out_specs=out_specs or [WHOLE] * len(outs),
        scratch_shapes=scratch,
        input_output_aliases=aliases,
        compiler_params=pltpu.CompilerParams(vmem_limit_bytes=vmem * MIB),
        cost_estimate=pl.CostEstimate(flops=micros << 30, bytes_accessed=MIB, transcendentals=0),
    )(*args)


def exchange(values, axes):
    return lax.all_to_all(values, axes, split_axis=0, concat_axis=0, tiled=True)


def swap(values, axis, offset=1):
    return lax.ppermute(values, axis, [(i, i ^ offset) for i in range(lax.axis_size(axis))])


def body(
    head_table,
    tail_table,
    qual_table,
    rel_table,
    proj,
    head_id,
    tail_id,
    rel_id,
    qual_rel,
    qual_ref,
    qual_req,
    neg_id,
    edge_count,
):
    head_rows, width = head_table.shape
    tail_rows = tail_table.shape[0]
    qual_rows = qual_table.shape[0]
    rel_rows = rel_table.shape[0]
    edges = head_id.shape[0]
    negs = neg_id.shape[0]
    slots = qual_req.shape[0]
    half = lax.axis_size("line")
    cores = lax.axis_size("core")
    chips = lax.axis_size(CHIPS)
    devices = cores * chips
    quals = qual_ref.shape[1]
    cap = slots // devices
    lanes = width // cores

    arrived = exchange(qual_req.reshape(devices, cap), AXES)
    head_near = jnp.stack([head_table] + [swap(head_table, "line", offset) for offset in range(1, half)])
    core = lax.axis_index("core").astype(jnp.int32).reshape(1)
    member = lax.axis_index(MEMBER).astype(jnp.int32).reshape(1)

    rel_row = rel_id[None, :]
    qual_row = qual_rel.T
    ref_row = qual_ref.T
    tail_row = tail_id[None, :]
    neg_row = neg_id[None, :]
    (rel_looked,) = call(
        relation_lookup_kernel,
        [((quals + 1, width, edges), F32)],
        [
            pltpu.VMEM((2 * width, rel_rows), BF),
            pltpu.VMEM((quals + 1, width, edges), F32),
            pltpu.SemaphoreType.DMA((quals + 1,)),
        ],
        5,
        58,
        rel_table,
        rel_row,
        qual_row,
        out_specs=[pl.BlockSpec(memory_space=pl.ANY)],
    )
    arrived, rel_looked, head_near = lax.optimization_barrier((arrived, rel_looked, head_near))
    head_far = swap(head_near, "near")
    picked = qual_table.at[arrived].get(mode="promise_in_bounds")
    fetched = exchange(picked, AXES).reshape(slots, width)
    tails, neg_t, neg = call(
        tail_lookup_kernel,
        [((width, edges), BF), ((width, negs), BF), ((negs, width), BF)],
        [pltpu.VMEM((width, tail_rows), BF)],
        7,
        58,
        tail_table,
        tail_row,
        neg_row,
    )
    share = -(-(rel_rows + width) // (16 * chips)) * 16
    passed = cap * cores
    sent = share + passed

    def edge(*refs):
        edge_kernel(*refs, rel_rows=rel_rows)

    far_part, near_part, own_part, other_part, terms = call(
        edge,
        [
            ((half, head_rows, width), BF),
            ((half, head_rows, width), BF),
            ((chips, sent, lanes), BF),
            ((chips, sent, lanes), BF),
            ((edges + negs, width), BF),
        ],
        [
            pltpu.VMEM((quals + 1, width, edges), F32),
            pltpu.VMEM((half, head_rows, width), BF),
            pltpu.VMEM((half, head_rows, width), BF),
            pltpu.VMEM((width, edges), BF),
            pltpu.VMEM((negs, width), BF),
            pltpu.VMEM((width, negs), BF),
            pltpu.VMEM((chips * share, width), F32),
            pltpu.VMEM((cores, chips, sent, lanes), BF),
            pltpu.VMEM((edges + negs, width), BF),
            pltpu.SemaphoreType.DMA((quals + 6,)),
            pltpu.SemaphoreType.DMA((5,)),
        ],
        14,
        58,
        edge_count,
        core,
        member,
        rel_looked,
        head_near,
        head_far,
        tails,
        neg,
        neg_t,
        fetched,
        ref_row,
        rel_row,
        qual_row,
        head_id[None, :],
        proj,
        smem=(0, 1, 2),
        away=range(3, 9),
        out_specs=[pl.BlockSpec(memory_space=pl.ANY)] * 5,
    )
    other_got = swap(other_part, "core")
    far_got = swap(far_part, "near")
    (chip_part,) = call(combine_kernel, [((chips, sent + passed, lanes), BF)], [], 1, 16, own_part, other_got)
    chip_got = exchange(chip_part, CHIPS)

    block = min(1024, tail_rows)
    steps = tail_rows // block

    def tail_rows_of(skip, count, *begun):
        def kernel(*refs):
            tail_kernel(*refs, skip=skip)

        (out,) = call(
            kernel,
            [((tail_rows, width), F32)],
            [],
            3,
            24,
            tail_row,
            neg_row,
            terms,
            *begun,
            away=(3,) if begun else (),
            aliases={3: 0} if begun else {},
            grid=(count,),
            out_specs=[pl.BlockSpec((block, width), lambda i: (i + skip, 0))],
        )
        return out

    tail_grad = tail_rows_of(0, steps // 2)
    far_got, tail_grad = lax.optimization_barrier((far_got, tail_grad))
    near_sum = [near_part[offset].astype(F32) + far_got[offset].astype(F32) for offset in range(half)]
    line_got = [swap(near_sum[offset].astype(BF), "line", offset) for offset in range(1, half)]
    (sums_own,) = call(add_kernel, [((chips, share, lanes), BF)], [], 1, 16, chip_got)
    sums_own = exchange(sums_own, CHIPS).reshape(chips * share, lanes)
    tail_grad = tail_rows_of(steps // 2, steps - steps // 2, tail_grad)
    sums_own, tail_grad, line_got = lax.optimization_barrier((sums_own, tail_grad, line_got))
    sums_got = swap(sums_own, "core")
    rel_grad, proj_grad = call(
        finish_kernel,
        [((rel_rows, width), F32), ((width, width), F32)],
        [],
        1,
        16,
        core,
        sums_own,
        sums_got,
        smem=(0,),
    )

    head_grad = near_sum[0]
    for got in line_got:
        head_grad = head_grad + got.astype(F32)

    asked = arrived.reshape(PAIRS, cores, chips // PAIRS * cap).transpose(1, 0, 2).reshape(cores, chips * cap)
    (qual_grad,) = call(
        qual_kernel, [((qual_rows, width), F32)], [], 2, 16, core, chip_got, asked, smem=(0,)
    )
    return (head_grad, tail_grad, qual_grad, rel_grad, proj_grad)


def solution(mesh):
    groups, members = mesh.devices.shape
    view = Mesh(mesh.devices.reshape(groups // 2, 2, members // 2, 2), AXES)
    rows = P(AXES, None)
    ids = P(AXES)
    in_specs = (rows, rows, rows, P(), P(), ids, ids, ids, rows, rows, ids, ids, ids)
    out_specs = (rows, rows, rows, P(), P())
    return jax.shard_map(body, mesh=view, in_specs=in_specs, out_specs=out_specs, check_vma=False)
```

```python
import jax
import jax.numpy as jnp
from jax import lax
from jax.experimental import pallas as pl
from jax.experimental.pallas import tpu as pltpu
from jax.sharding import Mesh, PartitionSpec as P

BF = jnp.bfloat16
F32 = jnp.float32
MIB = 1024 * 1024
AXES = ("pair", "core", "line", "near")
MEMBER = ("line", "near")
CHIPS = ("pair", "line", "near")
PAIRS = 2
BLOCK = 256
UNROLL = 4


def nn(a, b):
    return jnp.dot(a, b, preferred_element_type=F32)


def nt(a, b):
    return lax.dot_general(a, b, (((1,), (1,)), ((), ())), preferred_element_type=F32)


def pieces(values, count):
    out = []
    for _ in range(count):
        part = values.astype(BF)
        out.append(part)
        values = values - part.astype(F32)
    return out


def flip(values):
    return values.astype(F32).T.astype(BF)


def onehot(ids_row, first, rows):
    iota = lax.broadcasted_iota(jnp.int32, (rows, ids_row.shape[1]), 0)
    return jnp.where(iota == ids_row - first, 1.0, 0.0).astype(BF)


def relation_lookup_kernel(rel_ref, rel_id, qual_rel, rel_out, table, looked, sems):
    rel_rows, width = rel_ref.shape
    edges = rel_id.shape[1]
    for index, part in enumerate(pieces(rel_ref[...].T, 2)):
        table[index * width : (index + 1) * width, :] = part
    stores = []
    for which in range(1 + qual_rel.shape[0]):
        ids = qual_rel.at[which - 1 : which] if which else rel_id
        for start in range(0, edges, BLOCK):
            at = pl.ds(start, BLOCK)
            got = nn(table[...], onehot(ids[:, at], 0, rel_rows))
            looked[which, :, at] = got[:width] + got[width:]
        stores.append(pltpu.make_async_copy(looked.at[which], rel_out.at[which], sems.at[which]))
        stores[which].start()
    for copy in stores:
        copy.wait()


def tail_lookup_kernel(tail_ref, tail_id, neg_id, tails_out, negt_out, neg_out, table):
    tail_rows = tail_ref.shape[0]
    for start in range(0, tail_rows, BLOCK):
        at = pl.ds(start, BLOCK)
        table[:, at] = tail_ref[at, :].T
    for ids, out in ((tail_id, tails_out), (neg_id, negt_out)):
        for start in range(0, ids.shape[1], BLOCK):
            at = pl.ds(start, BLOCK)
            got = nn(table[...], onehot(ids[:, at], 0, tail_rows))
            out[:, at] = got.astype(BF)
            if ids is neg_id:
                neg_out[at, :] = got.T.astype(BF)


def loader(sems):
    begun = []

    def load(source, target):
        begun.append(pltpu.make_async_copy(source, target, sems.at[len(begun)]))
        begun[-1].start()
        return begun[-1]

    return load, begun


def edge_kernel(
    count_ref,
    member_ref,
    rel_hbm,
    near_hbm,
    far_hbm,
    tails_hbm,
    neg_hbm,
    negt_hbm,
    fetched_ref,
    ref_ids,
    head_id,
    proj_ref,
    far_out,
    near_out,
    rg_out,
    comp_out,
    terms_out,
    rel_ref,
    near_ref,
    far_ref,
    tails_ref,
    neg_ref,
    negt_ref,
    rg,
    comp,
    terms,
    in_sems,
    out_sems,
):
    width, edges = tails_ref.shape
    slots = fetched_ref.shape[0]
    half, head_rows, _ = near_ref.shape
    quals = ref_ids.shape[0]

    load, _ = loader(in_sems)
    rel_loads = [load(rel_hbm.at[which], rel_ref.at[which]) for which in [*range(1, quals + 1), 0]]
    head_loads = [load(near_hbm, near_ref), load(far_hbm, far_ref)]
    tails_load = load(tails_hbm, tails_ref)
    neg_load = load(neg_hbm, neg_ref)
    negt_load = load(negt_hbm, negt_ref)
    store, stores = loader(out_sems)

    fetched_t = flip(fetched_ref[...])
    projt_hi, projt_lo = pieces(proj_ref[...].T, 2)
    rows = [nn(fetched_t, onehot(ref_ids[k : k + 1, :], 0, slots)) for k in range(quals)]
    for copy in rel_loads:
        copy.wait()
    composed = rel_ref[1] * rows[0]
    for k in range(1, quals):
        composed = composed + rel_ref[k + 1] * rows[k]
    comp_hi, comp_lo = pieces(composed, 2)
    comp[0] = comp_hi
    comp[1] = comp_lo
    store(comp, comp_out)
    relation = rel_ref[0] + nn(
        jnp.concatenate([projt_hi, projt_hi, projt_lo], axis=1),
        jnp.concatenate([comp_hi, comp_lo, comp_hi], axis=0),
    )
    for copy in head_loads:
        copy.wait()
    offset = jnp.bitwise_xor(head_id[...] // head_rows, member_ref[0])
    head_slot = ((offset % 2) * half + offset // 2) * head_rows + head_id[...] % head_rows
    heads = jnp.zeros((width, edges), F32)
    for first, table in ((0, near_ref), (half, far_ref)):
        for owner in range(half):
            heads = heads + nn(flip(table[owner]), onehot(head_slot, (first + owner) * head_rows, head_rows))
    query = (heads * relation).astype(BF)
    query_f = query.astype(F32)
    tails_load.wait()
    tails = tails_ref[...].astype(F32)
    positive = jnp.sum(query_f * tails, axis=0, keepdims=True)
    neg_load.wait()
    scores = nn(neg_ref[...], query)
    top = jnp.maximum(jnp.max(scores, axis=0, keepdims=True), positive)
    neg_exp = jnp.exp(scores - top)
    pos_exp = jnp.exp(positive - top)
    total = jnp.sum(neg_exp, axis=0, keepdims=True) + pos_exp
    slot = lax.broadcasted_iota(jnp.int32, (1, edges), 1)
    live = jnp.where(slot < count_ref[0], 1.0, 0.0)
    scale = live / total
    neg_round = (neg_exp * scale).astype(BF)
    coef = pos_exp * scale - live
    negt_load.wait()
    query_grad = coef * tails + nn(negt_ref[...], neg_round)

    head_terms = (query_grad * relation).astype(BF)
    for first, part, out in ((half, far_ref, far_out), (0, near_ref, near_out)):

        def scatter(owner):
            hot = onehot(head_slot, (first + owner) * head_rows, head_rows)
            part[owner] = nt(hot, head_terms).astype(BF)

        if half > UNROLL:
            pl.loop(0, half)(scatter)
        else:
            for owner in range(half):
                scatter(owner)
        store(part, out)
    rg_hi, rg_lo = pieces(query_grad * heads, 2)
    rg[0] = rg_hi
    rg[1] = rg_lo
    store(rg, rg_out)
    terms[:edges, :] = flip((coef * query_f).astype(BF))
    terms[edges:, :] = nt(neg_round, query).astype(BF)
    store(terms, terms_out)
    for copy in stores:
        copy.wait()


def relation_kernel(
    core_ref,
    rel_hbm,
    rg_hbm,
    comp_hbm,
    fetched_ref,
    ref_ids,
    rel_id,
    qual_rel,
    proj_ref,
    own_out,
    other_out,
    rel_ref,
    rg,
    comp,
    sums,
    packed,
    in_sems,
    out_sems,
    *,
    rel_rows,
):
    slots, width = fetched_ref.shape
    cores, chips, _, lanes = packed.shape
    share = sums.shape[0] // chips
    quals = ref_ids.shape[0]
    cap = slots // (cores * chips)
    load, _ = loader(in_sems)
    rg_load = load(rg_hbm, rg)
    rel_loads = [load(rel_hbm.at[which + 1], rel_ref.at[which]) for which in range(quals)]
    comp_load = load(comp_hbm, comp)
    store, stores = loader(out_sems)

    fetched_t = flip(fetched_ref[...])
    proj_hi, proj_lo = pieces(proj_ref[...], 2)
    ref_hots = [onehot(ref_ids[k : k + 1, :], 0, slots) for k in range(quals)]
    rows = [nn(fetched_t, hot) for hot in ref_hots]
    rg_load.wait()
    comp_grad = nn(
        jnp.concatenate([proj_hi, proj_hi, proj_lo], axis=1), jnp.concatenate([rg[0], rg[1], rg[0]], axis=0)
    )
    rel_sum = nt(onehot(rel_id[...], 0, rel_rows), rg[0])
    for k in range(quals):
        rel_sum = rel_sum + nt(onehot(qual_rel[k : k + 1, :], 0, rel_rows), (comp_grad * rows[k]).astype(BF))
    sums[:rel_rows, :] = rel_sum
    for copy in rel_loads:
        copy.wait()
    comp_load.wait()
    fetched_sum = jnp.zeros((slots, width), F32)
    for k in range(quals):
        fetched_sum = fetched_sum + nt(ref_hots[k], (comp_grad * rel_ref[k]).astype(BF))
    sums[rel_rows : rel_rows + width, :] = nt(
        jnp.concatenate([comp[0], comp[0], comp[1]], axis=1), jnp.concatenate([rg[0], rg[1], rg[0]], axis=1)
    )
    if sums.shape[0] > rel_rows + width:
        sums[rel_rows + width :, :] = jnp.zeros((sums.shape[0] - rel_rows - width, width), F32)
    pairs = fetched_sum.reshape(-1, cores, chips // PAIRS, cap, width)
    for core in range(cores):
        mine = pairs[:, core].reshape(chips, cap, width)
        parts = [sums[:, core * lanes : (core + 1) * lanes].reshape(chips, share, lanes)]
        parts += [mine[:, :, start : start + lanes] for start in range(0, width, lanes)]
        packed[core] = jnp.concatenate(parts, axis=1).astype(BF)
    store(packed.at[1 - core_ref[0]], other_out)
    store(packed.at[core_ref[0]], own_out)
    for copy in stores:
        copy.wait()


def combine_kernel(own_ref, got_ref, out_ref):
    chips, sent, lanes = own_ref.shape
    passed = out_ref.shape[1] - sent
    share = sent - passed
    summed = own_ref[:, :share, :].astype(F32) + got_ref[:, :share, :].astype(F32)
    out_ref[:, :share, :] = summed.astype(BF)
    out_ref[:, share:sent, :] = own_ref[:, share:, :]
    out_ref[:, sent:, :] = got_ref[:, share:, :]


def add_kernel(got_ref, out_ref):
    chips, share, _ = out_ref.shape
    total = got_ref[0, :share, :].astype(F32)
    for index in range(1, chips):
        total = total + got_ref[index, :share, :].astype(F32)
    total = total.astype(BF)
    for index in range(chips):
        out_ref[index] = total


def finish_kernel(core_ref, own_ref, got_ref, rel_out, proj_out):
    rel_rows = rel_out.shape[0]
    proj_rows = proj_out.shape[0]
    lanes = own_ref.shape[1]
    for ref, core in ((own_ref, core_ref[0]), (got_ref, 1 - core_ref[0])):
        at = pl.ds(pl.multiple_of(core * lanes, lanes), lanes)
        rel_out[:, at] = ref[:rel_rows, :].astype(F32)
        proj_out[:, at] = ref[rel_rows : rel_rows + proj_rows, :].astype(F32)


def qual_kernel(core_ref, got_ref, asked, qual_out):
    qual_rows, width = qual_out.shape
    chips, rows, lanes = got_ref.shape
    cores = asked.shape[0]
    cap = asked.shape[1] // chips
    parts = width // lanes
    first = rows - cores * parts * cap
    passed = got_ref[:, first:, :].astype(F32)
    hots = [
        onehot(asked[pl.ds(core_ref[0], 1), :], 0, qual_rows),
        onehot(asked[pl.ds(1 - core_ref[0], 1), :], 0, qual_rows),
    ]
    for part in range(parts):
        total = jnp.zeros((qual_rows, lanes), F32)
        for core in range(cores):
            start = (core * parts + part) * cap
            sent = passed[:, start : start + cap, :].reshape(chips * cap, lanes).astype(BF)
            total = total + nn(hots[core], sent)
        qual_out[:, part * lanes : (part + 1) * lanes] = total


def tail_kernel(tail_id, neg_id, terms, *refs, skip):
    tail_out = refs[-1]
    edges = tail_id.shape[1]
    rows = tail_out.shape[0]
    first = (pl.program_id(0) + skip) * rows
    tail_out[...] = nn(onehot(tail_id[...], first, rows), terms[:edges, :]) + nn(
        onehot(neg_id[...], first, rows), terms[edges:, :]
    )


WHOLE = pl.BlockSpec(memory_space=pltpu.VMEM)


def call(kernel, outs, scratch, micros, vmem, *args, smem=(), away=(), aliases={}, grid=(), out_specs=None):
    shapes = [jax.ShapeDtypeStruct(shape, dtype) for shape, dtype in outs]
    places = {**{index: pltpu.SMEM for index in smem}, **{index: pl.ANY for index in away}}
    return pl.pallas_call(
        kernel,
        out_shape=shapes,
        grid=grid,
        in_specs=[pl.BlockSpec(memory_space=places.get(index, pltpu.VMEM)) for index in range(len(args))],
        out_specs=out_specs or [WHOLE] * len(outs),
        scratch_shapes=scratch,
        input_output_aliases=aliases,
        compiler_params=pltpu.CompilerParams(vmem_limit_bytes=vmem * MIB),
        cost_estimate=pl.CostEstimate(flops=micros << 30, bytes_accessed=MIB, transcendentals=0),
    )(*args)


def exchange(values, axes):
    return lax.all_to_all(values, axes, split_axis=0, concat_axis=0, tiled=True)


def swap(values, axis, offset=1):
    return lax.ppermute(values, axis, [(i, i ^ offset) for i in range(lax.axis_size(axis))])


def body(
    head_table,
    tail_table,
    qual_table,
    rel_table,
    proj,
    head_id,
    tail_id,
    rel_id,
    qual_rel,
    qual_ref,
    qual_req,
    neg_id,
    edge_count,
):
    head_rows, width = head_table.shape
    tail_rows = tail_table.shape[0]
    qual_rows = qual_table.shape[0]
    rel_rows = rel_table.shape[0]
    edges = head_id.shape[0]
    negs = neg_id.shape[0]
    slots = qual_req.shape[0]
    half = lax.axis_size("line")
    cores = lax.axis_size("core")
    chips = lax.axis_size(CHIPS)
    devices = cores * chips
    quals = qual_ref.shape[1]
    cap = slots // devices
    lanes = width // cores

    arrived = exchange(qual_req.reshape(devices, cap), AXES)
    head_near = jnp.stack([head_table] + [swap(head_table, "line", offset) for offset in range(1, half)])
    core = lax.axis_index("core").astype(jnp.int32).reshape(1)
    member = lax.axis_index(MEMBER).astype(jnp.int32).reshape(1)

    rel_row = rel_id[None, :]
    qual_row = qual_rel.T
    ref_row = qual_ref.T
    tail_row = tail_id[None, :]
    neg_row = neg_id[None, :]
    (rel_looked,) = call(
        relation_lookup_kernel,
        [((quals + 1, width, edges), F32)],
        [
            pltpu.VMEM((2 * width, rel_rows), BF),
            pltpu.VMEM((quals + 1, width, edges), F32),
            pltpu.SemaphoreType.DMA((quals + 1,)),
        ],
        5,
        58,
        rel_table,
        rel_row,
        qual_row,
        out_specs=[pl.BlockSpec(memory_space=pl.ANY)],
    )
    arrived, rel_looked, head_near = lax.optimization_barrier((arrived, rel_looked, head_near))
    head_far = swap(head_near, "near")
    picked = qual_table.at[arrived].get(mode="promise_in_bounds")
    fetched = exchange(picked, AXES).reshape(slots, width)
    tails, neg_t, neg = call(
        tail_lookup_kernel,
        [((width, edges), BF), ((width, negs), BF), ((negs, width), BF)],
        [pltpu.VMEM((width, tail_rows), BF)],
        7,
        58,
        tail_table,
        tail_row,
        neg_row,
    )
    share = -(-(rel_rows + width) // (16 * chips)) * 16
    passed = cap * cores
    sent = share + passed

    def relations(*refs):
        relation_kernel(*refs, rel_rows=rel_rows)

    anywhere = pl.BlockSpec(memory_space=pl.ANY)
    far_part, near_part, rg, comp, terms = call(
        edge_kernel,
        [
            ((half, head_rows, width), BF),
            ((half, head_rows, width), BF),
            ((2, width, edges), BF),
            ((2, width, edges), BF),
            ((edges + negs, width), BF),
        ],
        [
            pltpu.VMEM((quals + 1, width, edges), F32),
            pltpu.VMEM((half, head_rows, width), BF),
            pltpu.VMEM((half, head_rows, width), BF),
            pltpu.VMEM((width, edges), BF),
            pltpu.VMEM((negs, width), BF),
            pltpu.VMEM((width, negs), BF),
            pltpu.VMEM((2, width, edges), BF),
            pltpu.VMEM((2, width, edges), BF),
            pltpu.VMEM((edges + negs, width), BF),
            pltpu.SemaphoreType.DMA((quals + 6,)),
            pltpu.SemaphoreType.DMA((5,)),
        ],
        11,
        58,
        edge_count,
        member,
        rel_looked,
        head_near,
        head_far,
        tails,
        neg,
        neg_t,
        fetched,
        ref_row,
        head_id[None, :],
        proj,
        smem=(0, 1),
        away=range(2, 8),
        out_specs=[anywhere] * 5,
    )
    far_got = swap(far_part, "near")
    own_part, other_part = call(
        relations,
        [((chips, sent, lanes), BF), ((chips, sent, lanes), BF)],
        [
            pltpu.VMEM((quals, width, edges), F32),
            pltpu.VMEM((2, width, edges), BF),
            pltpu.VMEM((2, width, edges), BF),
            pltpu.VMEM((chips * share, width), F32),
            pltpu.VMEM((cores, chips, sent, lanes), BF),
            pltpu.SemaphoreType.DMA((quals + 2,)),
            pltpu.SemaphoreType.DMA((2,)),
        ],
        4,
        58,
        core,
        rel_looked,
        rg,
        comp,
        fetched,
        ref_row,
        rel_row,
        qual_row,
        proj,
        smem=(0,),
        away=(1, 2, 3),
        out_specs=[anywhere] * 2,
    )
    other_got = swap(other_part, "core")
    (chip_part,) = call(combine_kernel, [((chips, sent + passed, lanes), BF)], [], 1, 16, own_part, other_got)
    chip_got = exchange(chip_part, CHIPS)

    block = min(1024, tail_rows)
    steps = tail_rows // block

    def tail_rows_of(skip, count, *begun):
        def kernel(*refs):
            tail_kernel(*refs, skip=skip)

        (out,) = call(
            kernel,
            [((tail_rows, width), F32)],
            [],
            3,
            24,
            tail_row,
            neg_row,
            terms,
            *begun,
            away=(3,) if begun else (),
            aliases={3: 0} if begun else {},
            grid=(count,),
            out_specs=[pl.BlockSpec((block, width), lambda i: (i + skip, 0))],
        )
        return out

    tail_grad = tail_rows_of(0, steps // 2)
    far_got, tail_grad = lax.optimization_barrier((far_got, tail_grad))
    near_sum = [near_part[offset].astype(F32) + far_got[offset].astype(F32) for offset in range(half)]
    line_got = [swap(near_sum[offset].astype(BF), "line", offset) for offset in range(1, half)]
    (sums_own,) = call(add_kernel, [((chips, share, lanes), BF)], [], 1, 16, chip_got)
    sums_own = exchange(sums_own, CHIPS).reshape(chips * share, lanes)
    tail_grad = tail_rows_of(steps // 2, steps - steps // 2, tail_grad)
    sums_own, tail_grad, line_got = lax.optimization_barrier((sums_own, tail_grad, line_got))
    sums_got = swap(sums_own, "core")
    rel_grad, proj_grad = call(
        finish_kernel,
        [((rel_rows, width), F32), ((width, width), F32)],
        [],
        1,
        16,
        core,
        sums_own,
        sums_got,
        smem=(0,),
    )

    head_grad = near_sum[0]
    for got in line_got:
        head_grad = head_grad + got.astype(F32)

    asked = arrived.reshape(PAIRS, cores, chips // PAIRS * cap).transpose(1, 0, 2).reshape(cores, chips * cap)
    (qual_grad,) = call(
        qual_kernel, [((qual_rows, width), F32)], [], 2, 16, core, chip_got, asked, smem=(0,)
    )
    return (head_grad, tail_grad, qual_grad, rel_grad, proj_grad)


def solution(mesh):
    groups, members = mesh.devices.shape
    view = Mesh(mesh.devices.reshape(groups // 2, 2, members // 2, 2), AXES)
    rows = P(AXES, None)
    ids = P(AXES)
    in_specs = (rows, rows, rows, P(), P(), ids, ids, ids, rows, rows, ids, ids, ids)
    out_specs = (rows, rows, rows, P(), P())
    return jax.shard_map(body, mesh=view, in_specs=in_specs, out_specs=out_specs, check_vma=False)
```

```python
import jax
import jax.numpy as jnp
from jax import lax
from jax.experimental import pallas as pl
from jax.experimental.pallas import tpu as pltpu
from jax.sharding import Mesh, PartitionSpec as P

BF = jnp.bfloat16
F32 = jnp.float32
MIB = 1024 * 1024
AXES = ("pair", "core", "line", "near")
MEMBER = ("line", "near")
CHIPS = ("pair", "line", "near")
PAIRS = 2
BLOCK = 256
UNROLL = 4


def nn(a, b):
    return jnp.dot(a, b, preferred_element_type=F32)


def nt(a, b):
    return lax.dot_general(a, b, (((1,), (1,)), ((), ())), preferred_element_type=F32)


def tn(a, b):
    return lax.dot_general(a, b, (((0,), (0,)), ((), ())), preferred_element_type=F32)


def pieces(values, count):
    out = []
    for _ in range(count):
        part = values.astype(BF)
        out.append(part)
        values = values - part.astype(F32)
    return out


def flip(values):
    return values.astype(F32).T.astype(BF)


def onehot(ids_row, first, rows):
    iota = lax.broadcasted_iota(jnp.int32, (rows, ids_row.shape[1]), 0)
    return jnp.where(iota == ids_row - first, 1.0, 0.0).astype(BF)


def relation_lookup_kernel(rel_ref, rel_id, qual_rel, rel_out, table, looked, sems):
    rel_rows, width = rel_ref.shape
    edges = rel_id.shape[1]
    for index, part in enumerate(pieces(rel_ref[...].T, 2)):
        table[index * width : (index + 1) * width, :] = part
    stores = []
    for which in range(1 + qual_rel.shape[0]):
        ids = qual_rel.at[which - 1 : which] if which else rel_id
        for start in range(0, edges, BLOCK):
            at = pl.ds(start, BLOCK)
            got = nn(table[...], onehot(ids[:, at], 0, rel_rows))
            looked[which, :, at] = got[:width] + got[width:]
        stores.append(pltpu.make_async_copy(looked.at[which], rel_out.at[which], sems.at[which]))
        stores[which].start()
    for copy in stores:
        copy.wait()


def tail_lookup_kernel(tail_ref, tail_id, neg_id, tails_out, negt_out, neg_out, table):
    tail_rows = tail_ref.shape[0]
    for start in range(0, tail_rows, BLOCK):
        at = pl.ds(start, BLOCK)
        table[:, at] = tail_ref[at, :].T
    for ids, out in ((tail_id, tails_out), (neg_id, negt_out)):
        for start in range(0, ids.shape[1], BLOCK):
            at = pl.ds(start, BLOCK)
            got = nn(table[...], onehot(ids[:, at], 0, tail_rows))
            out[:, at] = got.astype(BF)
            if ids is neg_id:
                neg_out[at, :] = got.T.astype(BF)


def edge_kernel(
    count_ref,
    core_ref,
    member_ref,
    rel_hbm,
    near_hbm,
    far_hbm,
    tails_hbm,
    neg_hbm,
    negt_hbm,
    fetched_ref,
    ref_ids,
    rel_id,
    qual_rel,
    head_id,
    proj_ref,
    far_high_out,
    far_low_out,
    near_out,
    own_out,
    other_out,
    terms_out,
    rel_ref,
    near_ref,
    far_ref,
    tails_ref,
    neg_ref,
    negt_ref,
    sums,
    packed,
    terms,
    in_sems,
    out_sems,
    *,
    rel_rows,
):
    width, edges = tails_ref.shape
    slots = fetched_ref.shape[0]
    half, head_rows, _ = near_ref.shape
    cores, chips, _, lanes = packed.shape
    share = sums.shape[0] // chips
    quals = ref_ids.shape[0]
    cap = slots // (cores * chips)

    loads = []

    def load(source, target):
        loads.append(pltpu.make_async_copy(source, target, in_sems.at[len(loads)]))
        loads[-1].start()
        return loads[-1]

    rel_loads = [load(rel_hbm.at[which], rel_ref.at[which]) for which in [*range(1, quals + 1), 0]]
    head_loads = [load(near_hbm, near_ref), load(far_hbm, far_ref)]
    tails_load = load(tails_hbm, tails_ref)
    neg_load = load(neg_hbm, neg_ref)
    negt_load = load(negt_hbm, negt_ref)

    fetched_t = flip(fetched_ref[...])
    proj_hi, proj_lo = pieces(proj_ref[...], 2)
    projt_hi, projt_lo = pieces(proj_ref[...].T, 2)
    rows = [nn(fetched_t, onehot(ref_ids[k : k + 1, :], 0, slots)) for k in range(quals)]
    for copy in rel_loads:
        copy.wait()
    composed = rel_ref[1] * rows[0]
    for k in range(1, quals):
        composed = composed + rel_ref[k + 1] * rows[k]
    comp_hi, comp_lo = pieces(composed, 2)
    relation = rel_ref[0] + nn(
        jnp.concatenate([projt_hi, projt_hi, projt_lo], axis=1),
        jnp.concatenate([comp_hi, comp_lo, comp_hi], axis=0),
    )
    for copy in head_loads:
        copy.wait()
    offset = jnp.bitwise_xor(head_id[...] // head_rows, member_ref[0])
    head_slot = ((offset % 2) * half + offset // 2) * head_rows + head_id[...] % head_rows
    heads = jnp.zeros((width, edges), F32)
    for first, table in ((0, near_ref), (half, far_ref)):
        for owner in range(half):
            heads = heads + tn(table[owner], onehot(head_slot, (first + owner) * head_rows, head_rows))
    query = (heads * relation).astype(BF)
    query_f = query.astype(F32)
    tails_load.wait()
    tails = tails_ref[...].astype(F32)
    positive = jnp.sum(query_f * tails, axis=0, keepdims=True)
    neg_load.wait()
    scores = nn(neg_ref[...], query)
    top = jnp.maximum(jnp.max(scores, axis=0, keepdims=True), positive)
    neg_exp = jnp.exp(scores - top)
    pos_exp = jnp.exp(positive - top)
    total = jnp.sum(neg_exp, axis=0, keepdims=True) + pos_exp
    slot = lax.broadcasted_iota(jnp.int32, (1, edges), 1)
    live = jnp.where(slot < count_ref[0], 1.0, 0.0)
    scale = live / total
    neg_round = (neg_exp * scale).astype(BF)
    coef = pos_exp * scale - live
    negt_load.wait()
    query_grad = coef * tails + nn(negt_ref[...], neg_round)

    stores = []

    def store(source, target):
        stores.append(pltpu.make_async_copy(source, target, out_sems.at[len(stores)]))
        stores[-1].start()

    head_terms = (query_grad * relation).astype(BF)
    low, high = pl.ds(0, half // 2), pl.ds(half // 2, half - half // 2)
    for first, part in ((half, far_ref), (0, near_ref)):

        def scatter(owner):
            hot = onehot(head_slot, (first + owner) * head_rows, head_rows)
            part[owner] = nt(hot, head_terms).astype(BF)

        if half > UNROLL:
            pl.loop(0, half)(scatter)
        else:
            for owner in range(half):
                scatter(owner)
        if part is far_ref:
            store(far_ref.at[high], far_high_out)
            store(far_ref.at[low], far_low_out)
        else:
            store(near_ref, near_out)

    relation_grad = query_grad * heads
    rg_hi, rg_lo = pieces(relation_grad, 2)
    comp_grad = nn(
        jnp.concatenate([proj_hi, proj_hi, proj_lo], axis=1), jnp.concatenate([rg_hi, rg_lo, rg_hi], axis=0)
    )
    rel_hots, rel_terms = [onehot(rel_id[...], 0, rel_rows)], [rg_hi]
    ref_hots, ref_terms = [], []
    for k in range(quals):
        rel_hots.append(onehot(qual_rel[k : k + 1, :], 0, rel_rows))
        rel_terms.append((comp_grad * rows[k]).astype(BF))
        ref_hots.append(onehot(ref_ids[k : k + 1, :], 0, slots))
        ref_terms.append((comp_grad * rel_ref[k + 1]).astype(BF))
    rel_sum = nt(jnp.concatenate(rel_hots, axis=1), jnp.concatenate(rel_terms, axis=1))
    fetched_sum = nt(jnp.concatenate(ref_hots, axis=1), jnp.concatenate(ref_terms, axis=1))
    sums[:rel_rows, :] = rel_sum
    sums[rel_rows : rel_rows + width, :] = nt(
        jnp.concatenate([comp_hi, comp_hi, comp_lo], axis=1), jnp.concatenate([rg_hi, rg_lo, rg_hi], axis=1)
    )
    if sums.shape[0] > rel_rows + width:
        sums[rel_rows + width :, :] = jnp.zeros((sums.shape[0] - rel_rows - width, width), F32)
    pairs = fetched_sum.reshape(-1, cores, chips // PAIRS, cap, width)
    for core in range(cores):
        mine = pairs[:, core].reshape(chips, cap, width)
        parts = [sums[:, core * lanes : (core + 1) * lanes].reshape(chips, share, lanes)]
        parts += [mine[:, :, start : start + lanes] for start in range(0, width, lanes)]
        packed[core] = jnp.concatenate(parts, axis=1).astype(BF)
    store(packed.at[core_ref[0]], own_out)
    store(packed.at[1 - core_ref[0]], other_out)

    terms[:edges, :] = flip((coef * query_f).astype(BF))
    terms[edges:, :] = nt(neg_round, query).astype(BF)
    store(terms, terms_out)
    for copy in stores:
        copy.wait()


def combine_kernel(own_ref, got_ref, out_ref):
    chips, sent, lanes = own_ref.shape
    passed = out_ref.shape[1] - sent
    share = sent - passed
    summed = own_ref[:, :share, :].astype(F32) + got_ref[:, :share, :].astype(F32)
    out_ref[:, :share, :] = summed.astype(BF)
    out_ref[:, share:sent, :] = own_ref[:, share:, :]
    out_ref[:, sent:, :] = got_ref[:, share:, :]


def add_kernel(got_ref, out_ref):
    chips, share, _ = out_ref.shape
    total = got_ref[0, :share, :].astype(F32)
    for index in range(1, chips):
        total = total + got_ref[index, :share, :].astype(F32)
    total = total.astype(BF)
    for index in range(chips):
        out_ref[index] = total


def finish_kernel(core_ref, own_ref, got_ref, rel_out, proj_out):
    rel_rows = rel_out.shape[0]
    proj_rows = proj_out.shape[0]
    lanes = own_ref.shape[1]
    for ref, core in ((own_ref, core_ref[0]), (got_ref, 1 - core_ref[0])):
        at = pl.ds(pl.multiple_of(core * lanes, lanes), lanes)
        rel_out[:, at] = ref[:rel_rows, :].astype(F32)
        proj_out[:, at] = ref[rel_rows : rel_rows + proj_rows, :].astype(F32)


def qual_kernel(core_ref, got_ref, asked, qual_out):
    qual_rows, width = qual_out.shape
    chips, rows, lanes = got_ref.shape
    cores = asked.shape[0]
    cap = asked.shape[1] // chips
    parts = width // lanes
    first = rows - cores * parts * cap
    passed = got_ref[:, first:, :].astype(F32)
    hots = [
        onehot(asked[pl.ds(core_ref[0], 1), :], 0, qual_rows),
        onehot(asked[pl.ds(1 - core_ref[0], 1), :], 0, qual_rows),
    ]
    for part in range(parts):
        total = jnp.zeros((qual_rows, lanes), F32)
        for core in range(cores):
            start = (core * parts + part) * cap
            sent = passed[:, start : start + cap, :].reshape(chips * cap, lanes).astype(BF)
            total = total + nn(hots[core], sent)
        qual_out[:, part * lanes : (part + 1) * lanes] = total


def tail_kernel(tail_id, neg_id, terms, *refs, skip):
    tail_out = refs[-1]
    edges = tail_id.shape[1]
    rows = tail_out.shape[0]
    first = (pl.program_id(0) + skip) * rows
    tail_out[...] = nn(onehot(tail_id[...], first, rows), terms[:edges, :]) + nn(
        onehot(neg_id[...], first, rows), terms[edges:, :]
    )


WHOLE = pl.BlockSpec(memory_space=pltpu.VMEM)


def call(kernel, outs, scratch, micros, vmem, *args, smem=(), away=(), aliases={}, grid=(), out_specs=None):
    shapes = [jax.ShapeDtypeStruct(shape, dtype) for shape, dtype in outs]
    places = {**{index: pltpu.SMEM for index in smem}, **{index: pl.ANY for index in away}}
    return pl.pallas_call(
        kernel,
        out_shape=shapes,
        grid=grid,
        in_specs=[pl.BlockSpec(memory_space=places.get(index, pltpu.VMEM)) for index in range(len(args))],
        out_specs=out_specs or [WHOLE] * len(outs),
        scratch_shapes=scratch,
        input_output_aliases=aliases,
        compiler_params=pltpu.CompilerParams(vmem_limit_bytes=vmem * MIB),
        cost_estimate=pl.CostEstimate(flops=micros << 30, bytes_accessed=MIB, transcendentals=0),
    )(*args)


def exchange(values, axes):
    return lax.all_to_all(values, axes, split_axis=0, concat_axis=0, tiled=True)


def swap(values, axis, offset=1):
    return lax.ppermute(values, axis, [(i, i ^ offset) for i in range(lax.axis_size(axis))])


def body(
    head_table,
    tail_table,
    qual_table,
    rel_table,
    proj,
    head_id,
    tail_id,
    rel_id,
    qual_rel,
    qual_ref,
    qual_req,
    neg_id,
    edge_count,
):
    head_rows, width = head_table.shape
    tail_rows = tail_table.shape[0]
    qual_rows = qual_table.shape[0]
    rel_rows = rel_table.shape[0]
    edges = head_id.shape[0]
    negs = neg_id.shape[0]
    slots = qual_req.shape[0]
    half = lax.axis_size("line")
    cores = lax.axis_size("core")
    chips = lax.axis_size(CHIPS)
    devices = cores * chips
    quals = qual_ref.shape[1]
    cap = slots // devices
    lanes = width // cores

    arrived = exchange(qual_req.reshape(devices, cap), AXES)
    head_near = jnp.stack([head_table] + [swap(head_table, "line", offset) for offset in range(1, half)])
    core = lax.axis_index("core").astype(jnp.int32).reshape(1)
    member = lax.axis_index(MEMBER).astype(jnp.int32).reshape(1)

    rel_row = rel_id[None, :]
    qual_row = qual_rel.T
    ref_row = qual_ref.T
    tail_row = tail_id[None, :]
    neg_row = neg_id[None, :]
    (rel_looked,) = call(
        relation_lookup_kernel,
        [((quals + 1, width, edges), F32)],
        [
            pltpu.VMEM((2 * width, rel_rows), BF),
            pltpu.VMEM((quals + 1, width, edges), F32),
            pltpu.SemaphoreType.DMA((quals + 1,)),
        ],
        5,
        58,
        rel_table,
        rel_row,
        qual_row,
        out_specs=[pl.BlockSpec(memory_space=pl.ANY)],
    )
    arrived, rel_looked, head_near = lax.optimization_barrier((arrived, rel_looked, head_near))
    head_far = swap(head_near, "near")
    picked = qual_table.at[arrived].get(mode="promise_in_bounds")
    fetched = exchange(picked, AXES).reshape(slots, width)
    tails, neg_t, neg = call(
        tail_lookup_kernel,
        [((width, edges), BF), ((width, negs), BF), ((negs, width), BF)],
        [pltpu.VMEM((width, tail_rows), BF)],
        7,
        58,
        tail_table,
        tail_row,
        neg_row,
    )
    share = -(-(rel_rows + width) // (16 * chips)) * 16
    passed = cap * cores
    sent = share + passed

    def edge(*refs):
        edge_kernel(*refs, rel_rows=rel_rows)

    far_high, far_low, near_part, own_part, other_part, terms = call(
        edge,
        [
            ((half - half // 2, head_rows, width), BF),
            ((half // 2, head_rows, width), BF),
            ((half, head_rows, width), BF),
            ((chips, sent, lanes), BF),
            ((chips, sent, lanes), BF),
            ((edges + negs, width), BF),
        ],
        [
            pltpu.VMEM((quals + 1, width, edges), F32),
            pltpu.VMEM((half, head_rows, width), BF),
            pltpu.VMEM((half, head_rows, width), BF),
            pltpu.VMEM((width, edges), BF),
            pltpu.VMEM((negs, width), BF),
            pltpu.VMEM((width, negs), BF),
            pltpu.VMEM((chips * share, width), F32),
            pltpu.VMEM((cores, chips, sent, lanes), BF),
            pltpu.VMEM((edges + negs, width), BF),
            pltpu.SemaphoreType.DMA((quals + 6,)),
            pltpu.SemaphoreType.DMA((6,)),
        ],
        14,
        58,
        edge_count,
        core,
        member,
        rel_looked,
        head_near,
        head_far,
        tails,
        neg,
        neg_t,
        fetched,
        ref_row,
        rel_row,
        qual_row,
        head_id[None, :],
        proj,
        smem=(0, 1, 2),
        away=range(3, 9),
        out_specs=[pl.BlockSpec(memory_space=pl.ANY)] * 6,
    )
    other_got = swap(other_part, "core")
    high_got = swap(far_high, "near")
    low_got = swap(far_low, "near")
    (chip_part,) = call(combine_kernel, [((chips, sent + passed, lanes), BF)], [], 1, 16, own_part, other_got)
    chip_got = exchange(chip_part, CHIPS)

    block = min(1024, tail_rows)
    steps = tail_rows // block

    def tail_rows_of(skip, count, *begun):
        def kernel(*refs):
            tail_kernel(*refs, skip=skip)

        (out,) = call(
            kernel,
            [((tail_rows, width), F32)],
            [],
            3,
            24,
            tail_row,
            neg_row,
            terms,
            *begun,
            away=(3,) if begun else (),
            aliases={3: 0} if begun else {},
            grid=(count,),
            out_specs=[pl.BlockSpec((block, width), lambda i: (i + skip, 0))],
        )
        return out

    tail_grad = tail_rows_of(0, steps // 2)
    high_got, tail_grad = lax.optimization_barrier((high_got, tail_grad))

    def near_sum(offset):
        got = high_got[offset - half // 2] if offset >= half // 2 else low_got[offset]
        return near_part[offset].astype(F32) + got.astype(F32)

    line_got = [swap(near_sum(offset).astype(BF), "line", offset) for offset in reversed(range(1, half))]
    (sums_own,) = call(add_kernel, [((chips, share, lanes), BF)], [], 1, 16, chip_got)
    sums_own = exchange(sums_own, CHIPS).reshape(chips * share, lanes)
    tail_grad = tail_rows_of(steps // 2, steps - steps // 2, tail_grad)
    sums_own, tail_grad, line_got = lax.optimization_barrier((sums_own, tail_grad, line_got))
    sums_got = swap(sums_own, "core")
    rel_grad, proj_grad = call(
        finish_kernel,
        [((rel_rows, width), F32), ((width, width), F32)],
        [],
        1,
        16,
        core,
        sums_own,
        sums_got,
        smem=(0,),
    )

    head_grad = near_sum(0)
    for got in line_got:
        head_grad = head_grad + got.astype(F32)

    asked = arrived.reshape(PAIRS, cores, chips // PAIRS * cap).transpose(1, 0, 2).reshape(cores, chips * cap)
    (qual_grad,) = call(
        qual_kernel, [((qual_rows, width), F32)], [], 2, 16, core, chip_got, asked, smem=(0,)
    )
    return (head_grad, tail_grad, qual_grad, rel_grad, proj_grad)


def solution(mesh):
    groups, members = mesh.devices.shape
    view = Mesh(mesh.devices.reshape(groups // 2, 2, members // 2, 2), AXES)
    rows = P(AXES, None)
    ids = P(AXES)
    in_specs = (rows, rows, rows, P(), P(), ids, ids, ids, rows, rows, ids, ids, ids)
    out_specs = (rows, rows, rows, P(), P())
    return jax.shard_map(body, mesh=view, in_specs=in_specs, out_specs=out_specs, check_vma=False)
```

```python
import jax
import jax.numpy as jnp
from jax import lax
from jax.experimental import pallas as pl
from jax.experimental.pallas import tpu as pltpu
from jax.sharding import Mesh, PartitionSpec as P

BF = jnp.bfloat16
F32 = jnp.float32
MIB = 1024 * 1024
AXES = ("pair", "core", "line", "near")
MEMBER = ("line", "near")
CHIPS = ("pair", "line", "near")
PAIRS = 2
BLOCK = 256
UNROLL = 4


def nn(a, b):
    return jnp.dot(a, b, preferred_element_type=F32)


def nt(a, b):
    return lax.dot_general(a, b, (((1,), (1,)), ((), ())), preferred_element_type=F32)


def tn(a, b):
    return lax.dot_general(a, b, (((0,), (0,)), ((), ())), preferred_element_type=F32)


def pieces(values, count):
    out = []
    for _ in range(count):
        part = values.astype(BF)
        out.append(part)
        values = values - part.astype(F32)
    return out


def flip(values):
    return values.astype(F32).T.astype(BF)


def onehot(ids_row, first, rows):
    iota = lax.broadcasted_iota(jnp.int32, (rows, ids_row.shape[1]), 0)
    return jnp.where(iota == ids_row - first, 1.0, 0.0).astype(BF)


def relation_lookup_kernel(rel_ref, rel_id, qual_rel, rel_out, table, looked, sems):
    rel_rows, width = rel_ref.shape
    edges = rel_id.shape[1]
    for index, part in enumerate(pieces(rel_ref[...].T, 2)):
        table[index * width : (index + 1) * width, :] = part
    stores = []
    for which in range(1 + qual_rel.shape[0]):
        ids = qual_rel.at[which - 1 : which] if which else rel_id
        for start in range(0, edges, BLOCK):
            at = pl.ds(start, BLOCK)
            got = nn(table[...], onehot(ids[:, at], 0, rel_rows))
            looked[which, :, at] = got[:width] + got[width:]
        stores.append(pltpu.make_async_copy(looked.at[which], rel_out.at[which], sems.at[which]))
        stores[which].start()
    for copy in stores:
        copy.wait()


def tail_lookup_kernel(tail_ref, tail_id, neg_id, tails_out, negt_out, neg_out, table):
    tail_rows = tail_ref.shape[0]
    for start in range(0, tail_rows, BLOCK):
        at = pl.ds(start, BLOCK)
        table[:, at] = tail_ref[at, :].T
    for ids, out in ((tail_id, tails_out), (neg_id, negt_out)):
        for start in range(0, ids.shape[1], BLOCK):
            at = pl.ds(start, BLOCK)
            got = nn(table[...], onehot(ids[:, at], 0, tail_rows))
            out[:, at] = got.astype(BF)
            if ids is neg_id:
                neg_out[at, :] = got.T.astype(BF)


def pick_kernel(table_ref, ids_ref, out_ref):
    hot = onehot(ids_ref[...], 0, table_ref.shape[0])
    out_ref[...] = tn(hot, table_ref[...]).astype(BF)


def edge_kernel(
    count_ref,
    core_ref,
    member_ref,
    rel_hbm,
    near_hbm,
    far_hbm,
    tails_hbm,
    neg_hbm,
    negt_hbm,
    fetched_ref,
    ref_ids,
    rel_id,
    qual_rel,
    head_id,
    proj_ref,
    far_out,
    near_out,
    own_out,
    other_out,
    terms_out,
    rel_ref,
    near_ref,
    far_ref,
    tails_ref,
    neg_ref,
    negt_ref,
    sums,
    packed,
    terms,
    in_sems,
    out_sems,
    *,
    rel_rows,
):
    width, edges = tails_ref.shape
    slots = fetched_ref.shape[0]
    half, head_rows, _ = near_ref.shape
    cores, chips, _, lanes = packed.shape
    share = sums.shape[0] // chips
    quals = ref_ids.shape[0]
    cap = slots // (cores * chips)

    loads = []

    def load(source, target):
        loads.append(pltpu.make_async_copy(source, target, in_sems.at[len(loads)]))
        loads[-1].start()
        return loads[-1]

    head_loads = [load(near_hbm, near_ref), load(far_hbm, far_ref)]
    rel_loads = [load(rel_hbm.at[which], rel_ref.at[which]) for which in [*range(1, quals + 1), 0]]
    tails_load = load(tails_hbm, tails_ref)
    neg_load = load(neg_hbm, neg_ref)
    negt_load = load(negt_hbm, negt_ref)

    fetched_t = flip(fetched_ref[...])
    proj_hi, proj_lo = pieces(proj_ref[...], 2)
    projt_hi, projt_lo = pieces(proj_ref[...].T, 2)
    rows = [nn(fetched_t, onehot(ref_ids[k : k + 1, :], 0, slots)) for k in range(quals)]
    for copy in head_loads:
        copy.wait()
    offset = jnp.bitwise_xor(head_id[...] // head_rows, member_ref[0])
    head_slot = ((offset % 2) * half + offset // 2) * head_rows + head_id[...] % head_rows
    heads = jnp.zeros((width, edges), F32)
    for first, table in ((0, near_ref), (half, far_ref)):
        for owner in range(half):
            heads = heads + tn(table[owner], onehot(head_slot, (first + owner) * head_rows, head_rows))
    for copy in rel_loads:
        copy.wait()
    composed = rel_ref[1] * rows[0]
    for k in range(1, quals):
        composed = composed + rel_ref[k + 1] * rows[k]
    comp_hi, comp_lo = pieces(composed, 2)
    relation = rel_ref[0] + nn(
        jnp.concatenate([projt_hi, projt_hi, projt_lo], axis=1),
        jnp.concatenate([comp_hi, comp_lo, comp_hi], axis=0),
    )
    query = (heads * relation).astype(BF)
    query_f = query.astype(F32)
    tails_load.wait()
    tails = tails_ref[...].astype(F32)
    positive = jnp.sum(query_f * tails, axis=0, keepdims=True)
    neg_load.wait()
    scores = nn(neg_ref[...], query)
    top = jnp.maximum(jnp.max(scores, axis=0, keepdims=True), positive)
    neg_exp = jnp.exp(scores - top)
    pos_exp = jnp.exp(positive - top)
    total = jnp.sum(neg_exp, axis=0, keepdims=True) + pos_exp
    slot = lax.broadcasted_iota(jnp.int32, (1, edges), 1)
    live = jnp.where(slot < count_ref[0], 1.0, 0.0)
    scale = live / total
    neg_round = (neg_exp * scale).astype(BF)
    coef = pos_exp * scale - live
    negt_load.wait()
    query_grad = coef * tails + nn(negt_ref[...], neg_round)

    stores = []

    def store(source, target):
        stores.append(pltpu.make_async_copy(source, target, out_sems.at[len(stores)]))
        stores[-1].start()

    head_terms = (query_grad * relation).astype(BF)
    for first, part, out in ((half, far_ref, far_out), (0, near_ref, near_out)):

        def scatter(owner):
            hot = onehot(head_slot, (first + owner) * head_rows, head_rows)
            part[owner] = nt(hot, head_terms).astype(BF)

        if half > UNROLL:
            pl.loop(0, half)(scatter)
        else:
            for owner in range(half):
                scatter(owner)
        store(part, out)

    relation_grad = query_grad * heads
    rg_hi, rg_lo = pieces(relation_grad, 2)
    comp_grad = nn(
        jnp.concatenate([proj_hi, proj_hi, proj_lo], axis=1), jnp.concatenate([rg_hi, rg_lo, rg_hi], axis=0)
    )
    rel_hots, rel_terms = [onehot(rel_id[...], 0, rel_rows)], [rg_hi]
    ref_hots, ref_terms = [], []
    for k in range(quals):
        rel_hots.append(onehot(qual_rel[k : k + 1, :], 0, rel_rows))
        rel_terms.append((comp_grad * rows[k]).astype(BF))
        ref_hots.append(onehot(ref_ids[k : k + 1, :], 0, slots))
        ref_terms.append((comp_grad * rel_ref[k + 1]).astype(BF))
    rel_sum = nt(jnp.concatenate(rel_hots, axis=1), jnp.concatenate(rel_terms, axis=1))
    fetched_sum = nt(jnp.concatenate(ref_hots, axis=1), jnp.concatenate(ref_terms, axis=1))
    sums[:rel_rows, :] = rel_sum
    sums[rel_rows : rel_rows + width, :] = nt(
        jnp.concatenate([comp_hi, comp_hi, comp_lo], axis=1), jnp.concatenate([rg_hi, rg_lo, rg_hi], axis=1)
    )
    if sums.shape[0] > rel_rows + width:
        sums[rel_rows + width :, :] = jnp.zeros((sums.shape[0] - rel_rows - width, width), F32)
    pairs = fetched_sum.reshape(-1, cores, chips // PAIRS, cap, width)
    for core in range(cores):
        mine = pairs[:, core].reshape(chips, cap, width)
        parts = [sums[:, core * lanes : (core + 1) * lanes].reshape(chips, share, lanes)]
        parts += [mine[:, :, start : start + lanes] for start in range(0, width, lanes)]
        packed[core] = jnp.concatenate(parts, axis=1).astype(BF)
    store(packed.at[core_ref[0]], own_out)
    store(packed.at[1 - core_ref[0]], other_out)

    terms[:edges, :] = flip((coef * query_f).astype(BF))
    terms[edges:, :] = nt(neg_round, query).astype(BF)
    store(terms, terms_out)
    for copy in stores:
        copy.wait()


def combine_kernel(own_ref, got_ref, out_ref):
    chips, sent, lanes = own_ref.shape
    passed = out_ref.shape[1] - sent
    share = sent - passed
    summed = own_ref[:, :share, :].astype(F32) + got_ref[:, :share, :].astype(F32)
    out_ref[:, :share, :] = summed.astype(BF)
    out_ref[:, share:sent, :] = own_ref[:, share:, :]
    out_ref[:, sent:, :] = got_ref[:, share:, :]


def add_kernel(got_ref, out_ref):
    chips, share, _ = out_ref.shape
    total = got_ref[0, :share, :].astype(F32)
    for index in range(1, chips):
        total = total + got_ref[index, :share, :].astype(F32)
    total = total.astype(BF)
    for index in range(chips):
        out_ref[index] = total


def finish_kernel(core_ref, own_ref, got_ref, rel_out, proj_out):
    rel_rows = rel_out.shape[0]
    proj_rows = proj_out.shape[0]
    lanes = own_ref.shape[1]
    for ref, core in ((own_ref, core_ref[0]), (got_ref, 1 - core_ref[0])):
        at = pl.ds(pl.multiple_of(core * lanes, lanes), lanes)
        rel_out[:, at] = ref[:rel_rows, :].astype(F32)
        proj_out[:, at] = ref[rel_rows : rel_rows + proj_rows, :].astype(F32)


def qual_kernel(core_ref, got_ref, asked, qual_out):
    qual_rows, width = qual_out.shape
    chips, rows, lanes = got_ref.shape
    cores = asked.shape[0]
    cap = asked.shape[1] // chips
    parts = width // lanes
    first = rows - cores * parts * cap
    passed = got_ref[:, first:, :].astype(F32)
    hots = [
        onehot(asked[pl.ds(core_ref[0], 1), :], 0, qual_rows),
        onehot(asked[pl.ds(1 - core_ref[0], 1), :], 0, qual_rows),
    ]
    for part in range(parts):
        total = jnp.zeros((qual_rows, lanes), F32)
        for core in range(cores):
            start = (core * parts + part) * cap
            sent = passed[:, start : start + cap, :].reshape(chips * cap, lanes).astype(BF)
            total = total + nn(hots[core], sent)
        qual_out[:, part * lanes : (part + 1) * lanes] = total


def tail_kernel(tail_id, neg_id, terms, *refs, skip):
    tail_out = refs[-1]
    edges = tail_id.shape[1]
    rows = tail_out.shape[0]
    first = (pl.program_id(0) + skip) * rows
    tail_out[...] = nn(onehot(tail_id[...], first, rows), terms[:edges, :]) + nn(
        onehot(neg_id[...], first, rows), terms[edges:, :]
    )


WHOLE = pl.BlockSpec(memory_space=pltpu.VMEM)


def call(kernel, outs, scratch, micros, vmem, *args, smem=(), away=(), aliases={}, grid=(), out_specs=None):
    shapes = [jax.ShapeDtypeStruct(shape, dtype) for shape, dtype in outs]
    places = {**{index: pltpu.SMEM for index in smem}, **{index: pl.ANY for index in away}}
    return pl.pallas_call(
        kernel,
        out_shape=shapes,
        grid=grid,
        in_specs=[pl.BlockSpec(memory_space=places.get(index, pltpu.VMEM)) for index in range(len(args))],
        out_specs=out_specs or [WHOLE] * len(outs),
        scratch_shapes=scratch,
        input_output_aliases=aliases,
        compiler_params=pltpu.CompilerParams(vmem_limit_bytes=vmem * MIB),
        cost_estimate=pl.CostEstimate(flops=micros << 30, bytes_accessed=MIB, transcendentals=0),
    )(*args)


def exchange(values, axes):
    return lax.all_to_all(values, axes, split_axis=0, concat_axis=0, tiled=True)


def swap(values, axis, offset=1):
    return lax.ppermute(values, axis, [(i, i ^ offset) for i in range(lax.axis_size(axis))])


def body(
    head_table,
    tail_table,
    qual_table,
    rel_table,
    proj,
    head_id,
    tail_id,
    rel_id,
    qual_rel,
    qual_ref,
    qual_req,
    neg_id,
    edge_count,
):
    head_rows, width = head_table.shape
    tail_rows = tail_table.shape[0]
    qual_rows = qual_table.shape[0]
    rel_rows = rel_table.shape[0]
    edges = head_id.shape[0]
    negs = neg_id.shape[0]
    slots = qual_req.shape[0]
    half = lax.axis_size("line")
    cores = lax.axis_size("core")
    chips = lax.axis_size(CHIPS)
    devices = cores * chips
    quals = qual_ref.shape[1]
    cap = slots // devices
    lanes = width // cores

    arrived = exchange(qual_req.reshape(devices, cap), AXES)
    head_near = jnp.stack([head_table] + [swap(head_table, "line", offset) for offset in range(1, half)])
    core = lax.axis_index("core").astype(jnp.int32).reshape(1)
    member = lax.axis_index(MEMBER).astype(jnp.int32).reshape(1)

    rel_row = rel_id[None, :]
    qual_row = qual_rel.T
    ref_row = qual_ref.T
    tail_row = tail_id[None, :]
    neg_row = neg_id[None, :]
    (rel_looked,) = call(
        relation_lookup_kernel,
        [((quals + 1, width, edges), F32)],
        [
            pltpu.VMEM((2 * width, rel_rows), BF),
            pltpu.VMEM((quals + 1, width, edges), F32),
            pltpu.SemaphoreType.DMA((quals + 1,)),
        ],
        5,
        58,
        rel_table,
        rel_row,
        qual_row,
        out_specs=[pl.BlockSpec(memory_space=pl.ANY)],
    )
    arrived, rel_looked, head_near = lax.optimization_barrier((arrived, rel_looked, head_near))
    head_far = swap(head_near, "near")
    (picked,) = call(pick_kernel, [((slots, width), BF)], [], 1, 16, qual_table, arrived.reshape(1, slots))
    picked = picked.reshape(devices, cap, width)
    fetched = exchange(picked, AXES).reshape(slots, width)
    tails, neg_t, neg = call(
        tail_lookup_kernel,
        [((width, edges), BF), ((width, negs), BF), ((negs, width), BF)],
        [pltpu.VMEM((width, tail_rows), BF)],
        7,
        58,
        tail_table,
        tail_row,
        neg_row,
    )
    share = -(-(rel_rows + width) // (16 * chips)) * 16
    passed = cap * cores
    sent = share + passed

    def edge(*refs):
        edge_kernel(*refs, rel_rows=rel_rows)

    far_part, near_part, own_part, other_part, terms = call(
        edge,
        [
            ((half, head_rows, width), BF),
            ((half, head_rows, width), BF),
            ((chips, sent, lanes), BF),
            ((chips, sent, lanes), BF),
            ((edges + negs, width), BF),
        ],
        [
            pltpu.VMEM((quals + 1, width, edges), F32),
            pltpu.VMEM((half, head_rows, width), BF),
            pltpu.VMEM((half, head_rows, width), BF),
            pltpu.VMEM((width, edges), BF),
            pltpu.VMEM((negs, width), BF),
            pltpu.VMEM((width, negs), BF),
            pltpu.VMEM((chips * share, width), F32),
            pltpu.VMEM((cores, chips, sent, lanes), BF),
            pltpu.VMEM((edges + negs, width), BF),
            pltpu.SemaphoreType.DMA((quals + 6,)),
            pltpu.SemaphoreType.DMA((5,)),
        ],
        14,
        58,
        edge_count,
        core,
        member,
        rel_looked,
        head_near,
        head_far,
        tails,
        neg,
        neg_t,
        fetched,
        ref_row,
        rel_row,
        qual_row,
        head_id[None, :],
        proj,
        smem=(0, 1, 2),
        away=range(3, 9),
        out_specs=[pl.BlockSpec(memory_space=pl.ANY)] * 5,
    )
    other_got = swap(other_part, "core")
    far_got = swap(far_part, "near")
    (chip_part,) = call(combine_kernel, [((chips, sent + passed, lanes), BF)], [], 1, 16, own_part, other_got)
    chip_got = exchange(chip_part, CHIPS)

    block = min(1024, tail_rows)
    steps = tail_rows // block

    def tail_rows_of(skip, count, *begun):
        def kernel(*refs):
            tail_kernel(*refs, skip=skip)

        (out,) = call(
            kernel,
            [((tail_rows, width), F32)],
            [],
            3,
            24,
            tail_row,
            neg_row,
            terms,
            *begun,
            away=(3,) if begun else (),
            aliases={3: 0} if begun else {},
            grid=(count,),
            out_specs=[pl.BlockSpec((block, width), lambda i: (i + skip, 0))],
        )
        return out

    tail_grad = tail_rows_of(0, steps // 2)
    far_got, tail_grad = lax.optimization_barrier((far_got, tail_grad))
    near_sum = [near_part[offset].astype(F32) + far_got[offset].astype(F32) for offset in range(half)]
    line_got = [swap(near_sum[offset].astype(BF), "line", offset) for offset in range(1, half)]
    (sums_own,) = call(add_kernel, [((chips, share, lanes), BF)], [], 1, 16, chip_got)
    sums_own = exchange(sums_own, CHIPS).reshape(chips * share, lanes)
    tail_grad = tail_rows_of(steps // 2, steps - steps // 2, tail_grad)
    sums_own, tail_grad, line_got = lax.optimization_barrier((sums_own, tail_grad, line_got))
    sums_got = swap(sums_own, "core")
    rel_grad, proj_grad = call(
        finish_kernel,
        [((rel_rows, width), F32), ((width, width), F32)],
        [],
        1,
        16,
        core,
        sums_own,
        sums_got,
        smem=(0,),
    )

    head_grad = near_sum[0]
    for got in line_got:
        head_grad = head_grad + got.astype(F32)

    asked = arrived.reshape(PAIRS, cores, chips // PAIRS * cap).transpose(1, 0, 2).reshape(cores, chips * cap)
    (qual_grad,) = call(
        qual_kernel, [((qual_rows, width), F32)], [], 2, 16, core, chip_got, asked, smem=(0,)
    )
    return (head_grad, tail_grad, qual_grad, rel_grad, proj_grad)


def solution(mesh):
    groups, members = mesh.devices.shape
    view = Mesh(mesh.devices.reshape(groups // 2, 2, members // 2, 2), AXES)
    rows = P(AXES, None)
    ids = P(AXES)
    in_specs = (rows, rows, rows, P(), P(), ids, ids, ids, rows, rows, ids, ids, ids)
    out_specs = (rows, rows, rows, P(), P())
    return jax.shard_map(body, mesh=view, in_specs=in_specs, out_specs=out_specs, check_vma=False)
```

```python
import jax
import jax.numpy as jnp
from jax import lax
from jax.experimental import pallas as pl
from jax.experimental.pallas import tpu as pltpu
from jax.sharding import Mesh, PartitionSpec as P

BF = jnp.bfloat16
F32 = jnp.float32
MIB = 1024 * 1024
AXES = ("pair", "core", "line", "near")
MEMBER = ("line", "near")
CHIPS = ("pair", "line", "near")
PAIRS = 2
BLOCK = 256
UNROLL = 4


def nn(a, b):
    return jnp.dot(a, b, preferred_element_type=F32)


def nt(a, b):
    return lax.dot_general(a, b, (((1,), (1,)), ((), ())), preferred_element_type=F32)


def tn(a, b):
    return lax.dot_general(a, b, (((0,), (0,)), ((), ())), preferred_element_type=F32)


def pieces(values, count):
    out = []
    for _ in range(count):
        part = values.astype(BF)
        out.append(part)
        values = values - part.astype(F32)
    return out


def flip(values):
    return values.astype(F32).T.astype(BF)


def onehot(ids_row, first, rows):
    iota = lax.broadcasted_iota(jnp.int32, (rows, ids_row.shape[1]), 0)
    return jnp.where(iota == ids_row - first, 1.0, 0.0).astype(BF)


def relation_lookup_kernel(rel_ref, rel_id, qual_rel, rel_out, table, looked, sems):
    rel_rows, width = rel_ref.shape
    edges = rel_id.shape[1]
    for index, part in enumerate(pieces(rel_ref[...].T, 2)):
        table[index * width : (index + 1) * width, :] = part
    stores = []
    for which in range(1 + qual_rel.shape[0]):
        ids = qual_rel.at[which - 1 : which] if which else rel_id
        for start in range(0, edges, BLOCK):
            at = pl.ds(start, BLOCK)
            got = nn(table[...], onehot(ids[:, at], 0, rel_rows))
            looked[which, :, at] = got[:width] + got[width:]
        stores.append(pltpu.make_async_copy(looked.at[which], rel_out.at[which], sems.at[which]))
        stores[which].start()
    for copy in stores:
        copy.wait()


def tail_lookup_kernel(tail_ref, tail_id, neg_id, tails_out, negt_out, neg_out, table):
    tail_rows = tail_ref.shape[0]
    for start in range(0, tail_rows, BLOCK):
        at = pl.ds(start, BLOCK)
        table[:, at] = tail_ref[at, :].T
    for ids, out in ((tail_id, tails_out), (neg_id, negt_out)):
        for start in range(0, ids.shape[1], BLOCK):
            at = pl.ds(start, BLOCK)
            got = nn(table[...], onehot(ids[:, at], 0, tail_rows))
            out[:, at] = got.astype(BF)
            if ids is neg_id:
                neg_out[at, :] = got.T.astype(BF)


def pick_kernel(table_ref, ids_ref, out_ref):
    hot = onehot(ids_ref[...], 0, table_ref.shape[0])
    out_ref[...] = tn(hot, table_ref[...]).astype(BF)


def edge_kernel(
    count_ref,
    core_ref,
    member_ref,
    rel_hbm,
    near_hbm,
    far_hbm,
    tails_hbm,
    neg_hbm,
    negt_hbm,
    fetched_ref,
    ref_ids,
    rel_id,
    qual_rel,
    head_id,
    proj_ref,
    far_out,
    near_out,
    own_out,
    other_out,
    terms_out,
    rel_ref,
    near_ref,
    far_ref,
    tails_ref,
    neg_ref,
    negt_ref,
    sums,
    packed,
    terms,
    in_sems,
    out_sems,
    *,
    rel_rows,
):
    width, edges = tails_ref.shape
    slots = fetched_ref.shape[0]
    half, head_rows, _ = near_ref.shape
    cores, chips, _, lanes = packed.shape
    share = sums.shape[0] // chips
    quals = ref_ids.shape[0]
    cap = slots // (cores * chips)

    loads = []

    def load(source, target):
        loads.append(pltpu.make_async_copy(source, target, in_sems.at[len(loads)]))
        loads[-1].start()
        return loads[-1]

    head_loads = [load(near_hbm, near_ref), load(far_hbm, far_ref)]
    rel_loads = [load(rel_hbm.at[which], rel_ref.at[which]) for which in [*range(1, quals + 1), 0]]
    tails_load = load(tails_hbm, tails_ref)
    neg_load = load(neg_hbm, neg_ref)
    negt_load = load(negt_hbm, negt_ref)

    fetched_t = flip(fetched_ref[...])
    proj_hi, proj_lo = pieces(proj_ref[...], 2)
    projt_hi, projt_lo = pieces(proj_ref[...].T, 2)
    rows = [nn(fetched_t, onehot(ref_ids[k : k + 1, :], 0, slots)) for k in range(quals)]
    for copy in head_loads:
        copy.wait()
    offset = jnp.bitwise_xor(head_id[...] // head_rows, member_ref[0])
    head_slot = ((offset % 2) * half + offset // 2) * head_rows + head_id[...] % head_rows
    heads = jnp.zeros((width, edges), F32)
    for first, table in ((0, near_ref), (half, far_ref)):
        for owner in range(half):
            heads = heads + tn(table[owner], onehot(head_slot, (first + owner) * head_rows, head_rows))
    for copy in rel_loads:
        copy.wait()
    composed = rel_ref[1] * rows[0]
    for k in range(1, quals):
        composed = composed + rel_ref[k + 1] * rows[k]
    comp_hi, comp_lo = pieces(composed, 2)
    relation = rel_ref[0] + nn(
        jnp.concatenate([projt_hi, projt_hi, projt_lo], axis=1),
        jnp.concatenate([comp_hi, comp_lo, comp_hi], axis=0),
    )
    query = (heads * relation).astype(BF)
    query_f = query.astype(F32)
    tails_load.wait()
    tails = tails_ref[...].astype(F32)
    positive = jnp.sum(query_f * tails, axis=0, keepdims=True)
    neg_load.wait()
    scores = nn(neg_ref[...], query)
    top = jnp.maximum(jnp.max(scores, axis=0, keepdims=True), positive)
    neg_exp = jnp.exp(scores - top)
    pos_exp = jnp.exp(positive - top)
    total = jnp.sum(neg_exp, axis=0, keepdims=True) + pos_exp
    slot = lax.broadcasted_iota(jnp.int32, (1, edges), 1)
    live = jnp.where(slot < count_ref[0], 1.0, 0.0)
    scale = live / total
    neg_round = (neg_exp * scale).astype(BF)
    coef = pos_exp * scale - live
    negt_load.wait()
    query_grad = coef * tails + nn(negt_ref[...], neg_round)

    stores = []

    def store(source, target):
        stores.append(pltpu.make_async_copy(source, target, out_sems.at[len(stores)]))
        stores[-1].start()

    head_terms = (query_grad * relation).astype(BF)
    for first, part, out in ((half, far_ref, far_out), (0, near_ref, near_out)):

        def scatter(owner):
            hot = onehot(head_slot, (first + owner) * head_rows, head_rows)
            part[owner] = nt(hot, head_terms).astype(BF)

        if half > UNROLL:
            pl.loop(0, half)(scatter)
        else:
            for owner in range(half):
                scatter(owner)
        store(part, out)

    relation_grad = query_grad * heads
    rg_hi, rg_lo = pieces(relation_grad, 2)
    comp_grad = nn(
        jnp.concatenate([proj_hi, proj_hi, proj_lo], axis=1), jnp.concatenate([rg_hi, rg_lo, rg_hi], axis=0)
    )
    rel_hots, rel_terms = [onehot(rel_id[...], 0, rel_rows)], [rg_hi]
    ref_hots, ref_terms = [], []
    for k in range(quals):
        rel_hots.append(onehot(qual_rel[k : k + 1, :], 0, rel_rows))
        rel_terms.append((comp_grad * rows[k]).astype(BF))
        ref_hots.append(onehot(ref_ids[k : k + 1, :], 0, slots))
        ref_terms.append((comp_grad * rel_ref[k + 1]).astype(BF))
    rel_sum = nt(jnp.concatenate(rel_hots, axis=1), jnp.concatenate(rel_terms, axis=1))
    fetched_sum = nt(jnp.concatenate(ref_hots, axis=1), jnp.concatenate(ref_terms, axis=1))
    sums[:rel_rows, :] = rel_sum
    sums[rel_rows : rel_rows + width, :] = nt(
        jnp.concatenate([comp_hi, comp_hi, comp_lo], axis=1), jnp.concatenate([rg_hi, rg_lo, rg_hi], axis=1)
    )
    if sums.shape[0] > rel_rows + width:
        sums[rel_rows + width :, :] = jnp.zeros((sums.shape[0] - rel_rows - width, width), F32)
    pairs = fetched_sum.reshape(-1, cores, chips // PAIRS, cap, width)
    for core in range(cores):
        mine = pairs[:, core].reshape(chips, cap, width)
        parts = [sums[:, core * lanes : (core + 1) * lanes].reshape(chips, share, lanes)]
        parts += [mine[:, :, start : start + lanes] for start in range(0, width, lanes)]
        packed[core] = jnp.concatenate(parts, axis=1).astype(BF)
    store(packed.at[core_ref[0]], own_out)
    store(packed.at[1 - core_ref[0]], other_out)

    terms[:edges, :] = flip((coef * query_f).astype(BF))
    terms[edges:, :] = nt(neg_round, query).astype(BF)
    store(terms, terms_out)
    for copy in stores:
        copy.wait()


def combine_kernel(own_ref, got_ref, out_ref):
    chips, sent, lanes = own_ref.shape
    passed = out_ref.shape[1] - sent
    share = sent - passed
    summed = own_ref[:, :share, :].astype(F32) + got_ref[:, :share, :].astype(F32)
    out_ref[:, :share, :] = summed.astype(BF)
    out_ref[:, share:sent, :] = own_ref[:, share:, :]
    out_ref[:, sent:, :] = got_ref[:, share:, :]


def add_kernel(got_ref, out_ref):
    chips, share, _ = out_ref.shape
    total = got_ref[0, :share, :].astype(F32)
    for index in range(1, chips):
        total = total + got_ref[index, :share, :].astype(F32)
    total = total.astype(BF)
    for index in range(chips):
        out_ref[index] = total


def finish_kernel(core_ref, own_ref, got_ref, rel_out, proj_out):
    rel_rows = rel_out.shape[0]
    proj_rows = proj_out.shape[0]
    lanes = own_ref.shape[1]
    for ref, core in ((own_ref, core_ref[0]), (got_ref, 1 - core_ref[0])):
        at = pl.ds(pl.multiple_of(core * lanes, lanes), lanes)
        rel_out[:, at] = ref[:rel_rows, :].astype(F32)
        proj_out[:, at] = ref[rel_rows : rel_rows + proj_rows, :].astype(F32)


def qual_kernel(core_ref, got_ref, asked, qual_out):
    qual_rows, width = qual_out.shape
    chips, rows, lanes = got_ref.shape
    cores = asked.shape[0]
    cap = asked.shape[1] // chips
    parts = width // lanes
    first = rows - cores * parts * cap
    passed = got_ref[:, first:, :].astype(F32)
    hots = [
        onehot(asked[pl.ds(core_ref[0], 1), :], 0, qual_rows),
        onehot(asked[pl.ds(1 - core_ref[0], 1), :], 0, qual_rows),
    ]
    for part in range(parts):
        total = jnp.zeros((qual_rows, lanes), F32)
        for core in range(cores):
            start = (core * parts + part) * cap
            sent = passed[:, start : start + cap, :].reshape(chips * cap, lanes).astype(BF)
            total = total + nn(hots[core], sent)
        qual_out[:, part * lanes : (part + 1) * lanes] = total


def tail_kernel(tail_id, neg_id, terms, *refs, skip):
    tail_out = refs[-1]
    rows = tail_out.shape[0]
    first = (pl.program_id(0) + skip) * rows
    hots = [onehot(tail_id[...], first, rows), onehot(neg_id[...], first, rows)]
    tail_out[...] = nn(jnp.concatenate(hots, axis=1), terms[...])


WHOLE = pl.BlockSpec(memory_space=pltpu.VMEM)


def call(kernel, outs, scratch, micros, vmem, *args, smem=(), away=(), aliases={}, grid=(), out_specs=None):
    shapes = [jax.ShapeDtypeStruct(shape, dtype) for shape, dtype in outs]
    places = {**{index: pltpu.SMEM for index in smem}, **{index: pl.ANY for index in away}}
    return pl.pallas_call(
        kernel,
        out_shape=shapes,
        grid=grid,
        in_specs=[pl.BlockSpec(memory_space=places.get(index, pltpu.VMEM)) for index in range(len(args))],
        out_specs=out_specs or [WHOLE] * len(outs),
        scratch_shapes=scratch,
        input_output_aliases=aliases,
        compiler_params=pltpu.CompilerParams(vmem_limit_bytes=vmem * MIB),
        cost_estimate=pl.CostEstimate(flops=micros << 30, bytes_accessed=MIB, transcendentals=0),
    )(*args)


def exchange(values, axes):
    return lax.all_to_all(values, axes, split_axis=0, concat_axis=0, tiled=True)


def swap(values, axis, offset=1):
    return lax.ppermute(values, axis, [(i, i ^ offset) for i in range(lax.axis_size(axis))])


def body(
    head_table,
    tail_table,
    qual_table,
    rel_table,
    proj,
    head_id,
    tail_id,
    rel_id,
    qual_rel,
    qual_ref,
    qual_req,
    neg_id,
    edge_count,
):
    head_rows, width = head_table.shape
    tail_rows = tail_table.shape[0]
    qual_rows = qual_table.shape[0]
    rel_rows = rel_table.shape[0]
    edges = head_id.shape[0]
    negs = neg_id.shape[0]
    slots = qual_req.shape[0]
    half = lax.axis_size("line")
    cores = lax.axis_size("core")
    chips = lax.axis_size(CHIPS)
    devices = cores * chips
    quals = qual_ref.shape[1]
    cap = slots // devices
    lanes = width // cores

    arrived = exchange(qual_req.reshape(devices, cap), AXES)
    head_near = jnp.stack([head_table] + [swap(head_table, "line", offset) for offset in range(1, half)])
    core = lax.axis_index("core").astype(jnp.int32).reshape(1)
    member = lax.axis_index(MEMBER).astype(jnp.int32).reshape(1)

    rel_row = rel_id[None, :]
    qual_row = qual_rel.T
    ref_row = qual_ref.T
    tail_row = tail_id[None, :]
    neg_row = neg_id[None, :]
    (rel_looked,) = call(
        relation_lookup_kernel,
        [((quals + 1, width, edges), F32)],
        [
            pltpu.VMEM((2 * width, rel_rows), BF),
            pltpu.VMEM((quals + 1, width, edges), F32),
            pltpu.SemaphoreType.DMA((quals + 1,)),
        ],
        5,
        58,
        rel_table,
        rel_row,
        qual_row,
        out_specs=[pl.BlockSpec(memory_space=pl.ANY)],
    )
    arrived, rel_looked, head_near = lax.optimization_barrier((arrived, rel_looked, head_near))
    head_far = swap(head_near, "near")
    (picked,) = call(pick_kernel, [((slots, width), BF)], [], 1, 16, qual_table, arrived.reshape(1, slots))
    picked = picked.reshape(devices, cap, width)
    fetched = exchange(picked, AXES).reshape(slots, width)
    tails, neg_t, neg = call(
        tail_lookup_kernel,
        [((width, edges), BF), ((width, negs), BF), ((negs, width), BF)],
        [pltpu.VMEM((width, tail_rows), BF)],
        7,
        58,
        tail_table,
        tail_row,
        neg_row,
    )
    share = -(-(rel_rows + width) // (16 * chips)) * 16
    passed = cap * cores
    sent = share + passed

    def edge(*refs):
        edge_kernel(*refs, rel_rows=rel_rows)

    far_part, near_part, own_part, other_part, terms = call(
        edge,
        [
            ((half, head_rows, width), BF),
            ((half, head_rows, width), BF),
            ((chips, sent, lanes), BF),
            ((chips, sent, lanes), BF),
            ((edges + negs, width), BF),
        ],
        [
            pltpu.VMEM((quals + 1, width, edges), F32),
            pltpu.VMEM((half, head_rows, width), BF),
            pltpu.VMEM((half, head_rows, width), BF),
            pltpu.VMEM((width, edges), BF),
            pltpu.VMEM((negs, width), BF),
            pltpu.VMEM((width, negs), BF),
            pltpu.VMEM((chips * share, width), F32),
            pltpu.VMEM((cores, chips, sent, lanes), BF),
            pltpu.VMEM((edges + negs, width), BF),
            pltpu.SemaphoreType.DMA((quals + 6,)),
            pltpu.SemaphoreType.DMA((5,)),
        ],
        14,
        58,
        edge_count,
        core,
        member,
        rel_looked,
        head_near,
        head_far,
        tails,
        neg,
        neg_t,
        fetched,
        ref_row,
        rel_row,
        qual_row,
        head_id[None, :],
        proj,
        smem=(0, 1, 2),
        away=range(3, 9),
        out_specs=[pl.BlockSpec(memory_space=pl.ANY)] * 5,
    )
    other_got = swap(other_part, "core")
    far_got = swap(far_part, "near")
    (chip_part,) = call(combine_kernel, [((chips, sent + passed, lanes), BF)], [], 1, 16, own_part, other_got)
    chip_got = exchange(chip_part, CHIPS)

    block = min(1024, tail_rows)
    steps = tail_rows // block

    def tail_rows_of(skip, count, *begun):
        def kernel(*refs):
            tail_kernel(*refs, skip=skip)

        (out,) = call(
            kernel,
            [((tail_rows, width), F32)],
            [],
            3,
            24,
            tail_row,
            neg_row,
            terms,
            *begun,
            away=(3,) if begun else (),
            aliases={3: 0} if begun else {},
            grid=(count,),
            out_specs=[pl.BlockSpec((block, width), lambda i: (i + skip, 0))],
        )
        return out

    tail_grad = tail_rows_of(0, steps // 2)
    far_got, tail_grad = lax.optimization_barrier((far_got, tail_grad))
    near_sum = [near_part[offset].astype(F32) + far_got[offset].astype(F32) for offset in range(half)]
    line_got = [swap(near_sum[offset].astype(BF), "line", offset) for offset in range(1, half)]
    (sums_own,) = call(add_kernel, [((chips, share, lanes), BF)], [], 1, 16, chip_got)
    sums_own = exchange(sums_own, CHIPS).reshape(chips * share, lanes)
    tail_grad = tail_rows_of(steps // 2, steps - steps // 2, tail_grad)
    sums_own, tail_grad, line_got = lax.optimization_barrier((sums_own, tail_grad, line_got))
    sums_got = swap(sums_own, "core")
    rel_grad, proj_grad = call(
        finish_kernel,
        [((rel_rows, width), F32), ((width, width), F32)],
        [],
        1,
        16,
        core,
        sums_own,
        sums_got,
        smem=(0,),
    )

    head_grad = near_sum[0]
    for got in line_got:
        head_grad = head_grad + got.astype(F32)

    asked = arrived.reshape(PAIRS, cores, chips // PAIRS * cap).transpose(1, 0, 2).reshape(cores, chips * cap)
    (qual_grad,) = call(
        qual_kernel, [((qual_rows, width), F32)], [], 2, 16, core, chip_got, asked, smem=(0,)
    )
    return (head_grad, tail_grad, qual_grad, rel_grad, proj_grad)


def solution(mesh):
    groups, members = mesh.devices.shape
    view = Mesh(mesh.devices.reshape(groups // 2, 2, members // 2, 2), AXES)
    rows = P(AXES, None)
    ids = P(AXES)
    in_specs = (rows, rows, rows, P(), P(), ids, ids, ids, rows, rows, ids, ids, ids)
    out_specs = (rows, rows, rows, P(), P())
    return jax.shard_map(body, mesh=view, in_specs=in_specs, out_specs=out_specs, check_vma=False)
```
